32 devices in a mesh: seq: 8 (over y, x, core), dp: 4 (over z).
Axes of the slice: x: 2, y: 2, z: 4, core: 2. Of those that a mesh axis runs over, the one named last changes fastest.
Arguments:
- inputs: bfloat16 [8, 2048, 768], P('dp', 'seq'), may hold values from -6 to 6
- w_query: bfloat16 [768, 768], P(('seq', 'dp')), may hold values from -0.21875 to 0.21875
- w_keyval: bfloat16 [768, 128], P(('seq', 'dp')), may hold values from -0.21875 to 0.21875
- w_out: bfloat16 [768, 768], P(('seq', 'dp')), may hold values from -2.5 to 2.5
- w_up: bfloat16 [768, 3072], P(('seq', 'dp')), may hold values from -0.21875 to 0.21875
- w_down: bfloat16 [3072, 768], P(('seq', 'dp')), may hold values from -0.109375 to 0.109375
- norm_gain: bfloat16 [768, 2], P(('seq', 'dp')), may hold values from 0.099609375 to 1.8984375
- norm_bias: bfloat16 [768, 2], P(('seq', 'dp')), may hold values from -1.5 to 1.5
- out_cotangent: bfloat16 [8, 2048, 768], P('dp', 'seq'), may hold values from -6 to 6
- kv_cotangent: bfloat16 [8, 2048, 128], P('dp', 'seq'), may hold values from -6 to 6
Outputs:
- output: bfloat16 [8, 2048, 768], P('dp', 'seq')
- keyval: bfloat16 [8, 2048, 128], P('dp', 'seq')
- grad_inputs: float32 [8, 2048, 768], P('dp', 'seq')
- grad_query: float32 [768, 768], P(('seq', 'dp'))
- grad_keyval: float32 [768, 128], P(('seq', 'dp'))
- grad_out: float32 [768, 768], P(('seq', 'dp'))
- grad_up: float32 [768, 3072], P(('seq', 'dp'))
- grad_down: float32 [3072, 768], P(('seq', 'dp'))
- grad_gain: float32 [768, 2], P(('seq', 'dp'))
- grad_bias: float32 [768, 2], P(('seq', 'dp'))
The draws below stay inside these ranges and needn't reach their ends.
All inputs are finite; a program needn't handle non-finite values.
Results may differ from the reference program's by a relative error of at most 0.011.
Values may be sent and summed in bfloat16 or wider, within the bound.
No kernel may reach another device: no remote copies, remote signals or barrier semaphores. Data moves between devices by JAX's collectives and lax.ppermute only.
A program may use at most 128 MiB of HBM per device.

```python
import math
import jax
import jax.numpy as jnp
from jax import lax

D = 768
HEADS = 12
HEAD = 64
FF = 3072
ROT = 16
LENGTH = 2048
SEQS = 8


def shard_levels(key, shape, shards, least, high):
    level = 1.0
    for dim, parts in shards:
        heights = jax.random.uniform(jax.random.fold_in(jax.random.fold_in(key, 6), dim), (parts,), jnp.float32, least / len(shards), high / len(shards))
        level = level * jnp.repeat(jnp.exp(heights), shape[dim] // parts).reshape((-1,) + (1,) * (len(shape) - 1 - dim))
    return level


def bell_draw(own_key, shape, width, most, pieces=(), kind=jnp.bfloat16):
    values = jax.random.normal(own_key, shape, jnp.float32) * width
    if len(pieces) > 0:
        values = shard_levels(own_key, shape, pieces, -0.22, 0.18) * values
    return jnp.clip(values, min=-most, max=most).astype(kind)


def setup_inputs(seed: int = 0) -> dict:
    streams_of = jax.random.split(jax.random.key(seed), 11)
    return {
        "inputs": bell_draw(streams_of[0], (SEQS, LENGTH, D), 1.0, 6.0, ((0, 4), (1, 8))),
        "w_query": bell_draw(streams_of[1], (D, D), D ** -0.5, 0.21875, ((0, 32),)),
        "w_keyval": bell_draw(streams_of[2], (D, 2 * HEAD), D ** -0.5, 0.21875, ((0, 32),)),
        "w_out": bell_draw(streams_of[3], (D, D), (max(16 * D // LENGTH, 1)) ** -0.5, 2.5, ((0, 32),)),
        "w_up": bell_draw(streams_of[4], (D, FF), D ** -0.5, 0.21875, ((0, 32),)),
        "w_down": bell_draw(streams_of[5], (FF, D), FF ** -0.5, 0.109375, ((0, 32),)),
        "norm_gain": jnp.clip(1.0 + 0.18 * jax.random.normal(streams_of[6], (D, 2), jnp.float32), 0.099609375, 1.8984375).astype(jnp.bfloat16),
        "norm_bias": bell_draw(streams_of[7], (D, 2), 0.3, 1.5, ((0, 32),)),
        "out_cotangent": bell_draw(streams_of[8], (SEQS, LENGTH, D), 1.0, 6.0, ((0, 4), (1, 8))),
        "kv_cotangent": bell_draw(streams_of[9], (SEQS, LENGTH, 2 * HEAD), 1.0, 6.0, ((0, 4), (1, 8))),
    }


highest = lax.Precision.HIGHEST
epsilon = 1e-05
negative = -1e+30

@jax.custom_vjp
def low(v):
    return lax.optimization_barrier(v.astype(jnp.bfloat16)).astype(jnp.float32)

@jax.custom_vjp
def low_back(v):
    return v

def low_keep(v):
    return (low(v), None)

def low_pass(kept, grad):
    return (grad,)

def back_keep(v):
    return (v, None)

def back_low(kept, grad):
    return (low(grad),)
low.defvjp(low_keep, low_pass)
low_back.defvjp(back_keep, back_low)

def matmul(left, right):
    return jnp.dot(left, right, precision=highest, preferred_element_type=jnp.float32)

def layer_norm(values, gain, shift):
    center = values - lax.optimization_barrier(jnp.mean(values, axis=-1, keepdims=True))
    spread = lax.optimization_barrier(jnp.mean(center * center, axis=-1, keepdims=True))
    return center * lax.rsqrt(spread + epsilon) * gain + shift

def rotate(values, positions):
    half_rot = ROT // 2
    exponent = jnp.arange(half_rot, dtype=jnp.float32) * (2.0 / ROT)
    frequency = jnp.exp(-math.log(10000.0) * exponent)
    angles = (positions.astype(jnp.float32) * 0.25)[:, None] * frequency[None, :]
    cos_table = jnp.cos(angles)[:, None, :]
    sin_table = jnp.sin(angles)[:, None, :]
    first = values[..., :half_rot]
    second = values[..., half_rot:ROT]
    return jnp.concatenate([first * cos_table - second * sin_table, second * cos_table + first * sin_table, values[..., ROT:]], axis=-1)

def attend_sequence(items):
    queries, keys, values = items
    seq_len = queries.shape[0]
    block = min(512, seq_len)
    blocks = queries.reshape(seq_len // block, block, HEADS, HEAD)
    starts = jnp.arange(seq_len // block, dtype=jnp.int32) * block
    scale = 1.0 / math.sqrt(HEAD)

    def one_block(args):
        part, first = args
        raw = jnp.einsum('qhd,kd->hqk', part, keys, precision=highest)
        scores = low_back(raw * scale)
        query_pos = first + jnp.arange(block, dtype=jnp.int32)
        key_pos = jnp.arange(seq_len, dtype=jnp.int32)
        allowed = key_pos[None, :] <= query_pos[:, None]
        scores = jnp.where(allowed[None], scores, negative)
        peak = lax.optimization_barrier(jnp.max(scores, axis=-1, keepdims=True))
        weights = jnp.where(allowed[None], jnp.exp(scores - peak), 0.0)
        probs = low(weights / lax.optimization_barrier(jnp.sum(weights, axis=-1, keepdims=True)))
        return jnp.einsum('hqk,kd->qhd', probs, values, precision=highest)
    result = lax.map(jax.checkpoint(one_block), (blocks, starts))
    return result.reshape(seq_len, HEADS, HEAD)

def forward(inputs, w_query, w_keyval, w_out, w_up, w_down, norm_gain, norm_bias):
    seq_count, seq_len, _ = inputs.shape
    positions = jnp.arange(seq_len, dtype=jnp.int32)
    normed_attn = low(layer_norm(inputs, norm_gain[:, 0], norm_bias[:, 0]))
    normed_mlp = low(layer_norm(inputs, norm_gain[:, 1], norm_bias[:, 1]))
    query_pre = low_back(matmul(normed_attn, w_query))
    queries = low(rotate(query_pre.reshape(seq_count, seq_len, HEADS, HEAD), positions))
    keyval_pre = low_back(matmul(normed_attn, w_keyval))
    keys = low(rotate(keyval_pre[..., :HEAD][:, :, None, :], positions)[:, :, 0, :])
    values = low(keyval_pre[..., HEAD:])
    keyval = jnp.concatenate([keys, values], axis=-1)
    context = lax.map(attend_sequence, (queries, keys, values))
    context = low(low_back(context.reshape(seq_count, seq_len, D)))
    attn_out = matmul(context, w_out)
    hidden_pre = low_back(matmul(normed_mlp, w_up))
    hidden = low(jax.nn.gelu(hidden_pre, approximate=False))
    mlp_out = matmul(hidden, w_down)
    return (inputs + attn_out + mlp_out, keyval)

def reference(inputs, w_query, w_keyval, w_out, w_up, w_down, norm_gain, norm_bias, out_cotangent, kv_cotangent):
    floats = [arr.astype(jnp.float32) for arr in (inputs, w_query, w_keyval, w_out, w_up, w_down, norm_gain, norm_bias)]
    (output, keyval), pullback = jax.vjp(forward, *floats)
    grads = pullback((out_cotangent.astype(jnp.float32), kv_cotangent.astype(jnp.float32)))
    return (output.astype(jnp.bfloat16), keyval.astype(jnp.bfloat16), grads[0], grads[1], grads[2], grads[3], grads[4], grads[5], grads[6], grads[7])
```

```python
import functools
import math

import jax
import jax.numpy as jnp
from jax import lax
from jax.experimental import pallas as pl
from jax.experimental.pallas import tpu as pltpu
from jax.sharding import PartitionSpec as P

HEADS = 12
HEAD = 64
ROT = 16
TEAM = 4
MINE = HEADS // TEAM
WIDE = 2 * HEAD
EPSILON = 1e-05
BF = jnp.bfloat16
F32 = jnp.float32
SCALE = 1.0 / math.sqrt(HEAD)
MB = 1 << 20


def dot(left, right):
    return lax.dot_general(left, right, (((1,), (0,)), ((), ())), preferred_element_type=F32)


def dot_rt(left, right):
    return lax.dot_general(left, right, (((1,), (1,)), ((), ())), preferred_element_type=F32)


def dot_lt(left, right):
    return lax.dot_general(left, right, (((0,), (0,)), ((), ())), preferred_element_type=F32)


def lanes(shape):
    return lax.broadcasted_iota(jnp.int32, shape, len(shape) - 1)


def turn(values, cos_table, sin_table, sign):
    near = (lanes(values.shape) % HEAD) < ROT // 2
    swapped = jnp.where(
        near, pltpu.roll(values, WIDE - ROT // 2, 1), pltpu.roll(values, ROT // 2, 1)
    )
    return values * cos_table + (sign * swapped) * sin_table


def standardize(tokens):
    center = tokens - jnp.mean(tokens, axis=-1, keepdims=True)
    spread = jnp.mean(center * center, axis=-1, keepdims=True)
    scale = lax.rsqrt(spread + EPSILON)
    return center * scale, scale


def norm_back(hat, scale, pulled):
    return scale * (
        pulled
        - jnp.mean(pulled, axis=-1, keepdims=True)
        - hat * jnp.mean(pulled * hat, axis=-1, keepdims=True)
    )


def three_parts(column):
    high = column.astype(BF)
    rest = column - high.astype(F32)
    mid = rest.astype(BF)
    low = (rest - mid.astype(F32)).astype(BF)
    return high, mid, low


def marked(lane, base, parts):
    out = jnp.zeros(lane.shape, BF)
    for index, part in enumerate(parts):
        out = jnp.where(lane == base + index, part, out)
    return out


def prepare_kernel(x_ref, weight_ref, norm_ref, cos_ref, sin_ref, attn_ref, mlp_ref, query_ref, keyval_ref):
    tokens = x_ref[0, 0].astype(F32)
    hat, _ = standardize(tokens)
    normed = (hat * norm_ref[0:1, :] + norm_ref[2:3, :]).astype(BF)
    attn_ref[0, 0] = normed
    mlp_ref[0, 0] = (hat * norm_ref[1:2, :] + norm_ref[3:4, :]).astype(BF)
    made = dot(normed, weight_ref[...])
    cos_table = cos_ref[0]
    sin_table = sin_ref[0]
    keys_side = lanes(cos_table.shape) < HEAD
    keyval_ref[0, 0] = turn(
        made[:, :WIDE], jnp.where(keys_side, cos_table, 1.0), jnp.where(keys_side, sin_table, 0.0), 1.0
    ).astype(BF)
    for part in range(2):
        piece = made[:, WIDE * (part + 1) : WIDE * (part + 2)]
        query_ref[0, 0, :, WIDE * part : WIDE * (part + 1)] = (
            turn(piece, cos_table, sin_table, 1.0) * SCALE
        ).astype(BF)


def rank_of(own, block, top):
    return own ^ ((block % 2) * top) ^ (block // 2)


def slot_of(away, top, wide):
    return ((away // 2) % wide) * TEAM + (away // top) % 2 + 2 * (away % 2)


def forward_kernel(top, wide, own_ref, query_ref, keyval_ref, context_ref, marked_ref, low_ref, score_ref, peak_ref):
    rows = query_ref.shape[2]
    own = own_ref[0]
    rank = rank_of(own, pl.program_id(1), top)
    lane = lanes((rows, WIDE))
    first = query_ref[0, 0, :, :WIDE]
    last = query_ref[0, 0, :, WIDE:]
    heads = [first, pltpu.roll(first.astype(F32), HEAD, 1).astype(BF), last]
    for head in range(MINE):
        low_ref[head] = heads[head]
    keep = lax.broadcasted_iota(jnp.int32, (rows, rows), 1) <= lax.broadcasted_iota(
        jnp.int32, (rows, rows), 0
    )

    def keys_of(step):
        block = keyval_ref[slot_of(step ^ own, top, wide), 0]
        return block, jnp.where(lane < HEAD, block, jnp.zeros_like(block))

    def score(step, masked):
        _, keys = keys_of(step)
        for head in range(MINE):
            scores = dot_rt(low_ref[head], keys)
            if masked:
                scores = jnp.where(keep, scores, -1e30)
            score_ref[step, head] = scores
            best = jnp.maximum(scores[:, :WIDE], scores[:, WIDE:])
            peak_ref[head] = best if masked else jnp.maximum(peak_ref[head], best)

    score(rank, True)

    @pl.loop(0, rank)
    def _(step):
        score(step, False)

    for head in range(MINE):
        peak_ref[head] = jnp.broadcast_to(
            jnp.max(peak_ref[head], axis=-1, keepdims=True), (rows, WIDE)
        )

    def weigh(step, sums):
        block, _ = keys_of(step)
        block = jnp.where(lane < HEAD, jnp.ones_like(block), block)
        out = []
        for head in range(MINE):
            peak = peak_ref[head]
            weights = jnp.exp(
                score_ref[step, head] - jnp.concatenate([peak] * (rows // WIDE), axis=1)
            )
            out.append(sums[head] + dot(weights.astype(BF), block))
        return tuple(out)

    sums = lax.fori_loop(
        0, rank + 1, weigh, tuple(jnp.zeros((rows, WIDE), F32) for _ in range(MINE))
    )
    made = []
    for head in range(MINE):
        swapped = pltpu.roll(sums[head], HEAD, 1)
        total = jnp.where(lane < HEAD, sums[head], swapped)
        made.append(jnp.where(lane < HEAD, swapped, sums[head]) / total)
        logsum = peak_ref[head] + jnp.log(total)
        query = low_ref[head]
        marked_ref[0, 0, head] = jnp.where(
            lane < HEAD, query, marked(lane, HEAD, three_parts(-logsum))
        )
    context_ref[0, 0, :, :WIDE] = jnp.where(lane < HEAD, made[0], made[1]).astype(BF)
    context_ref[0, 0, :, WIDE:] = jnp.where(lane < HEAD, made[2], 0.0).astype(BF)


def context_kernel(context_ref, grad_ref, out_ref, marked_ref, total_ref):
    rows = context_ref.shape[2]
    grad = grad_ref[0, 0]
    context = context_ref[0, 0]
    lane = lanes((rows, WIDE))
    pulled = dot_rt(grad, out_ref[...]).astype(BF)
    product = pulled.astype(F32) * context.astype(F32)
    for head in range(MINE):
        column = WIDE * (head // 2)
        side = (lane < HEAD) if head % 2 == 0 else (lane >= HEAD)
        delta = jnp.sum(
            jnp.where(side, product[:, column : column + WIDE], 0.0), axis=-1, keepdims=True
        )
        piece = pulled[:, column : column + WIDE]
        if head % 2 == 0:
            piece = pltpu.roll(piece.astype(F32), HEAD, 1).astype(BF)
        marked_ref[0, 0, head] = jnp.where(
            lane >= HEAD, piece, marked(lane, 0, three_parts(jnp.broadcast_to(-delta, lane.shape)))
        )
    made = dot_lt(context, grad)
    first = (pl.program_id(0) == 0) & (pl.program_id(1) == 0)

    @pl.when(first)
    def _():
        total_ref[...] = made

    @pl.when(jnp.logical_not(first))
    def _():
        total_ref[...] += made


def backward_kernel(top, wide, own_ref, query_ref, grad_ref, keyval_ref, cos_ref, sin_ref, dquery_ref, dkeyval_ref, sum_ref):
    rows = query_ref.shape[3]
    own = own_ref[0]
    rank = rank_of(own, pl.program_id(0), top)
    lane = lanes((rows, WIDE))
    ones_low = jnp.where(lane < 3, 1.0, 0.0).astype(BF)
    ones_high = jnp.where((lane >= HEAD) & (lane < HEAD + 3), 1.0, 0.0).astype(BF)
    keep = lax.broadcasted_iota(jnp.int32, (rows, rows), 0) <= lax.broadcasted_iota(
        jnp.int32, (rows, rows), 1
    )

    @pl.when(pl.program_id(0) == 0)
    def _():
        dkeyval_ref[...] = jnp.zeros_like(dkeyval_ref)

    def visit(step, masked):
        slot = slot_of(step ^ own, top, wide)
        block = keyval_ref[slot, 0]
        keys = jnp.where(lane < HEAD, block, ones_high)
        values = jnp.where(lane < HEAD, ones_low, block)
        d_keys = jnp.zeros((rows, WIDE), F32)
        d_values = jnp.zeros((rows, WIDE), F32)
        for head in range(MINE):
            query = query_ref[0, 0, head]
            grad = grad_ref[0, 0, head]
            probs = jnp.exp(dot_rt(keys, query))
            if masked:
                probs = jnp.where(keep, probs, 0.0)
            d_scores = (probs * dot_rt(values, grad)).astype(BF)
            d_values += dot(probs.astype(BF), grad)
            d_keys += dot(d_scores, query)
            d_query = dot_lt(keys, d_scores)
            sum_ref[head] = d_query if masked else sum_ref[head] + d_query
        dkeyval_ref[slot] += jnp.where(lane < HEAD, d_keys, d_values)

    visit(rank, True)

    @pl.loop(0, rank)
    def _(step):
        visit(step, False)

    turned = [jnp.transpose(sum_ref[head]) * SCALE for head in range(MINE)]
    both = jnp.where(lane < HEAD, turned[0], pltpu.roll(turned[1], HEAD, 1))
    last = jnp.where(lane < HEAD, turned[2], 0.0)
    cos_table = cos_ref[0]
    sin_table = sin_ref[0]
    dquery_ref[0, :, :WIDE] = turn(both, cos_table, sin_table, -1.0).astype(BF)
    dquery_ref[0, :, WIDE:] = turn(last, cos_table, sin_table, -1.0).astype(BF)


def hidden_kernel(normed_ref, grad_ref, context_ref, up_ref, down_ref, out_ref, made_ref, dnormed_ref, gup_ref, gdown_ref, up_sum, down_sum):
    def flat(ref):
        return ref[0].reshape(ref.shape[1] * ref.shape[2], ref.shape[3])

    normed = flat(normed_ref)
    grad = flat(grad_ref)
    raw = dot(normed, up_ref[...])
    bell = 0.5 + 0.5 * lax.erf(raw * math.sqrt(0.5))
    slope = bell + raw * (jnp.exp(raw * raw * -0.5) * (1.0 / math.sqrt(2.0 * math.pi)))
    hidden = (raw * bell).astype(BF)
    d_raw = (dot_rt(grad, down_ref[...]) * slope).astype(BF)
    made = dot(hidden, down_ref[...]) + dot(flat(context_ref), out_ref[...])
    made_ref[0] = made.astype(BF).reshape(made_ref.shape[1:])
    dnormed_ref[0] = dot_rt(d_raw, up_ref[...]).astype(BF).reshape(dnormed_ref.shape[1:])
    step = pl.program_id(0)
    gdown = dot_lt(hidden, grad)
    gup = dot_lt(normed, d_raw)

    @pl.when(step == 0)
    def _():
        down_sum[...] = gdown
        up_sum[...] = gup

    @pl.when(step > 0)
    def _():
        down_sum[...] += gdown
        up_sum[...] += gup

    @pl.when(step == pl.num_programs(0) - 1)
    def _():
        gdown_ref[...] = down_sum[...].astype(BF)
        gup_ref[...] = up_sum[...].astype(BF)


def tokens_kernel(x_ref, normed_ref, dnormed_ref, dquery_ref, weight_ref, norm_ref, dx_ref, gquery_ref, gnorm_ref):
    hat, scale = standardize(x_ref[0, 0].astype(F32))
    d_query = dquery_ref[0, 0]
    d_attn = dot_rt(d_query, weight_ref[...])
    d_mlp = dnormed_ref[0, 0].astype(F32)
    dx_ref[0, 0] = norm_back(hat, scale, d_attn * norm_ref[0:1, :] + d_mlp * norm_ref[1:2, :]).astype(BF)
    sums = [
        jnp.sum(piece, axis=0, keepdims=True) for piece in (d_attn * hat, d_mlp * hat, d_attn, d_mlp)
    ]
    sums = jnp.concatenate(sums + [jnp.zeros_like(sums[0])] * 4, axis=0)
    gquery = dot_lt(normed_ref[0, 0], d_query)
    first = (pl.program_id(0) == 0) & (pl.program_id(1) == 0)

    @pl.when(first)
    def _():
        gquery_ref[...] = gquery
        gnorm_ref[...] = sums

    @pl.when(jnp.logical_not(first))
    def _():
        gquery_ref[...] += gquery
        gnorm_ref[...] += sums


def keyval_kernel(x_ref, normed_ref, dkeyval_ref, cotangent_ref, weight_ref, norm_ref, cos_ref, sin_ref, dx_ref, gkeyval_ref, gnorm_ref):
    hat, scale = standardize(x_ref[0].astype(F32))
    keys_side = lanes(cos_ref.shape[1:]) < HEAD
    d_keyval = dkeyval_ref[0] + cotangent_ref[0].astype(F32)
    d_pre = turn(
        d_keyval, jnp.where(keys_side, cos_ref[0], 1.0), jnp.where(keys_side, sin_ref[0], 0.0), -1.0
    ).astype(BF)
    d_attn = dot_rt(d_pre, weight_ref[...])
    dx_ref[0] = norm_back(hat, scale, d_attn * norm_ref[0:1, :])
    sums = [jnp.sum(piece, axis=0, keepdims=True) for piece in (d_attn * hat, d_attn)]
    blank = jnp.zeros_like(sums[0])
    sums = jnp.concatenate([sums[0], blank, sums[1]] + [blank] * 5, axis=0)
    gkeyval = dot_lt(normed_ref[0, 0], d_pre)
    first = pl.program_id(0) == 0

    @pl.when(first)
    def _():
        gkeyval_ref[...] = gkeyval
        gnorm_ref[...] = sums

    @pl.when(jnp.logical_not(first))
    def _():
        gkeyval_ref[...] += gkeyval
        gnorm_ref[...] += sums


def params(limit):
    return pltpu.CompilerParams(vmem_limit_bytes=limit * MB)


def cost(flops, moved, exps=0):
    return pl.CostEstimate(flops=int(flops), bytes_accessed=int(moved), transcendentals=int(exps))


def struct(shape, kind):
    return jax.ShapeDtypeStruct(shape, kind)


def whole(*shape):
    return pl.BlockSpec(shape, lambda *_: (0,) * len(shape))


def on_device(nseq, ndp, inputs, w_query, w_keyval, w_out, w_up, w_down, norm_gain, norm_bias, out_cotangent, kv_cotangent):
    count, rows, width = inputs.shape
    top = nseq // 2
    wide = nseq // TEAM
    own = lax.axis_index("seq")
    own_y, own_x, own_c = own // top, (own // 2) % wide, own % 2
    own_z = lax.axis_index("dp")
    share = w_query.shape[0]
    hidden = w_up.shape[1] // TEAM
    heads_wide = MINE * HEAD

    def flip(value, mask):
        return lax.ppermute(value, "seq", [(i, i ^ mask) for i in range(nseq)])

    def flip_z(value, mask):
        return lax.ppermute(value, "dp", [(i, i ^ mask) for i in range(ndp)])

    def in_order(bit, mine, other, axis):
        return jnp.where(
            bit == 0, jnp.stack([mine, other], axis), jnp.stack([other, mine], axis)
        )

    def pick(value, index, axis):
        return lax.dynamic_index_in_dim(value, index, axis, keepdims=False)

    def gather(value):
        value = value[None]
        mask = ndp // 2
        while mask:
            value = in_order((own_z // mask) % 2, value, flip_z(value, mask), 1)
            value = value.reshape((-1,) + value.shape[2:])
            mask //= 2
        value = value[None]
        mask = wide // 2
        while mask:
            value = in_order((own_x // mask) % 2, value, flip(value, 2 * mask), 1)
            value = value.reshape((-1,) + value.shape[2:])
            mask //= 2
        return value

    def scatter(value):
        mask = wide // 2
        while mask:
            bit = (own_x // mask) % 2
            value = value.reshape((2, -1) + value.shape[1:])
            got = flip(pick(value, 1 - bit, 0), 2 * mask)
            value = (pick(value, bit, 0).astype(F32) + got.astype(F32)).astype(BF)
            mask //= 2
        value = value.reshape(value.shape[1:])
        mask = 1
        while mask < ndp:
            bit = (own_z // mask) % 2
            value = value.reshape((-1, 2) + value.shape[1:])
            got = flip_z(pick(value, 1 - bit, 1).astype(BF), mask)
            value = pick(value, bit, 1).astype(F32) + got.astype(F32)
            mask *= 2
        return value.reshape(value.shape[1:])

    def team(value):
        value = value[None]
        value = jnp.concatenate([value, flip(value, top)], axis=0)
        return jnp.concatenate([value, flip(value, 1)], axis=0)

    norms = jnp.concatenate([norm_gain, norm_bias], axis=1)
    queries_of = w_query.reshape(share, 2, 2, heads_wide).transpose(1, 2, 0, 3)
    same = jnp.concatenate([w_keyval, norms], axis=1)
    ups = w_up.reshape(share, 2, wide, 2, hidden // wide).transpose(1, 3, 0, 2, 4)
    ups = ups.reshape(2, 2, share, hidden)
    pad = jnp.zeros((2, 2, share, 3 * WIDE - WIDE - heads_wide - norms.shape[1]), BF)
    spread = (2, 2, share)
    pack = jnp.concatenate(
        [
            jnp.broadcast_to(same[:, :WIDE], spread + (WIDE,)),
            queries_of,
            jnp.broadcast_to(same[:, WIDE:], spread + (norms.shape[1],)),
            pad,
            ups,
        ],
        axis=3,
    )
    pack = in_order(own_y, pick(pack, own_y, 0), flip(pick(pack, 1 - own_y, 0), top), 0)
    pack = in_order(own_c, pick(pack, own_c, 1), flip(pick(pack, 1 - own_c, 1), 1), 1)

    def moved(target_of):
        pairs = []
        for rank in range(nseq):
            for z in range(ndp):
                member = 2 * (rank // top) + rank % 2
                place = ((rank // 2) % wide) * ndp + z
                pairs.append((member * (nseq * ndp // TEAM) + place, rank * ndp + z))
        return [pair if target_of else pair[::-1] for pair in pairs]

    out_rows = lax.ppermute(w_out, ("seq", "dp"), moved(True))

    tokens = team(inputs)

    def rows_of(value):
        order = (2, 0, 3, 1, 4, 5)
        return value.transpose(order).reshape(-1, value.shape[-1])

    front = rows_of(gather(pack[..., : 3 * WIDE]))
    low_rows = jnp.concatenate([out_rows, w_down], axis=0)
    back = gather(low_rows)
    full_out = back[:, :, :share].reshape(heads_wide, width)
    full_out = jnp.concatenate([full_out, jnp.zeros((2 * WIDE - heads_wide, width), BF)], axis=0)
    full_down = back[:, :, share:].reshape(hidden, width)
    full_up = rows_of(gather(pack[..., 3 * WIDE :]))
    grads = team(out_cotangent)

    norm_rows = front[:, WIDE + heads_wide : WIDE + heads_wide + 4].astype(F32).T
    norm_rows = jnp.concatenate([norm_rows, jnp.zeros_like(norm_rows)], axis=0)

    lane = jnp.arange(WIDE, dtype=jnp.int32) % HEAD
    frequency = jnp.exp(
        -math.log(10000.0) * ((lane % (ROT // 2)).astype(F32) * (2.0 / ROT))
    )
    ranks = jnp.stack([rank_of(own, r, top) for r in range(TEAM)])
    positions = ranks[:, None] * rows + jnp.arange(rows, dtype=jnp.int32)[None]
    angles = (positions.astype(F32) * 0.25)[..., None] * frequency
    cos_table = jnp.where(lane < ROT, jnp.cos(angles), 1.0)
    sin_table = jnp.where(lane < ROT, jnp.sin(angles), 0.0)
    sin_table = jnp.where(lane < ROT // 2, -sin_table, sin_table)
    own_rank = own.reshape(1).astype(jnp.int32)

    total = TEAM * count * rows

    def by_rows(last):
        return pl.BlockSpec((1, 1, rows, last), lambda r, b, *_: (r, b, 0, 0))

    table = pl.BlockSpec((1, rows, WIDE), lambda r, *_: (r, 0, 0))
    normed_attn, normed_mlp, queries, keyval = pl.pallas_call(
        prepare_kernel,
        grid=(TEAM, count),
        in_specs=[by_rows(width), whole(*front.shape), whole(8, width), table, table],
        out_specs=[by_rows(width), by_rows(width), by_rows(2 * WIDE), by_rows(WIDE)],
        out_shape=[
            struct((TEAM, count, rows, width), BF),
            struct((TEAM, count, rows, width), BF),
            struct((TEAM, count, rows, 2 * WIDE), BF),
            struct((TEAM, count, rows, WIDE), BF),
        ],
        compiler_params=params(40),
        cost_estimate=cost(2 * total * width * 3 * WIDE, total * width * 6),
        name="prepare",
    )(tokens, front, norm_rows, cos_table, sin_table)

    everyone = keyval
    mask = 1
    while mask < wide:
        everyone = jnp.concatenate([everyone, flip(everyone, 2 * mask)], axis=0)
        mask *= 2
    slots = TEAM * wide
    pairs = MINE * total * (slots // 2 + 1) * rows

    by_query = pl.BlockSpec((1, 1, rows, 2 * WIDE), lambda b, r, *_: (r, b, 0, 0))
    by_heads = pl.BlockSpec((1, 1, MINE, rows, WIDE), lambda b, r, *_: (r, b, 0, 0, 0))
    context, marked_query = pl.pallas_call(
        functools.partial(forward_kernel, top, wide),
        grid_spec=pltpu.PrefetchScalarGridSpec(
            num_scalar_prefetch=1,
            grid=(count, TEAM),
            in_specs=[
                by_query,
                pl.BlockSpec((slots, 1, rows, WIDE), lambda b, r, *_: (0, b, 0, 0)),
            ],
            out_specs=[by_query, by_heads],
            scratch_shapes=[
                pltpu.VMEM((MINE, rows, WIDE), BF),
                pltpu.VMEM((slots, MINE, rows, rows), F32),
                pltpu.VMEM((MINE, rows, WIDE), F32),
            ],
        ),
        out_shape=[
            struct((TEAM, count, rows, 2 * WIDE), BF),
            struct((TEAM, count, MINE, rows, WIDE), BF),
        ],
        compiler_params=params(40),
        cost_estimate=cost(pairs * 2 * 4 * HEAD, total * WIDE * 8, pairs),
        name="attend",
    )(own_rank, queries, everyone)

    by_grad = pl.BlockSpec((1, 1, rows, width), lambda b, r, *_: (r, b, 0, 0))
    marked_grad, grad_out_local = pl.pallas_call(
        context_kernel,
        grid=(count, TEAM),
        in_specs=[by_query, by_grad, whole(*full_out.shape)],
        out_specs=[by_heads, whole(*full_out.shape)],
        out_shape=[
            struct((TEAM, count, MINE, rows, WIDE), BF),
            struct(full_out.shape, F32),
        ],
        compiler_params=params(40),
        cost_estimate=cost(4 * total * width * 2 * WIDE, total * width * 4),
        name="pull_context",
    )(context, grads, full_out)

    by_seqs = pl.BlockSpec((1, count, rows, width), lambda r: (r, 0, 0, 0))
    made, d_normed, grad_up_local, grad_down_local = pl.pallas_call(
        hidden_kernel,
        grid=(TEAM,),
        in_specs=[
            by_seqs,
            by_seqs,
            pl.BlockSpec((1, count, rows, 2 * WIDE), lambda r: (r, 0, 0, 0)),
            whole(width, hidden),
            whole(hidden, width),
            whole(*full_out.shape),
        ],
        out_specs=[by_seqs, by_seqs, whole(width, hidden), whole(hidden, width)],
        out_shape=[
            struct((TEAM, count, rows, width), BF),
            struct((TEAM, count, rows, width), BF),
            struct((width, hidden), BF),
            struct((hidden, width), BF),
        ],
        scratch_shapes=[pltpu.VMEM((width, hidden), F32), pltpu.VMEM((hidden, width), F32)],
        compiler_params=params(56),
        cost_estimate=cost(12 * total * width * hidden, total * width * 10, total * hidden * 2),
        name="hidden",
    )(normed_mlp, grads, context, full_up, full_down, full_out)

    def team_sum(value):
        got = flip(value[2:], 1)
        value = value[:2].astype(F32) + got.astype(F32)
        return value[0] + flip(value[1].astype(BF), top).astype(F32)

    output = (inputs.astype(F32) + team_sum(made)).astype(BF)

    d_queries = []
    d_keyvals = []
    for b in range(count):
        d_query, d_keyval = pl.pallas_call(
            functools.partial(backward_kernel, top, wide),
            grid_spec=pltpu.PrefetchScalarGridSpec(
                num_scalar_prefetch=1,
                grid=(TEAM,),
                in_specs=[
                    pl.BlockSpec((1, 1, MINE, rows, WIDE), lambda r, *_, b=b: (r, b, 0, 0, 0)),
                    pl.BlockSpec((1, 1, MINE, rows, WIDE), lambda r, *_, b=b: (r, b, 0, 0, 0)),
                    pl.BlockSpec((slots, 1, rows, WIDE), lambda r, *_, b=b: (0, b, 0, 0)),
                    table,
                    table,
                ],
                out_specs=[
                    pl.BlockSpec((1, rows, 2 * WIDE), lambda r, *_: (r, 0, 0)),
                    whole(slots, rows, WIDE),
                ],
                scratch_shapes=[pltpu.VMEM((MINE, WIDE, rows), F32)],
            ),
            out_shape=[
                struct((TEAM, rows, 2 * WIDE), BF),
                struct((slots, rows, WIDE), F32),
            ],
            compiler_params=params(40),
            cost_estimate=cost(pairs * 2 * 5 * HEAD, total * WIDE * 8, pairs),
            name="attend_back",
        )(own_rank, marked_query, marked_grad, everyone, cos_table, sin_table)
        d_queries.append(d_query)
        mask = wide // 2
        while mask:
            half = d_keyval.shape[0] // 2
            got = flip(d_keyval[half:].astype(BF), 2 * mask)
            d_keyval = d_keyval[:half] + got.astype(F32)
            mask //= 2
        got = flip(d_keyval[2:].astype(BF), 1)
        d_keyval = d_keyval[:2] + got.astype(F32)
        d_keyvals.append(d_keyval[0] + flip(d_keyval[1].astype(BF), top).astype(F32))
    d_queries = jnp.stack(d_queries, axis=1)
    d_keyvals = jnp.stack(d_keyvals)

    query_weight = jnp.concatenate(
        [front[:, WIDE : WIDE + heads_wide], jnp.zeros((width, 2 * WIDE - heads_wide), BF)], axis=1
    )
    d_tokens, grad_query_local, norm_sums = pl.pallas_call(
        tokens_kernel,
        grid=(TEAM, count),
        in_specs=[
            by_rows(width),
            by_rows(width),
            by_rows(width),
            by_rows(2 * WIDE),
            whole(*query_weight.shape),
            whole(8, width),
        ],
        out_specs=[by_rows(width), whole(*query_weight.shape), whole(8, width)],
        out_shape=[
            struct((TEAM, count, rows, width), BF),
            struct(query_weight.shape, F32),
            struct((8, width), F32),
        ],
        compiler_params=params(40),
        cost_estimate=cost(4 * total * width * 2 * WIDE, total * width * 8),
        name="pull_tokens",
    )(tokens, normed_attn, d_normed, d_queries, query_weight, norm_rows)

    by_own = pl.BlockSpec((1, rows, width), lambda b: (b, 0, 0))
    by_keys = pl.BlockSpec((1, rows, WIDE), lambda b: (b, 0, 0))
    own_table = pl.BlockSpec((1, rows, WIDE), lambda b: (0, 0, 0))
    d_own, grad_keyval_local, norm_sums_own = pl.pallas_call(
        keyval_kernel,
        grid=(count,),
        in_specs=[
            by_own,
            pl.BlockSpec((1, 1, rows, width), lambda b: (0, b, 0, 0)),
            by_keys,
            by_keys,
            pl.BlockSpec((width, WIDE), lambda b: (0, 0)),
            whole(8, width),
            own_table,
            own_table,
        ],
        out_specs=[by_own, whole(width, WIDE), whole(8, width)],
        out_shape=[
            struct((count, rows, width), F32),
            struct((width, WIDE), F32),
            struct((8, width), F32),
        ],
        compiler_params=params(40),
        cost_estimate=cost(4 * count * rows * width * WIDE, count * rows * width * 8),
        name="pull_keyval",
    )(inputs, normed_attn, d_keyvals, kv_cotangent, front, norm_rows, cos_table, sin_table)

    grad_inputs = out_cotangent.astype(F32) + d_own + team_sum(d_tokens)

    def grouped(value):
        value = value.reshape(2, wide, 2, ndp, share, value.shape[-1])
        return value.transpose(1, 3, 0, 2, 4, 5)

    low_grads = jnp.concatenate(
        [
            grad_out_local[:heads_wide].astype(BF).reshape(wide, ndp, share, width),
            grad_down_local.reshape(wide, ndp, hidden // (wide * ndp), width),
        ],
        axis=2,
    )
    low_grads = scatter(low_grads)
    grad_down = low_grads[share:]
    grad_out = lax.ppermute(low_grads[:share].astype(BF), ("seq", "dp"), moved(False)).astype(F32)
    up_grads = scatter(grouped(grad_up_local))
    front_local = jnp.concatenate(
        [grad_keyval_local, grad_query_local[:, :heads_wide], (norm_sums + norm_sums_own)[:4].T],
        axis=1,
    ).astype(BF)
    front_grads = scatter(grouped(front_local))

    def swap_back(value, summed):
        got = flip(pick(value, 1 - own_c, 1).astype(BF), 1).astype(F32)
        mine = pick(value, own_c, 1)
        parts = in_order(own_c, mine[..., summed:], got[..., summed:], 1)
        sums = mine[..., :summed] + got[..., :summed]
        sent = jnp.concatenate([sums, parts[:, 0], parts[:, 1]], axis=-1)
        got = flip(pick(sent, 1 - own_y, 0).astype(BF), top).astype(F32)
        mine = pick(sent, own_y, 0)
        parts = in_order(own_y, mine[..., summed:], got[..., summed:], 1)
        return mine[..., :summed] + got[..., :summed], parts

    _, grad_up = swap_back(up_grads, 0)
    grad_up = grad_up.reshape(share, 2, 2, wide, hidden // wide).transpose(0, 1, 3, 2, 4)
    grad_up = grad_up.reshape(share, TEAM * hidden)
    ends = front_grads[..., WIDE + heads_wide :]
    front_grads = jnp.concatenate([front_grads[..., :WIDE], ends, front_grads[..., WIDE : WIDE + heads_wide]], axis=-1)
    sums, grad_query = swap_back(front_grads, WIDE + ends.shape[-1])
    grad_query = grad_query.reshape(share, HEADS * HEAD)
    return (
        output,
        keyval[0],
        grad_inputs,
        grad_query,
        sums[:, :WIDE],
        grad_out,
        grad_up,
        grad_down,
        sums[:, WIDE : WIDE + 2],
        sums[:, WIDE + 2 : WIDE + 4],
    )


def solution(mesh):
    rows = P("dp", "seq", None)
    split = P(("seq", "dp"), None)
    return jax.shard_map(
        functools.partial(on_device, mesh.shape["seq"], mesh.shape["dp"]),
        mesh=mesh,
        in_specs=(rows,) + (split,) * 7 + (rows, rows),
        out_specs=(rows,) * 3 + (split,) * 7,
        check_vma=False,
    )
```

```python
import functools
import math

import jax
import jax.numpy as jnp
from jax import lax
from jax.experimental import pallas as pl
from jax.experimental.pallas import tpu as pltpu
from jax.sharding import PartitionSpec as P

HEADS = 12
HEAD = 64
ROT = 16
TEAM = 4
MINE = HEADS // TEAM
WIDE = 2 * HEAD
EPSILON = 1e-05
BF = jnp.bfloat16
F32 = jnp.float32
SCALE = 1.0 / math.sqrt(HEAD)
MB = 1 << 20


def dot(left, right):
    return lax.dot_general(left, right, (((1,), (0,)), ((), ())), preferred_element_type=F32)


def dot_rt(left, right):
    return lax.dot_general(left, right, (((1,), (1,)), ((), ())), preferred_element_type=F32)


def dot_lt(left, right):
    return lax.dot_general(left, right, (((0,), (0,)), ((), ())), preferred_element_type=F32)


def lanes(shape):
    return lax.broadcasted_iota(jnp.int32, shape, len(shape) - 1)


def turn(values, cos_table, sin_table, sign):
    near = (lanes(values.shape) % HEAD) < ROT // 2
    swapped = jnp.where(
        near, pltpu.roll(values, WIDE - ROT // 2, 1), pltpu.roll(values, ROT // 2, 1)
    )
    return values * cos_table + (sign * swapped) * sin_table


def standardize(tokens):
    center = tokens - jnp.mean(tokens, axis=-1, keepdims=True)
    spread = jnp.mean(center * center, axis=-1, keepdims=True)
    scale = lax.rsqrt(spread + EPSILON)
    return center * scale, scale


def norm_back(hat, scale, pulled):
    return scale * (
        pulled
        - jnp.mean(pulled, axis=-1, keepdims=True)
        - hat * jnp.mean(pulled * hat, axis=-1, keepdims=True)
    )


def three_parts(column):
    high = column.astype(BF)
    rest = column - high.astype(F32)
    mid = rest.astype(BF)
    low = (rest - mid.astype(F32)).astype(BF)
    return high, mid, low


def marked(lane, base, parts):
    out = jnp.zeros(lane.shape, BF)
    for index, part in enumerate(parts):
        out = jnp.where(lane == base + index, part, out)
    return out


def choose(r, refs, held):
    for index, ref in enumerate(refs):

        @pl.when(r == index)
        def _(ref=ref):
            held[...] = ref[...].reshape(held.shape)


def put(r, near_ref, far_ref, value):
    @pl.when(r < 2)
    def _():
        near_ref[0] = value

    @pl.when(r >= 2)
    def _():
        far_ref[0] = value


def assemble(own_x, refs, groups, held):
    wide = sum(ref.shape[0] for ref in refs)
    relative = 0
    for ref in refs:
        block = ref.shape[2]
        for index in range(ref.shape[0]):
            x = own_x ^ relative
            for group in range(groups):
                place = (group // 2 * wide + x) * 2 + group % 2 if groups > 1 else x
                start = pl.multiple_of(place * block, block)
                held[pl.ds(start, block), :] = ref[index, group]
            relative += 1


def prepare_kernel(parts, first, own_ref, *refs):
    x_refs, refs = refs[:4], refs[4:]
    front_refs, refs = refs[:parts], refs[parts:]
    cos_ref, sin_ref, attn_ref, mlp_ref, query_ref, keyval_ref, *refs = refs
    if first:
        front_ref, norm_ref, held = refs

        @pl.when(pl.program_id(0) == 0)
        def _():
            assemble(own_ref[0], front_refs, TEAM, front_ref)
            tail = front_ref[:, 2 * WIDE :].astype(F32)
            norm_ref[...] = jnp.transpose(tail)[HEAD : HEAD + 8]
    else:
        (held,) = refs
        front_ref, norm_ref = front_refs
    choose(pl.program_id(0), x_refs, held)
    hat, _ = standardize(held[...].astype(F32))
    normed = (hat * norm_ref[0:1, :] + norm_ref[2:3, :]).astype(BF)
    attn_ref[0] = normed
    mlp_ref[0] = (hat * norm_ref[1:2, :] + norm_ref[3:4, :]).astype(BF)
    made = dot(normed, front_ref[...])
    cos_table = cos_ref[0]
    sin_table = sin_ref[0]
    keys_side = lanes(cos_table.shape) < HEAD
    keyval_ref[0] = turn(
        made[:, :WIDE], jnp.where(keys_side, cos_table, 1.0), jnp.where(keys_side, sin_table, 0.0), 1.0
    ).astype(BF)
    for part in range(2):
        piece = made[:, WIDE * (part + 1) : WIDE * (part + 2)]
        query_ref[0, :, WIDE * part : WIDE * (part + 1)] = (
            turn(piece, cos_table, sin_table, 1.0) * SCALE
        ).astype(BF)


def rank_of(own, block, top):
    return own ^ ((block % 2) * top) ^ (block // 2)


def slot_of(away, top, wide):
    return ((away // 2) % wide) * TEAM + (away // top) % 2 + 2 * (away % 2)


def load_keyval(refs, keys_ref, values_ref, base):
    start = 0
    for ref in refs:
        count, rows, _ = ref.shape
        lane = lanes((rows, WIDE))
        for index in range(count):
            block = ref[index]
            keys_ref[start + index] = jnp.where(lane < HEAD, block, base[1])
            values_ref[start + index] = jnp.where(lane < HEAD, base[0], block)
        start += count


def forward_kernel(top, wide, own_ref, query_ref, *refs):
    kv_refs, (context_ref, marked_ref, low_ref, score_ref, peak_ref, keys_ref, values_ref) = refs[:-7], refs[-7:]
    rows = query_ref.shape[1]
    own = own_ref[0]
    rank = rank_of(own, pl.program_id(0), top)
    lane = lanes((rows, WIDE))
    one = jnp.ones((rows, WIDE), BF)

    @pl.when(pl.program_id(0) == 0)
    def _():
        load_keyval(kv_refs, keys_ref, values_ref, (one, jnp.zeros_like(one)))

    first = query_ref[0, :, :WIDE]
    low_ref[:rows] = first
    low_ref[rows : 2 * rows] = pltpu.roll(first.astype(F32), HEAD, 1).astype(BF)
    low_ref[2 * rows :] = query_ref[0, :, WIDE:]
    keep = lax.broadcasted_iota(jnp.int32, (rows, rows), 1) <= lax.broadcasted_iota(
        jnp.int32, (rows, rows), 0
    )
    keep = jnp.concatenate([keep] * MINE, axis=0)

    def score(step, masked):
        scores = dot_rt(low_ref[...], keys_ref[slot_of(step ^ own, top, wide)])
        if masked:
            scores = jnp.where(keep, scores, -1e30)
        score_ref[step] = scores
        best = jnp.maximum(scores[:, :WIDE], scores[:, WIDE:])
        peak_ref[...] = best if masked else jnp.maximum(peak_ref[...], best)

    score(rank, True)

    @pl.loop(0, rank)
    def _(step):
        score(step, False)

    peak_ref[...] = jnp.broadcast_to(jnp.max(peak_ref[...], axis=-1, keepdims=True), peak_ref.shape)

    def weigh(step, sums):
        peak = peak_ref[...]
        weights = jnp.exp(score_ref[step] - jnp.concatenate([peak] * (rows // WIDE), axis=1))
        return sums + dot(weights.astype(BF), values_ref[slot_of(step ^ own, top, wide)])

    sums = lax.fori_loop(0, rank + 1, weigh, jnp.zeros((MINE * rows, WIDE), F32))
    made = []
    for head in range(MINE):
        at = slice(head * rows, (head + 1) * rows)
        part = sums[at]
        swapped = pltpu.roll(part, HEAD, 1)
        total = jnp.where(lane < HEAD, part, swapped)
        made.append(jnp.where(lane < HEAD, swapped, part) / total)
        logsum = peak_ref[at] + jnp.log(total)
        marked_ref[0, head] = jnp.where(
            lane < HEAD, low_ref[at], marked(lane, HEAD, three_parts(-logsum))
        )
    context_ref[0, :, :WIDE] = jnp.where(lane < HEAD, made[0], made[1]).astype(BF)
    context_ref[0, :, WIDE:] = jnp.where(lane < HEAD, made[2], 0.0).astype(BF)


def backward_kernel(top, wide, own_ref, query_ref, grad_ref, cos_ref, sin_ref, *refs):
    kv_refs, (dquery_ref, keep_ref, send_ref, sum_ref, keys_ref, values_ref, dkeyval_ref) = refs[:-7], refs[-7:]
    rows = query_ref.shape[2]
    own = own_ref[0]
    rank = rank_of(own, pl.program_id(0), top)
    lane = lanes((rows, WIDE))
    keep = lax.broadcasted_iota(jnp.int32, (rows, rows), 0) <= lax.broadcasted_iota(
        jnp.int32, (rows, rows), 1
    )

    @pl.when(pl.program_id(0) == 0)
    def _():
        dkeyval_ref[...] = jnp.zeros_like(dkeyval_ref)
        ones_low = jnp.where(lane < 3, 1.0, 0.0).astype(BF)
        ones_high = jnp.where((lane >= HEAD) & (lane < HEAD + 3), 1.0, 0.0).astype(BF)
        load_keyval(kv_refs, keys_ref, values_ref, (ones_low, ones_high))

    def visit(step, masked):
        slot = slot_of(step ^ own, top, wide)
        keys = keys_ref[slot]
        values = values_ref[slot]
        d_keys = jnp.zeros((rows, WIDE), F32)
        d_values = jnp.zeros((rows, WIDE), F32)
        for head in range(MINE):
            query = query_ref[0, head]
            grad = grad_ref[0, head]
            probs = jnp.exp(dot_rt(keys, query))
            if masked:
                probs = jnp.where(keep, probs, 0.0)
            d_scores = (probs * dot_rt(values, grad)).astype(BF)
            d_values += dot(probs.astype(BF), grad)
            d_keys += dot(d_scores, query)
            d_query = dot_lt(keys, d_scores)
            sum_ref[head] = d_query if masked else sum_ref[head] + d_query
        dkeyval_ref[slot] += jnp.where(lane < HEAD, d_keys, d_values)

    visit(rank, True)

    @pl.loop(0, rank)
    def _(step):
        visit(step, False)

    turned = [jnp.transpose(sum_ref[head]) * SCALE for head in range(MINE)]
    both = jnp.where(lane < HEAD, turned[0], pltpu.roll(turned[1], HEAD, 1))
    last = jnp.where(lane < HEAD, turned[2], 0.0)
    cos_table = cos_ref[0]
    sin_table = sin_ref[0]
    dquery_ref[0, :, :WIDE] = turn(both, cos_table, sin_table, -1.0).astype(BF)
    dquery_ref[0, :, WIDE:] = turn(last, cos_table, sin_table, -1.0).astype(BF)

    @pl.when(pl.program_id(0) == pl.num_programs(0) - 1)
    def _():
        half = send_ref.shape[0]
        keep_ref[...] = dkeyval_ref[:half]
        send_ref[...] = dkeyval_ref[half:].astype(BF)


def split_rows(own_x, groups, total, keep_ref, send_ref):
    wide = 2 * keep_ref.shape[0]
    block = keep_ref.shape[2]
    for side, ref in enumerate((keep_ref, send_ref)):
        half = own_x // (wide // 2) ^ side
        for index in range(wide // 2):
            x = half * (wide // 2) + index
            for group in range(groups):
                place = (group // 2 * wide + x) * 2 + group % 2 if groups > 1 else x
                start = pl.multiple_of(place * block, block)
                ref[index, group] = total[pl.ds(start, block), :].astype(ref.dtype)


def hidden_kernel(count, parts, own_ref, *refs):
    grad_refs, refs = refs[:4], refs[4:]
    normed_refs, refs = refs[:count], refs[count:]
    context_refs, refs = refs[:count], refs[count:]
    more_refs, refs = refs[:parts], refs[parts:]
    down_refs, refs = refs[:parts], refs[parts:]
    (made_ref, made_far_ref, dnormed_ref, marked_ref, more_keep, more_send, down_keep, down_send, *refs) = refs
    (up_sum, down_sum, out_sum, held, up_ref, down_ref, out_ref) = refs
    step = pl.program_id(0)
    own_x = own_ref[0]

    @pl.when(step == 0)
    def _():
        out_ref[...] = jnp.zeros_like(out_ref)
        assemble(own_x, more_refs, TEAM, up_ref)
        assemble(own_x, [ref.at[:, TEAM:] for ref in more_refs], 1, out_ref)
        assemble(own_x, down_refs, 1, down_ref)

    rows = normed_refs[0].shape[1]
    normed = jnp.concatenate([ref[0] for ref in normed_refs], axis=0)
    context = jnp.concatenate([ref[0] for ref in context_refs], axis=0)
    choose(step, grad_refs, held)
    grad = held[...]
    raw = dot(normed, up_ref[...])
    bell = 0.5 + 0.5 * lax.erf(raw * math.sqrt(0.5))
    slope = bell + raw * (jnp.exp(raw * raw * -0.5) * (1.0 / math.sqrt(2.0 * math.pi)))
    hidden = (raw * bell).astype(BF)
    d_raw = (dot_rt(grad, down_ref[...]) * slope).astype(BF)
    made = dot(hidden, down_ref[...]) + dot(context, out_ref[...])
    put(step, made_ref, made_far_ref, made.astype(BF).reshape(made_ref.shape[1:]))
    dnormed_ref[0] = dot_rt(d_raw, up_ref[...]).astype(BF).reshape(dnormed_ref.shape[1:])
    gdown = dot_lt(hidden, grad)
    gup = dot_lt(normed, d_raw)
    gout = dot_lt(context, grad)

    pulled = dot_rt(grad, out_ref[...]).astype(BF)
    product = pulled.astype(F32) * context.astype(F32)
    lane = lanes((count * rows, WIDE))
    for head in range(MINE):
        column = WIDE * (head // 2)
        side = (lane < HEAD) if head % 2 == 0 else (lane >= HEAD)
        delta = jnp.sum(
            jnp.where(side, product[:, column : column + WIDE], 0.0), axis=-1, keepdims=True
        )
        piece = pulled[:, column : column + WIDE]
        if head % 2 == 0:
            piece = pltpu.roll(piece.astype(F32), HEAD, 1).astype(BF)
        piece = jnp.where(
            lane >= HEAD, piece, marked(lane, 0, three_parts(jnp.broadcast_to(-delta, lane.shape)))
        )
        marked_ref[0, :, head] = piece.reshape(count, rows, WIDE)

    @pl.when(step == 0)
    def _():
        down_sum[...] = gdown
        up_sum[...] = gup
        out_sum[...] = gout

    @pl.when(step > 0)
    def _():
        down_sum[...] += gdown
        up_sum[...] += gup
        out_sum[...] += gout

    @pl.when(step == pl.num_programs(0) - 1)
    def _():
        split_rows(own_x, TEAM, up_sum, more_keep, more_send)
        split_rows(own_x, 1, out_sum, more_keep.at[:, TEAM:], more_send.at[:, TEAM:])
        split_rows(own_x, 1, down_sum, down_keep, down_send)


def tokens_kernel(last, own_ref, x0_ref, x1_ref, x2_ref, x3_ref, normed_ref, dnormed_ref, dquery_ref, dkeyval_ref, cotangent_ref, weight_ref, norm_ref, cos_ref, sin_ref, *refs):
    if last:
        start_ref, nstart_ref, dx_ref, dx_far_ref, keep_ref, send_ref, gfront_ref, gnorm_ref, held = refs
    else:
        dx_ref, dx_far_ref, gfront_ref, gnorm_ref, held = refs
    step = pl.program_id(0)
    choose(step, (x0_ref, x1_ref, x2_ref, x3_ref), held)
    hat, scale = standardize(held[...].astype(F32))
    cos_table = cos_ref[0]
    keys_side = lanes(cos_table.shape) < HEAD
    d_keyval = dkeyval_ref[0] + jnp.where(step == 0, cotangent_ref[0].astype(F32), 0.0)
    d_keyval = turn(
        d_keyval, jnp.where(keys_side, cos_table, 1.0), jnp.where(keys_side, sin_ref[0], 0.0), -1.0
    ).astype(BF)
    d_front = jnp.concatenate([d_keyval, dquery_ref[0]], axis=1)
    d_attn = dot_rt(d_front, weight_ref[...])
    d_mlp = dnormed_ref[0, 0].astype(F32)
    d_tokens = norm_back(hat, scale, d_attn * norm_ref[0:1, :] + d_mlp * norm_ref[1:2, :])
    put(step, dx_ref, dx_far_ref, d_tokens.astype(BF))
    sums = [
        jnp.sum(piece, axis=0, keepdims=True) for piece in (d_attn * hat, d_mlp * hat, d_attn, d_mlp)
    ]
    sums = jnp.concatenate(sums + [jnp.zeros_like(sums[0])] * 4, axis=0)
    gfront = dot_lt(normed_ref[0], d_front)

    @pl.when(step == 0)
    def _():
        gfront_ref[...] = start_ref[...] + gfront if last else gfront
        gnorm_ref[...] = nstart_ref[...] + sums if last else sums

    @pl.when(step > 0)
    def _():
        gfront_ref[...] += gfront
        gnorm_ref[...] += sums

    if last:

        @pl.when(step == pl.num_programs(0) - 1)
        def _():
            width = gnorm_ref.shape[1]
            sums = jnp.concatenate(
                [jnp.zeros((HEAD, width), F32), gnorm_ref[...], jnp.zeros((HEAD - 8, width), F32)], axis=0
            )
            gfront_ref[:, 2 * WIDE :] += jnp.transpose(sums)
            split_rows(own_ref[0], TEAM, gfront_ref, keep_ref, send_ref)


def params(limit):
    return pltpu.CompilerParams(vmem_limit_bytes=limit * MB)


def cost(micros):
    return pl.CostEstimate(flops=int(micros * 1.1e9), bytes_accessed=0, transcendentals=0)


def struct(shape, kind):
    return jax.ShapeDtypeStruct(shape, kind)


def whole(*shape):
    return pl.BlockSpec(shape, lambda *_: (0,) * len(shape))


def on_device(nseq, ndp, inputs, w_query, w_keyval, w_out, w_up, w_down, norm_gain, norm_bias, out_cotangent, kv_cotangent):
    count, rows, width = inputs.shape
    top = nseq // 2
    wide = nseq // TEAM
    own = lax.axis_index("seq")
    own_y, own_x, own_c = own // top, (own // 2) % wide, own % 2
    own_z = lax.axis_index("dp")
    share = w_query.shape[0]
    down_share = w_down.shape[0]
    hidden = w_up.shape[1] // TEAM
    heads_wide = MINE * HEAD
    front_wide = 3 * WIDE
    slots = TEAM * wide

    def flip(value, mask, what):
        with jax.named_scope("swap_" + what):
            return lax.ppermute(value, "seq", [(i, i ^ mask) for i in range(nseq)])

    def flip_z(value, mask, what):
        with jax.named_scope("swap_" + what):
            return lax.ppermute(value, "dp", [(i, i ^ mask) for i in range(ndp)])

    def hold(*values):
        return lax.optimization_barrier(values)

    def after(value, *others):
        return hold(value, *others)[0]

    def in_order(bit, mine, other, axis):
        return jnp.where(
            bit == 0, jnp.stack([mine, other], axis), jnp.stack([other, mine], axis)
        )

    def merge(value, axis):
        return value.reshape(value.shape[:axis] + (-1,) + value.shape[axis + 2 :])

    def pick(value, index, axis):
        return lax.dynamic_index_in_dim(value, index, axis, keepdims=False)

    def swap_z(value, mask, axis, what):
        other = flip_z(value, mask, f"{what}_z{mask}")

        def join(other):
            return merge(in_order((own_z // mask) % 2, value, other, axis + 1), axis)

        return other, join

    def gather_z(value, axis, what, step=None):
        masks = [ndp >> (index + 1) for index in range(ndp.bit_length() - 1)]
        for mask in masks if step is None else masks[step]:
            other, join = swap_z(value, mask, axis, what)
            value = join(other)
        return value

    def gather_x(value, what):
        parts = [value[None]]
        mask = 1
        while mask < wide:
            sent = jnp.concatenate(parts) if mask > 1 else parts[0]
            parts.append(flip(sent, 2 * mask, f"{what}_x{mask}"))
            mask *= 2
        return parts

    def flip_x(send, what):
        return flip(send, wide, f"{what}_x{wide // 2}")

    def scatter_x(keep, got, what):
        mask = wide // 2
        while True:
            value = keep.astype(F32) + got.astype(F32)
            mask //= 2
            if mask == 0:
                return value[0]
            bit = (own_x // mask) % 2
            value = value.reshape((2, -1) + value.shape[1:])
            keep = pick(value, bit, 0)
            got = flip(pick(value, 1 - bit, 0).astype(BF), 2 * mask, f"{what}_x{mask}")

    def halve_z(value, axis, what, mask):
        bit = (own_z // mask) % 2
        value = value.reshape(value.shape[:axis] + (-1, 2) + value.shape[axis + 1 :])
        got = flip_z(pick(value, 1 - bit, axis + 1).astype(BF), mask, f"{what}_z{mask}")
        return pick(value, bit, axis + 1), got

    def add_z(pair):
        return pair[0].astype(F32) + pair[1].astype(F32)

    def finish_z(value, axis, what):
        mask = 2
        while mask < ndp:
            value = add_z(halve_z(value, axis, what, mask))
            mask *= 2
        return jnp.squeeze(value, axis)

    def moved(onward):
        pairs = []
        for rank in range(nseq):
            for z in range(ndp):
                member = 2 * (rank // top) + rank % 2
                place = ((rank // 2) % wide) * ndp + z
                pairs.append((member * (nseq * ndp // TEAM) + place, rank * ndp + z))
        return [pair if onward else pair[::-1] for pair in pairs]

    def team(value, what, first, second):
        across = flip(after(value, first), top, what + "_y")
        return [value, across, flip(value, 1, what + "_c"), flip(after(across, second), 1, what + "_yc")]

    norms = jnp.concatenate([norm_gain, norm_bias], axis=1)
    queries_of = w_query.reshape(share, 2, 2, heads_wide).transpose(1, 2, 0, 3)
    same = jnp.concatenate([w_keyval, norms], axis=1)
    ups = w_up.reshape(share, 2, wide, 2, hidden // wide).transpose(1, 3, 0, 2, 4)
    ups = ups.reshape(2, 2, share, hidden)
    pad = jnp.zeros((2, 2, share, 2 * WIDE - heads_wide - norms.shape[1]), BF)
    spread = (2, 2, share)
    pack = jnp.concatenate(
        [
            jnp.broadcast_to(same[:, :WIDE], spread + (WIDE,)),
            queries_of,
            jnp.broadcast_to(same[:, WIDE:], spread + (norms.shape[1],)),
            pad,
            ups,
        ],
        axis=3,
    )
    masks = [ndp >> (index + 1) for index in range(ndp.bit_length() - 1)]
    near_masks, far_masks = masks[-1:], masks[:-1]

    def spread_z(value, axis, what, some):
        for mask in some:
            other, join = swap_z(value, mask, axis, what)
            value = join(other)
        return value

    def begin_z(value, axis, what, some):
        if not some:
            return value, lambda value: value
        return swap_z(spread_z(value, axis, what, some[:-1]), some[-1], axis, what)

    pack_y = flip(pick(pack, 1 - own_y, 0), top, "pack_y")
    with jax.named_scope("swap_out_moved"):
        out_rows = lax.ppermute(w_out, ("seq", "dp"), moved(True))
    sequences = [inputs[b : b + 1] for b in range(count)]
    across = []
    before = pack_y
    for b in range(count):
        across.append(flip(after(sequences[b], before), top, f"tokens{b}_y"))
        before = across[b]
    tokens_c = [flip(sequences[b], 1, f"tokens{b}_c") for b in range(count)]
    pack = in_order(own_y, pick(pack, own_y, 0), pack_y, 0)
    pack_c = flip(pick(pack, 1 - own_c, 1), 1, "pack_c")
    pack, pack_c, out_rows = hold(pack, pack_c, out_rows)
    pack = in_order(own_c, pick(pack, own_c, 1), pack_c, 1)

    front_z = pack[..., :front_wide].reshape(TEAM, 1, share, front_wide)
    front_z = spread_z(front_z, 1, "front", far_masks)
    front_z = spread_z(front_z, 1, "front", near_masks)
    front_z, pack, across[0], down_z = hold(front_z, pack, across[0], w_down[None])
    down_got, join_down = begin_z(down_z, 0, "down", far_masks)
    tokens = [[sequences[0], across[0], tokens_c[0], flip(across[0], 1, "tokens0_yc")]]
    front_parts = gather_x(front_z.reshape(TEAM, ndp * share, front_wide), "front")
    front_parts, tokens[0], pack, down_got = hold(front_parts, tokens[0], pack, down_got)

    lane = jnp.arange(WIDE, dtype=jnp.int32) % HEAD
    frequency = jnp.exp(
        -math.log(10000.0) * ((lane % (ROT // 2)).astype(F32) * (2.0 / ROT))
    )
    ranks = jnp.stack([rank_of(own, r, top) for r in range(TEAM)])
    positions = ranks[:, None] * rows + jnp.arange(rows, dtype=jnp.int32)[None]
    angles = (positions.astype(F32) * 0.25)[..., None] * frequency
    cos_table = jnp.where(lane < ROT, jnp.cos(angles), 1.0)
    sin_table = jnp.where(lane < ROT, jnp.sin(angles), 0.0)
    sin_table = jnp.where(lane < ROT // 2, -sin_table, sin_table)
    own_rank = own.reshape(1).astype(jnp.int32)
    own_place = own_x.reshape(1).astype(jnp.int32)

    def by_r(*last):
        return pl.BlockSpec((1,) + last, lambda r, *_: (r,) + (0,) * len(last))

    one_sequence = [pl.BlockSpec((1, rows, width), lambda r, *_: (0, 0, 0)) for _ in range(TEAM)]

    def near(*last):
        return pl.BlockSpec((1,) + last, lambda r, *_: (jnp.minimum(r, 1),) + (0,) * len(last))

    def far(*last):
        return pl.BlockSpec((1,) + last, lambda r, *_: (jnp.maximum(r - 2, 0),) + (0,) * len(last))

    def call(kernel, scalar, inputs, in_specs, out_specs, out_shape, scratch, limit, micros, name):
        return pl.pallas_call(
            kernel,
            grid_spec=pltpu.PrefetchScalarGridSpec(
                num_scalar_prefetch=1,
                grid=(TEAM,),
                in_specs=in_specs,
                out_specs=out_specs,
                scratch_shapes=scratch,
            ),
            out_shape=out_shape,
            compiler_params=params(limit),
            cost_estimate=cost(micros),
            name=name,
        )(scalar, *inputs)

    table = by_r(rows, WIDE)
    block = pltpu.VMEM((rows, width), BF)

    def prepare(b, weights):
        first = b == 0
        more_out = [struct((width, front_wide), BF), struct((8, width), F32)] if first else []
        return call(
            functools.partial(prepare_kernel, len(weights), first),
            own_place,
            [*tokens[b], *weights, cos_table, sin_table],
            one_sequence + [whole(*part.shape) for part in weights] + [table, table],
            [by_r(rows, width), by_r(rows, width), by_r(rows, 2 * WIDE), by_r(rows, WIDE)]
            + [whole(*out.shape) for out in more_out],
            [
                struct((TEAM, rows, width), BF),
                struct((TEAM, rows, width), BF),
                struct((TEAM, rows, 2 * WIDE), BF),
                struct((TEAM, rows, WIDE), BF),
            ]
            + more_out,
            [block],
            56,
            4,
            "prepare",
        )

    more = jnp.concatenate(
        [pack[..., front_wide:].reshape(TEAM, share, hidden), out_rows.reshape(1, share, width)]
    )
    down_got, join_near = begin_z(join_down(down_got), 0, "down", near_masks)

    *made_first, front, norm_rows = prepare(0, front_parts)
    prepared = [made_first]
    prepared[0], front, across[1:], more = hold(prepared[0], front, across[1:], more)
    for b in range(1, count):
        tokens.append([sequences[b], across[b], tokens_c[b], flip(across[b], 1, f"tokens{b}_yc")])
    more_got, join_more = begin_z(more[:, None], 1, "more", far_masks)
    prepared += [prepare(b, [front, norm_rows]) for b in range(1, count)]
    normed_attn, normed_mlp, queries, keyvals = [list(part) for part in zip(*prepared)]

    def keys_of_all(value, what):
        parts = [value]
        mask = 1
        while mask < wide:
            sent = jnp.concatenate(parts) if mask > 1 else parts[0]
            parts.append(flip(sent, 2 * mask, f"{what}_x{mask}"))
            mask *= 2
        return parts

    everyone = [keys_of_all(keyvals[b], f"keyval{b}") for b in range(count)]
    kv_specs = [whole(*part.shape) for part in everyone[0]]
    kv_scratch = [pltpu.VMEM((slots, rows, WIDE), BF)] * 2

    grads_y = flip(after(out_cotangent, tokens[-1][1]), top, "grads_y")
    grads_c = flip(out_cotangent, 1, "grads_c")
    everyone[0], queries, keyvals, more_got, down_got = hold(
        everyone[0], queries, keyvals, more_got, down_got
    )
    down_z = join_near(down_got)
    more_z = join_more(more_got)
    down_parts = gather_x(down_z.reshape(1, ndp * down_share, width), "down")
    more_got, join_more = begin_z(more_z, 1, "more", near_masks)

    contexts = []
    marked_queries = []
    for b in range(count):
        context, marked_query = call(
            functools.partial(forward_kernel, top, wide),
            own_rank,
            [queries[b], *everyone[b]],
            [by_r(rows, 2 * WIDE)] + kv_specs,
            [by_r(rows, 2 * WIDE), by_r(MINE, rows, WIDE)],
            [struct((TEAM, rows, 2 * WIDE), BF), struct((TEAM, MINE, rows, WIDE), BF)],
            [
                pltpu.VMEM((MINE * rows, WIDE), BF),
                pltpu.VMEM((slots, MINE * rows, rows), F32),
                pltpu.VMEM((MINE * rows, WIDE), F32),
            ]
            + kv_scratch,
            24,
            15,
            "attend",
        )
        contexts.append(context)
        marked_queries.append(marked_query)
        if b == 0:
            contexts[0], everyone[1:], queries, more_got, grads_y = hold(
                contexts[0], everyone[1:], queries, more_got, grads_y
            )
            more_z = join_more(more_got)
            grads = [out_cotangent, grads_y, grads_c, flip(grads_y, 1, "grads_yc")]
            more_parts = gather_x(more_z.reshape(TEAM + 1, ndp * share, width), "more")
    contexts, grads, more_parts, down_parts = hold(contexts, grads, more_parts, down_parts)

    half = max(wide // 2, 1)
    more_half = (half, TEAM + 1, ndp * share, width)
    down_half = (half, 1, ndp * down_share, width)
    both = pl.BlockSpec((count, rows, width), lambda r, *_: (0, 0, 0))
    made, made_far, d_normed, marked_grad, more_keep, more_send, down_keep, down_send = call(
        functools.partial(hidden_kernel, count, len(more_parts)),
        own_place,
        [*grads, *normed_mlp, *contexts, *more_parts, *down_parts],
        [both] * TEAM
        + [by_r(rows, width)] * count
        + [by_r(rows, 2 * WIDE)] * count
        + [whole(*part.shape) for part in more_parts + down_parts],
        [
            near(count, rows, width),
            far(count, rows, width),
            by_r(count, rows, width),
            by_r(count, MINE, rows, WIDE),
            whole(*more_half),
            whole(*more_half),
            whole(*down_half),
            whole(*down_half),
        ],
        [
            struct((2, count, rows, width), BF),
            struct((2, count, rows, width), BF),
            struct((TEAM, count, rows, width), BF),
            struct((TEAM, count, MINE, rows, WIDE), BF),
            struct(more_half, BF),
            struct(more_half, BF),
            struct(down_half, BF),
            struct(down_half, BF),
        ],
        [
            pltpu.VMEM((width, hidden), F32),
            pltpu.VMEM((hidden, width), F32),
            pltpu.VMEM((2 * WIDE, width), F32),
            pltpu.VMEM((count * rows, width), BF),
            pltpu.VMEM((width, hidden), BF),
            pltpu.VMEM((hidden, width), BF),
            pltpu.VMEM((2 * WIDE, width), BF),
        ],
        52,
        27,
        "hidden",
    )

    def sum_c(value, what, *others):
        return value[0].astype(F32) + after(flip(value[1], 1, what + "_c"), *others).astype(F32)

    def sum_y(value, what, *others):
        got = flip(value[1].astype(BF), top, what + "_y")
        return value[0] + after(got, *others).astype(F32)

    d_queries = []
    kept = []
    sent = []
    key_half = (slots // 2, rows, WIDE)
    for b in range(count):
        d_query, keep, send = call(
            functools.partial(backward_kernel, top, wide),
            own_rank,
            [marked_queries[b], marked_grad, cos_table, sin_table, *everyone[b]],
            [
                by_r(MINE, rows, WIDE),
                pl.BlockSpec((1, None, MINE, rows, WIDE), lambda r, *_, b=b: (r, b, 0, 0, 0)),
                table,
                table,
            ]
            + kv_specs,
            [by_r(rows, 2 * WIDE), whole(*key_half), whole(*key_half)],
            [struct((TEAM, rows, 2 * WIDE), BF), struct(key_half, F32), struct(key_half, BF)],
            [pltpu.VMEM((MINE, WIDE, rows), F32)] + kv_scratch + [pltpu.VMEM((slots, rows, WIDE), F32)],
            16,
            20,
            "attend_back",
        )
        d_queries.append(d_query)
        kept.append(keep)
        sent.append(send)
        if b == 0:
            got_c = flip(made_far, 1, "made_c")
            got_x = flip_x(more_send, "gmore")
            (d_queries, kept, sent, marked_grad, made, got_c, more_keep, got_x, down_send) = hold(
                d_queries, kept, sent, marked_grad, made, got_c, more_keep, got_x, down_send
            )
            made = made.astype(F32) + got_c.astype(F32)
            more_grads = scatter_x(more_keep, got_x, "gmore").reshape(TEAM + 1, ndp, share, width)
            got_y = flip(made[1].astype(BF), top, "made_y")
            more_z = halve_z(more_grads, 1, "gmore", 1)
            keys_got = flip_x(sent[0], "gkeyval0")
            got_x = flip_x(down_send, "gdown")
    (d_queries, kept, sent, made, got_y, more_z, keys_got, down_keep, got_x) = hold(
        d_queries, kept, sent, made, got_y, more_z, keys_got, down_keep, got_x
    )
    output = (inputs.astype(F32) + made[0] + got_y.astype(F32)).astype(BF)
    more_grads = add_z(more_z)
    down_grads = scatter_x(down_keep, got_x, "gdown").reshape(ndp, down_share, width)
    keys_gots = [keys_got] + [flip_x(sent[b], f"gkeyval{b}") for b in range(1, count)]

    def keys_back(b):
        keep, got = kept[b], keys_gots[b]
        mask = wide // 2
        while True:
            value = keep + got.astype(F32)
            mask //= 2
            if mask == 0:
                return value
            keep = value[: value.shape[0] // 2]
            got = flip(value[value.shape[0] // 2 :].astype(BF), 2 * mask, f"gkeyval{b}_x{mask}")

    def join_c(value, got):
        mine = pick(value.reshape((2, 2) + value.shape[1:]), own_c, 1)
        got = got.astype(F32)
        return jnp.where(own_c == 0, mine, got), jnp.where(own_c == 0, got, mine)

    def join_y(value, got):
        mine = pick(value, own_y, 0)
        got = got.astype(F32)
        return jnp.where(own_y == 0, mine, got), jnp.where(own_y == 0, got, mine)

    pulled = []
    carried = []
    front_half = (half, TEAM, ndp * share, front_wide)
    for b in range(count):
        last = b == count - 1
        outs = [struct((2, rows, width), BF), struct((2, rows, width), BF)]
        out_specs = [near(rows, width), far(rows, width)]
        sums = [struct((width, front_wide), F32), struct((8, width), F32)]
        if last:
            outs += [struct(front_half, F32), struct(front_half, BF)]
        else:
            outs += sums
        d_tokens, d_tokens_far, *carried = call(
            functools.partial(tokens_kernel, last),
            own_place,
            [
                *tokens[b],
                normed_attn[b],
                d_normed,
                d_queries[b],
                keys_back(b),
                kv_cotangent,
                front,
                norm_rows,
                cos_table,
                sin_table,
                *carried,
            ],
            one_sequence
            + [
                by_r(rows, width),
                pl.BlockSpec((1, 1, rows, width), lambda r, *_, b=b: (r, b, 0, 0)),
                by_r(rows, 2 * WIDE),
                table,
                pl.BlockSpec((1, rows, WIDE), lambda r, *_, b=b: (b, 0, 0)),
                whole(width, front_wide),
                whole(8, width),
                table,
                table,
            ]
            + [whole(*part.shape) for part in carried],
            out_specs + [whole(*out.shape) for out in outs[2:]],
            outs,
            ([pltpu.VMEM(out.shape, F32) for out in sums] if last else []) + [block],
            14,
            7,
            "pull_tokens",
        )
        pulled.append((d_tokens, d_tokens_far))
        if b == 0:
            mask = 2
            while mask < ndp:
                more_z = halve_z(more_grads, 1, "gmore", mask)
                more_grads = add_z(more_z)
                mask *= 2
            down_z = halve_z(down_grads, 0, "gdown", 1)
            (carried, pulled, more_grads, keys_gots, kept, d_queries) = hold(
                carried, pulled, more_grads, keys_gots, kept, d_queries
            )
            more_grads = jnp.squeeze(more_grads, 1)
            got_c = flip(pulled[0][1], 1, "dtokens0_c")
            ups_c = flip(
                pick(more_grads[:TEAM].reshape(2, 2, share, hidden), 1 - own_c, 1).astype(BF), 1, "gup_c"
            )
    front_keep, front_send = carried
    front_keep, front_send, pulled, got_c, ups_c, down_z, more_grads = hold(
        front_keep, front_send, pulled, got_c, ups_c, down_z, more_grads
    )
    down_grads = finish_z(add_z(down_z), 0, "gdown")

    def add_c(pair, got):
        return pair[0].astype(F32) + got.astype(F32)

    front_got = flip_x(front_send, "gfront")
    halves = [add_c(pulled[0], got_c)]
    got_y = flip(halves[0][1].astype(BF), top, "dtokens0_y")
    gots_c = [flip(pulled[b][1], 1, f"dtokens{b}_c") for b in range(1, count)]
    ups = jnp.concatenate(join_c(more_grads[:TEAM], ups_c), axis=-1)
    ups_y = flip(pick(ups, 1 - own_y, 0).astype(BF), top, "gup_y")
    front_keep, front_got, gots_c, more_grads = hold(front_keep, front_got, gots_c, more_grads)
    halves += [add_c(pulled[b], gots_c[b - 1]) for b in range(1, count)]
    with jax.named_scope("swap_gout_moved"):
        grad_out = lax.ppermute(more_grads[TEAM].astype(BF), ("seq", "dp"), moved(False)).astype(F32)
    front_grads = scatter_x(front_keep, front_got, "gfront").reshape(TEAM, ndp, share, front_wide)
    front_z = halve_z(front_grads, 1, "gfront", 1)
    gots_y = [got_y] + [
        flip(halves[b][1].astype(BF), top, f"dtokens{b}_y") for b in range(1, count)
    ]
    front_z, gots_y[0], halves, ups, ups_y = hold(front_z, gots_y[0], halves, ups, ups_y)
    front_grads = finish_z(add_z(front_z), 1, "gfront")

    piece = hidden // wide
    ups = join_y(ups, ups_y)
    grad_up = jnp.concatenate(
        [
            ups[y][:, hidden * c + piece * x : hidden * c + piece * (x + 1)]
            for y in range(2)
            for x in range(wide)
            for c in range(2)
        ],
        axis=-1,
    )
    front_grads, gots_y, grad_up, grad_out, down_grads = hold(
        front_grads, gots_y, grad_up, grad_out, down_grads
    )
    d_rows = [halves[b][0] + gots_y[b].astype(F32) for b in range(count)]
    grad_inputs = out_cotangent.astype(F32) + jnp.stack(d_rows)
    got_c = flip(pick(front_grads.reshape(2, 2, share, front_wide), 1 - own_c, 1).astype(BF), 1, "gfront_c")
    front_grads, got_c, grad_inputs = hold(front_grads, got_c, grad_inputs)

    low, high = join_c(front_grads, got_c)
    query = slice(WIDE, WIDE + heads_wide)
    ends = slice(WIDE + heads_wide, WIDE + heads_wide + 4)
    front_grads = (
        jnp.concatenate(
            [low[..., :WIDE] + high[..., :WIDE], low[..., query], high[..., query], low[..., ends] + high[..., ends]],
            axis=-1,
        )
    )
    got_y = flip(pick(front_grads, 1 - own_y, 0).astype(BF), top, "gfront_y")
    fronts = join_y(front_grads, got_y)
    both_heads = slice(WIDE, WIDE + 2 * heads_wide)
    grad_query = jnp.concatenate([part[:, both_heads] for part in fronts], axis=-1)
    grad_keyval = fronts[0][:, :WIDE] + fronts[1][:, :WIDE]
    norm_grads = (fronts[0] + fronts[1])[:, WIDE + 2 * heads_wide :]
    return (
        output,
        jnp.stack([part[0] for part in keyvals]),
        grad_inputs,
        grad_query,
        grad_keyval,
        grad_out,
        grad_up,
        down_grads,
        norm_grads[:, :2],
        norm_grads[:, 2:],
    )


def solution(mesh):
    rows = P("dp", "seq", None)
    split = P(("seq", "dp"), None)
    return jax.shard_map(
        functools.partial(on_device, mesh.shape["seq"], mesh.shape["dp"]),
        mesh=mesh,
        in_specs=(rows,) + (split,) * 7 + (rows, rows),
        out_specs=(rows,) * 3 + (split,) * 7,
        check_vma=False,
    )
```

```python
import functools
import math

import jax
import jax.numpy as jnp
import numpy as np
from jax import lax
from jax.experimental import pallas as pl
from jax.experimental.pallas import tpu as pltpu
from jax.sharding import PartitionSpec as P

HEADS = 12
HEAD = 64
ROT = 16
TEAM = 4
MINE = HEADS // TEAM
WIDE = 2 * HEAD
EPSILON = 1e-05
BF = jnp.bfloat16
F32 = jnp.float32
SCALE = 1.0 / math.sqrt(HEAD)
MB = 1 << 20


def dot(left, right):
    return lax.dot_general(left, right, (((1,), (0,)), ((), ())), preferred_element_type=F32)


def dot_rt(left, right):
    return lax.dot_general(left, right, (((1,), (1,)), ((), ())), preferred_element_type=F32)


def dot_lt(left, right):
    return lax.dot_general(left, right, (((0,), (0,)), ((), ())), preferred_element_type=F32)


def lanes(shape):
    return lax.broadcasted_iota(jnp.int32, shape, len(shape) - 1)


def angle_tables(rows, count):
    lane = np.arange(WIDE) % HEAD
    frequency = np.exp(-math.log(10000.0) * (lane % (ROT // 2)) * (2.0 / ROT)) * (lane < ROT)
    sign = np.where(lane < ROT // 2, -1.0, 1.0)
    out = []
    for positions in (np.arange(rows), np.arange(count) * rows):
        angles = 0.25 * positions[:, None] * frequency
        out.append(np.stack([np.cos(angles), sign * np.sin(angles)]).astype(np.float32))
    return out


def table_of(place_ref, start_ref, rank):
    cos_row, sin_row = place_ref[0], place_ref[1]
    cos_start, sin_start = start_ref[0, pl.ds(rank, 1)], start_ref[1, pl.ds(rank, 1)]
    return cos_row * cos_start - sin_row * sin_start, sin_row * cos_start + cos_row * sin_start


def keys_only(tables):
    keys_side = lanes(tables[0].shape) < HEAD
    return jnp.where(keys_side, tables[0], 1.0), jnp.where(keys_side, tables[1], 0.0)


def turn(values, tables, sign):
    near = (lanes(values.shape) % HEAD) < ROT // 2
    swapped = jnp.where(
        near, pltpu.roll(values, WIDE - ROT // 2, 1), pltpu.roll(values, ROT // 2, 1)
    )
    return values * tables[0] + (sign * swapped) * tables[1]


def standardize(tokens):
    center = tokens - jnp.mean(tokens, axis=-1, keepdims=True)
    spread = jnp.mean(center * center, axis=-1, keepdims=True)
    scale = lax.rsqrt(spread + EPSILON)
    return center * scale, scale


def norm_back(hat, scale, pulled):
    return scale * (
        pulled
        - jnp.mean(pulled, axis=-1, keepdims=True)
        - hat * jnp.mean(pulled * hat, axis=-1, keepdims=True)
    )


def three_parts(column):
    high = column.astype(BF)
    rest = column - high.astype(F32)
    mid = rest.astype(BF)
    low = (rest - mid.astype(F32)).astype(BF)
    return high, mid, low


def marked(lane, base, parts):
    out = jnp.zeros(lane.shape, BF)
    for index, part in enumerate(parts):
        out = jnp.where(lane == base + index, part, out)
    return out


def fetch(refs, held, arrived):
    step = pl.program_id(0)

    def start(r):
        for index, ref in enumerate(refs):

            @pl.when(r == index)
            def _(ref=ref):
                pltpu.make_async_copy(ref, held.at[r % 2], arrived.at[r % 2]).start()

    @pl.when(step == 0)
    def _():
        start(step)

    @pl.when(step + 1 < len(refs))
    def _():
        start(step + 1)

    pltpu.make_async_copy(refs[0], held.at[step % 2], arrived.at[step % 2]).wait()
    return held[step % 2]


def normalize(hat, norm_ref, which):
    return (hat * norm_ref[which : which + 1, :] + norm_ref[which + 2 : which + 3, :]).astype(BF)


def put(r, near_ref, far_ref, value):
    @pl.when(r < 2)
    def _():
        near_ref[0] = value

    @pl.when(r >= 2)
    def _():
        far_ref[0] = value


def assemble(own_x, refs, groups, held):
    wide = sum(ref.shape[0] for ref in refs)
    relative = 0
    for ref in refs:
        block = ref.shape[2]
        for index in range(ref.shape[0]):
            x = own_x ^ relative
            for group in range(groups):
                place = (group // 2 * wide + x) * 2 + group % 2 if groups > 1 else x
                start = pl.multiple_of(place * block, block)
                held[pl.ds(start, block), :] = ref[index, group]
            relative += 1


def prepare_kernel(parts, first, last, top, wide, own_ref, *refs):
    x_refs, refs = refs[: TEAM * last], refs[TEAM * last :]
    front_refs, refs = refs[:parts], refs[parts:]
    place_ref, start_ref, query_ref, keyval_ref, *refs = refs
    *refs, held, arrived = refs
    own = own_ref[0]
    copies = [pltpu.make_async_copy(ref, held.at[i], arrived.at[i]) for i, ref in enumerate(x_refs)]
    for copy in copies:
        copy.start()
    if first:
        front_ref, norm_ref = refs
        assemble((own // 2) % wide, front_refs, TEAM, front_ref)
        norm_ref[...] = jnp.transpose(front_ref[:, 2 * WIDE :].astype(F32))[HEAD : HEAD + 8]
    else:
        front_ref, norm_ref = front_refs
        (mlp_ref,) = refs

    for copy in copies:
        copy.wait()

    @pl.loop(0, TEAM)
    def _(r):
        hat, _ = standardize(held[r, 0].astype(F32))
        made = dot(normalize(hat, norm_ref, 0), front_ref[...])
        tables = table_of(place_ref, start_ref, rank_of(own, r, top))
        keyval_ref[r] = turn(made[:, :WIDE], keys_only(tables), 1.0).astype(BF)
        for part in range(2):
            piece = made[:, WIDE * (part + 1) : WIDE * (part + 2)]
            query_ref[r, :, WIDE * part : WIDE * (part + 1)] = (turn(piece, tables, 1.0) * SCALE).astype(BF)
        if not first:
            mlp_ref[r, last - 1] = normalize(hat, norm_ref, 1)
            for index in range(1, last):
                hat, _ = standardize(held[index * TEAM + r, 0].astype(F32))
                mlp_ref[r, index - 1] = normalize(hat, norm_ref, 1)


def rank_of(own, block, top):
    return own ^ ((block % 2) * top) ^ (block // 2)


def slot_of(away, top, wide):
    return ((away // 2) % wide) * TEAM + (away // top) % 2 + 2 * (away % 2)


def load_keyval(own, top, wide, refs, keys_ref, values_ref, base):
    slots = {}
    start = 0
    for ref in refs:
        for index in range(ref.shape[0]):
            slots[start + index] = ref, index
        start += ref.shape[0]
    for away in range(start):
        ref, index = slots[(away // 2) % wide * TEAM + (away // top) % 2 + 2 * (away % 2)]
        block = ref[index]
        rows = block.shape[0]
        at = pl.ds(pl.multiple_of((own ^ away) * rows, rows), rows)
        lane = lanes((rows, WIDE))
        keys_ref[at] = jnp.where(lane < HEAD, block, base[1])
        values_ref[at] = jnp.where(lane < HEAD, base[0], block)


def forward_kernel(top, wide, own_ref, query_ref, *refs):
    kv_refs, (context_ref, marked_ref, low_ref, score_ref, peak_ref, keys_ref, values_ref) = refs[:-7], refs[-7:]
    rows = query_ref.shape[2]
    groups = 2 * MINE
    own = own_ref[0]
    step = pl.program_id(0)
    mine = own ^ (step * top)
    base = mine // 2 * 2
    lane = lanes((rows, WIDE))

    @pl.when(step == 0)
    def _():
        one = jnp.ones((rows, WIDE), BF)
        load_keyval(own, top, wide, kv_refs, keys_ref, values_ref, (one, jnp.zeros_like(one)))

    for c in range(2):
        first = query_ref[c, 0, :, :WIDE]
        at = c * MINE * rows
        low_ref[at : at + rows] = first
        low_ref[at + rows : at + 2 * rows] = pltpu.roll(first.astype(F32), HEAD, 1).astype(BF)
        low_ref[at + 2 * rows : at + 3 * rows] = query_ref[c, 0, :, WIDE:]

    def score(index, masked):
        at = pl.ds(pl.multiple_of(index * 2 * rows, 2 * rows), 2 * rows)
        scores = dot_rt(low_ref[...], keys_ref[at])
        if masked:
            key = lax.broadcasted_iota(jnp.int32, (rows, 2 * rows), 1)
            query = lax.broadcasted_iota(jnp.int32, (rows, 2 * rows), 0)
            keeps = [key <= query + ((mine ^ c) - base) * rows for c in range(2)]
            scores = jnp.concatenate(
                [
                    jnp.where(keeps[group // MINE], scores[group * rows : (group + 1) * rows], -1e30)
                    for group in range(groups)
                ],
                axis=0,
            )
        score_ref[index] = scores
        best = functools.reduce(
            jnp.maximum, [scores[:, part : part + WIDE] for part in range(0, 2 * rows, WIDE)]
        )
        peak_ref[...] = best if masked else jnp.maximum(peak_ref[...], best)

    count = base // 2
    score(count, True)

    @pl.loop(0, count)
    def _(index):
        score(index, False)

    peak_ref[...] = jnp.broadcast_to(jnp.max(peak_ref[...], axis=-1, keepdims=True), peak_ref.shape)

    def weigh(index, sums):
        at = pl.ds(pl.multiple_of(index * 2 * rows, 2 * rows), 2 * rows)
        peak = peak_ref[...]
        weights = jnp.exp(score_ref[index] - jnp.concatenate([peak] * (2 * rows // WIDE), axis=1))
        return sums + dot(weights.astype(BF), values_ref[at])

    sums = lax.fori_loop(0, count + 1, weigh, jnp.zeros((groups * rows, WIDE), F32))
    for c in range(2):
        made = []
        for head in range(MINE):
            at = slice((c * MINE + head) * rows, (c * MINE + head + 1) * rows)
            part = sums[at]
            swapped = pltpu.roll(part, HEAD, 1)
            total = jnp.where(lane < HEAD, part, swapped)
            made.append(jnp.where(lane < HEAD, swapped, part) / total)
            logsum = peak_ref[at] + jnp.log(total)
            marked_ref[c, 0, head] = jnp.where(
                lane < HEAD, low_ref[at], marked(lane, HEAD, three_parts(-logsum))
            )
        context_ref[c, 0, :, :WIDE] = jnp.where(lane < HEAD, made[0], made[1]).astype(BF)
        context_ref[c, 0, :, WIDE:] = jnp.where(lane < HEAD, made[2], 0.0).astype(BF)


def backward_kernel(top, wide, own_ref, query_ref, grad_ref, place_ref, start_ref, *refs):
    kv_refs, (dquery_ref, keep_ref, send_ref, sum_ref, keys_ref, values_ref, dkeyval_ref) = refs[:-7], refs[-7:]
    rows = query_ref.shape[3]
    own = own_ref[0]
    step = pl.program_id(0)
    mine = own ^ (step * top)
    base = mine // 2 * 2
    lane = lanes((rows, WIDE))
    wide_lane = lanes((2 * rows, WIDE))

    @pl.when(step == 0)
    def _():
        dkeyval_ref[...] = jnp.zeros_like(dkeyval_ref)
        ones_low = jnp.where(lane < 3, 1.0, 0.0).astype(BF)
        ones_high = jnp.where((lane >= HEAD) & (lane < HEAD + 3), 1.0, 0.0).astype(BF)
        load_keyval(own, top, wide, kv_refs, keys_ref, values_ref, (ones_low, ones_high))

    def visit(index, masked):
        at = pl.ds(pl.multiple_of(index * 2 * rows, 2 * rows), 2 * rows)
        keys = keys_ref[at]
        values = values_ref[at]
        d_keys = jnp.zeros((2 * rows, WIDE), F32)
        d_values = jnp.zeros((2 * rows, WIDE), F32)
        for c in range(2):
            for head in range(MINE):
                query = query_ref[c, 0, head]
                grad = grad_ref[c, 0, head]
                probs = jnp.exp(dot_rt(keys, query))
                if masked:
                    key = lax.broadcasted_iota(jnp.int32, probs.shape, 0)
                    row = lax.broadcasted_iota(jnp.int32, probs.shape, 1)
                    probs = jnp.where(key <= row + ((mine ^ c) - base) * rows, probs, 0.0)
                d_scores = (probs * dot_rt(values, grad)).astype(BF)
                d_values += dot(probs.astype(BF), grad)
                d_keys += dot(d_scores, query)
                d_query = dot_lt(keys, d_scores)
                sum_ref[c, head] = d_query if masked else sum_ref[c, head] + d_query
        dkeyval_ref[at] += jnp.where(wide_lane < HEAD, d_keys, d_values)

    visit(base // 2, True)

    @pl.loop(0, base // 2)
    def _(index):
        visit(index, False)

    for c in range(2):
        turned = [jnp.transpose(sum_ref[c, head]) * SCALE for head in range(MINE)]
        both = jnp.where(lane < HEAD, turned[0], pltpu.roll(turned[1], HEAD, 1))
        last = jnp.where(lane < HEAD, turned[2], 0.0)
        tables = table_of(place_ref, start_ref, mine ^ c)
        dquery_ref[c, 0, :, :WIDE] = turn(both, tables, -1.0).astype(BF)
        dquery_ref[c, 0, :, WIDE:] = turn(last, tables, -1.0).astype(BF)

    @pl.when(step == pl.num_programs(0) - 1)
    def _():
        half = send_ref.shape[0]
        for rank in range(2 * half):
            slot = slot_of(rank ^ own, top, wide)
            block = dkeyval_ref[rank * rows : (rank + 1) * rows]

            @pl.when(slot < half)
            def _():
                keep_ref[jnp.minimum(slot, half - 1)] = block

            @pl.when(slot >= half)
            def _():
                send_ref[jnp.maximum(slot - half, 0)] = block.astype(BF)


def split_rows(own_x, groups, total, keep_ref, send_ref):
    wide = 2 * keep_ref.shape[0]
    block = keep_ref.shape[2]
    for side, ref in enumerate((keep_ref, send_ref)):
        half = own_x // (wide // 2) ^ side
        for index in range(wide // 2):
            x = half * (wide // 2) + index
            for group in range(groups):
                place = (group // 2 * wide + x) * 2 + group % 2 if groups > 1 else x
                start = pl.multiple_of(place * block, block)
                ref[index, group] = total[pl.ds(start, block), :].astype(ref.dtype)


def split_z(own_z, total, keep_ref, send_ref):
    wide, half, block = keep_ref.shape[:3]
    for side, ref in enumerate((keep_ref, send_ref)):
        for x in range(wide):
            for index in range(half):
                place = (x * half + index) * 2 + (own_z % 2 ^ side)
                start = pl.multiple_of(place * block, block)
                ref[x, index] = total[pl.ds(start, block), :].astype(ref.dtype)


def hidden_kernel(count, parts, down_parts, own_ref, *refs):
    grad_refs, refs = refs[:4], refs[4:]
    normed_ref, *refs = refs
    context_refs, refs = refs[:count], refs[count:]
    more_refs, refs = refs[:parts], refs[parts:]
    down_refs, refs = refs[:down_parts], refs[down_parts:]
    (made_ref, made_far_ref, dnormed_ref, marked_ref, more_keep, more_send, down_keep, down_send, *refs) = refs
    (up_sum, low_sum, held, arrived, up_ref, low_ref) = refs
    step = pl.program_id(0)
    own_x = own_ref[0]
    rows = context_refs[0].shape[1]
    units = up_ref.shape[1]

    @pl.when(step == 0)
    def _():
        low_ref[units:] = jnp.zeros_like(low_ref[units:])
        assemble(own_x, more_refs, TEAM, up_ref)
        assemble(own_x, [ref.at[:, TEAM:] for ref in more_refs], 1, low_ref.at[units:])
        assemble(own_x, down_refs, 1, low_ref)

    normed = normed_ref[0].reshape(count * rows, normed_ref.shape[-1])
    context = jnp.concatenate([ref[0] for ref in context_refs], axis=0)
    grad = fetch(grad_refs, held, arrived).reshape(normed.shape)
    raw = dot(normed, up_ref[...])
    bell = 0.5 + 0.5 * lax.erf(raw * math.sqrt(0.5))
    slope = bell + raw * (jnp.exp(raw * raw * -0.5) * (1.0 / math.sqrt(2.0 * math.pi)))
    low = jnp.concatenate([(raw * bell).astype(BF), context], axis=1)
    pulled = dot_rt(grad, low_ref[...])
    d_raw = (pulled[:, :units] * slope).astype(BF)
    made = dot(low, low_ref[...]).astype(BF)
    put(step, made_ref, made_far_ref, made.reshape(made_ref.shape[1:]))
    dnormed_ref[0] = dot_rt(d_raw, up_ref[...]).astype(BF).reshape(dnormed_ref.shape[1:])
    glow = dot_lt(low, grad)
    gup = dot_lt(normed, d_raw)

    pulled = pulled[:, units:].astype(BF)
    product = pulled.astype(F32) * context.astype(F32)
    lane = lanes((grad.shape[0], WIDE))
    for head in range(MINE):
        column = WIDE * (head // 2)
        side = (lane < HEAD) if head % 2 == 0 else (lane >= HEAD)
        delta = jnp.sum(
            jnp.where(side, product[:, column : column + WIDE], 0.0), axis=-1, keepdims=True
        )
        piece = pulled[:, column : column + WIDE]
        if head % 2 == 0:
            piece = pltpu.roll(piece.astype(F32), HEAD, 1).astype(BF)
        piece = jnp.where(
            lane >= HEAD, piece, marked(lane, 0, three_parts(jnp.broadcast_to(-delta, lane.shape)))
        )
        marked_ref[0, :, head] = piece.reshape(count, rows, WIDE)

    @pl.when(step == 0)
    def _():
        low_sum[...] = glow
        up_sum[...] = gup

    @pl.when(step > 0)
    def _():
        low_sum[...] += glow
        up_sum[...] += gup

    @pl.when(step == pl.num_programs(0) - 1)
    def _():
        split_rows(own_x, TEAM, up_sum, more_keep, more_send)
        split_rows(own_x, 1, low_sum.at[units:], more_keep.at[:, TEAM:], more_send.at[:, TEAM:])
        split_z(own_ref[1], low_sum, down_keep, down_send)


def tokens_kernel(last, top, wide, own_ref, x0_ref, x1_ref, x2_ref, x3_ref, dnormed_ref, dquery_ref, dkeyval_ref, cotangent_ref, weight_ref, norm_ref, place_ref, start_ref, *refs):
    if last:
        before_ref, nbefore_ref, dx_ref, dx_far_ref, keep_ref, send_ref, gfront_ref, gnorm_ref, held, arrived = refs
    else:
        dx_ref, dx_far_ref, gfront_ref, gnorm_ref, held, arrived = refs
    step = pl.program_id(0)
    tokens = fetch((x0_ref, x1_ref, x2_ref, x3_ref), held, arrived)
    hat, scale = standardize(tokens[0].astype(F32))
    tables = table_of(place_ref, start_ref, rank_of(own_ref[0], step, top))
    d_keyval = dkeyval_ref[0] + jnp.where(step == 0, cotangent_ref[0].astype(F32), 0.0)
    d_keyval = turn(d_keyval, keys_only(tables), -1.0).astype(BF)
    d_front = jnp.concatenate([d_keyval, dquery_ref[0]], axis=1)
    d_attn = dot_rt(d_front, weight_ref[...])
    d_mlp = dnormed_ref[0, 0].astype(F32)
    d_tokens = norm_back(hat, scale, d_attn * norm_ref[0:1, :] + d_mlp * norm_ref[1:2, :])
    put(step, dx_ref, dx_far_ref, d_tokens.astype(BF))
    sums = [
        jnp.sum(piece, axis=0, keepdims=True) for piece in (d_attn * hat, d_mlp * hat, d_attn, d_mlp)
    ]
    sums = jnp.concatenate(sums + [jnp.zeros_like(sums[0])] * 4, axis=0)
    gfront = dot_lt(normalize(hat, norm_ref, 0), d_front)

    @pl.when(step == 0)
    def _():
        gfront_ref[...] = before_ref[...] + gfront if last else gfront
        gnorm_ref[...] = nbefore_ref[...] + sums if last else sums

    @pl.when(step > 0)
    def _():
        gfront_ref[...] += gfront
        gnorm_ref[...] += sums

    if last:

        @pl.when(step == pl.num_programs(0) - 1)
        def _():
            width = gnorm_ref.shape[1]
            sums = jnp.concatenate(
                [jnp.zeros((HEAD, width), F32), gnorm_ref[...], jnp.zeros((HEAD - 8, width), F32)], axis=0
            )
            gfront_ref[:, 2 * WIDE :] += jnp.transpose(sums)
            split_rows((own_ref[0] // 2) % wide, TEAM, gfront_ref, keep_ref, send_ref)


def finish_kernel(own_ref, mine_ref, c_ref, y_ref, both_ref, query_ref, keyval_ref, gain_ref, bias_ref, turned_ref):
    parts = [mine_ref[...]] + [ref[...].astype(F32) for ref in (c_ref, y_ref, both_ref)]
    total = parts[0] + parts[1] + parts[2] + parts[3]
    keyval_ref[...] = total[:, :WIDE]
    turned_ref[...] = jnp.zeros_like(turned_ref)
    turned_ref[: total.shape[0]] = total[:, 2 * WIDE :]
    ends = jnp.transpose(turned_ref[...])[HEAD : HEAD + 4, : total.shape[0]]
    gain_ref[...] = ends[:2]
    bias_ref[...] = ends[2:]
    for index in range(2):
        bit = own_ref[index] == 0
        parts = [jnp.where(bit, parts[place], parts[place ^ (1 << index)]) for place in range(TEAM)]
    query_ref[...] = jnp.concatenate([part[:, WIDE : WIDE + MINE * HEAD] for part in parts], axis=1)


def params(limit):
    return pltpu.CompilerParams(vmem_limit_bytes=limit * MB)


def cost(micros):
    return pl.CostEstimate(flops=int(micros * 1.1e9), bytes_accessed=0, transcendentals=0)


def struct(shape, kind):
    return jax.ShapeDtypeStruct(shape, kind)


def whole(*shape):
    return pl.BlockSpec(shape, lambda *_: (0,) * len(shape))


def on_device(nseq, ndp, inputs, w_query, w_keyval, w_out, w_up, w_down, norm_gain, norm_bias, out_cotangent, kv_cotangent):
    count, rows, width = inputs.shape
    top = nseq // 2
    wide = nseq // TEAM
    own = lax.axis_index("seq")
    own_y, own_x, own_c = own // top, (own // 2) % wide, own % 2
    own_z = lax.axis_index("dp")
    share = w_query.shape[0]
    down_share = w_down.shape[0]
    hidden = w_up.shape[1] // TEAM
    heads_wide = MINE * HEAD
    front_wide = 3 * WIDE
    slots = TEAM * wide

    def flip(value, mask, what):
        with jax.named_scope("swap_" + what):
            return lax.ppermute(value, "seq", [(i, i ^ mask) for i in range(nseq)])

    def flip_z(value, mask, what):
        with jax.named_scope("swap_" + what):
            return lax.ppermute(value, "dp", [(i, i ^ mask) for i in range(ndp)])

    def hold(*values):
        return lax.optimization_barrier(values)

    def after(value, *others):
        return hold(value, *others)[0]

    def in_order(bit, mine, other, axis):
        return jnp.where(
            bit == 0, jnp.stack([mine, other], axis), jnp.stack([other, mine], axis)
        )

    def merge(value, axis):
        return value.reshape(value.shape[:axis] + (-1,) + value.shape[axis + 2 :])

    def pick(value, index, axis):
        return lax.dynamic_index_in_dim(value, index, axis, keepdims=False)

    def swap_z(value, mask, axis, what):
        other = flip_z(value, mask, f"{what}_z{mask}")

        def join(other):
            return merge(in_order((own_z // mask) % 2, value, other, axis + 1), axis)

        return other, join

    def gather_z(value, axis, what, step=None):
        masks = [ndp >> (index + 1) for index in range(ndp.bit_length() - 1)]
        for mask in masks if step is None else masks[step]:
            other, join = swap_z(value, mask, axis, what)
            value = join(other)
        return value

    def by_place(relative, bits):
        for index, bit in enumerate(bits):
            relative = [
                jnp.where(bit == 0, relative[place], relative[place ^ (1 << index)])
                for place in range(len(relative))
            ]
        return relative

    z_bits = [(own_z >> index) % 2 for index in range(ndp.bit_length() - 1)]

    def gather_x(value, what):
        parts = [value[None]]
        mask = 1
        while mask < wide:
            sent = jnp.concatenate(parts) if mask > 1 else parts[0]
            parts.append(flip(sent, 2 * mask, f"{what}_x{mask}"))
            mask *= 2
        return parts

    def flip_x(send, what):
        return flip(send, wide, f"{what}_x{wide // 2}")

    def scatter_x(keep, got, what):
        mask = wide // 2
        while True:
            value = keep.astype(F32) + got.astype(F32)
            mask //= 2
            if mask == 0:
                return value[0]
            bit = (own_x // mask) % 2
            value = value.reshape((2, -1) + value.shape[1:])
            keep = pick(value, bit, 0)
            got = flip(pick(value, 1 - bit, 0).astype(BF), 2 * mask, f"{what}_x{mask}")

    def halve_z(value, axis, what, mask):
        bit = (own_z // mask) % 2
        value = value.reshape(value.shape[:axis] + (-1, 2) + value.shape[axis + 1 :])
        got = flip_z(pick(value, 1 - bit, axis + 1).astype(BF), mask, f"{what}_z{mask}")
        return pick(value, bit, axis + 1), got

    def add_z(pair):
        return pair[0].astype(F32) + pair[1].astype(F32)

    def finish_z(value, axis, what):
        mask = 2
        while mask < ndp:
            value = add_z(halve_z(value, axis, what, mask))
            mask *= 2
        return jnp.squeeze(value, axis)

    def moved(onward):
        pairs = []
        for rank in range(nseq):
            for z in range(ndp):
                member = 2 * (rank // top) + rank % 2
                place = ((rank // 2) % wide) * ndp + z
                pairs.append((member * (nseq * ndp // TEAM) + place, rank * ndp + z))
        return [pair if onward else pair[::-1] for pair in pairs]

    def team(value, what, first, second):
        across = flip(after(value, first), top, what + "_y")
        return [value, across, flip(value, 1, what + "_c"), flip(after(across, second), 1, what + "_yc")]

    norms = jnp.concatenate([norm_gain, norm_bias], axis=1)
    queries_of = w_query.reshape(share, 2, 2, heads_wide).transpose(1, 2, 0, 3)
    same = jnp.concatenate([w_keyval, norms], axis=1)
    ups = w_up.reshape(share, 2, wide, 2, hidden // wide).transpose(1, 3, 0, 2, 4)
    ups = ups.reshape(2, 2, share, hidden)
    pad = jnp.zeros((2, 2, share, 2 * WIDE - heads_wide - norms.shape[1]), BF)
    spread = (2, 2, share)
    pack = jnp.concatenate(
        [
            jnp.broadcast_to(same[:, :WIDE], spread + (WIDE,)),
            queries_of,
            jnp.broadcast_to(same[:, WIDE:], spread + (norms.shape[1],)),
            pad,
            ups,
        ],
        axis=3,
    )
    masks = [ndp >> (index + 1) for index in range(ndp.bit_length() - 1)]
    near_masks, far_masks = masks[-1:], masks[:-1]

    def spread_z(value, axis, what, some):
        for mask in some:
            other, join = swap_z(value, mask, axis, what)
            value = join(other)
        return value

    def begin_z(value, axis, what, some):
        if not some:
            return value, lambda value: value
        return swap_z(spread_z(value, axis, what, some[:-1]), some[-1], axis, what)

    sequences = [inputs[b : b + 1] for b in range(count)]
    got = [
        flip(pick(pick(pack, own_y ^ (d // 2), 0), own_c ^ (d % 2), 0), top * (d // 2) + d % 2, f"pack_{d}")
        for d in range(1, TEAM)
    ]
    pack, got, sequences, w_out = hold(pack, got, sequences, w_out)
    across = [flip(sequences[0], top, "tokens0_y")]
    mine = pick(pick(pack, own_y, 0), own_c, 0)
    pack = jnp.stack(by_place([mine] + got, [own_c, own_y])).reshape(2, 2, share, -1)
    with jax.named_scope("swap_out_moved"):
        out_rows = lax.ppermute(w_out, ("seq", "dp"), moved(True))
    tokens_c = [flip(sequences[b], 1, f"tokens{b}_c") for b in range(count)]

    front_z = pack[..., :front_wide].reshape(TEAM, share, front_wide)
    got = [flip_z(front_z, mask, f"front_z{mask}") for mask in range(1, ndp)]
    front_z = jnp.stack(by_place([front_z] + got, z_bits), axis=1)
    down_x = jnp.concatenate(gather_x(w_down[None], "down"))
    front_z, pack, out_rows, across[0] = hold(front_z, pack, out_rows, across[0])
    for b in range(1, count):
        across.append(flip(after(sequences[b], across[b - 1]), top, f"tokens{b}_y"))
    tokens = [[sequences[0], across[0], tokens_c[0], flip(across[0], 1, "tokens0_yc")]]
    front_parts = gather_x(front_z.reshape(TEAM, ndp * share, front_wide), "front")
    more = jnp.concatenate(
        [pack[..., front_wide:].reshape(TEAM, share, hidden), out_rows.reshape(1, share, width)]
    )
    more_got, join_more = begin_z(more[:, None], 1, "more", far_masks)
    front_parts, tokens[0], down_x = hold(front_parts, tokens[0], down_x)
    own_rank = own.reshape(1).astype(jnp.int32)
    own_place = jnp.stack([own_x, own_z]).astype(jnp.int32)
    tables = [jnp.asarray(part) for part in angle_tables(rows, nseq)]

    def by_r(*last):
        return pl.BlockSpec((1,) + last, lambda r, *_: (r,) + (0,) * len(last))

    members = [pl.BlockSpec(memory_space=pl.ANY)] * TEAM

    def near(*last):
        return pl.BlockSpec((1,) + last, lambda r, *_: (jnp.minimum(r, 1),) + (0,) * len(last))

    def far(*last):
        return pl.BlockSpec((1,) + last, lambda r, *_: (jnp.maximum(r - 2, 0),) + (0,) * len(last))

    def call(kernel, scalar, inputs, in_specs, out_specs, out_shape, scratch, limit, micros, name, steps=TEAM):
        return pl.pallas_call(
            kernel,
            grid_spec=pltpu.PrefetchScalarGridSpec(
                num_scalar_prefetch=1,
                grid=(steps,),
                in_specs=in_specs,
                out_specs=out_specs,
                scratch_shapes=scratch,
            ),
            out_shape=out_shape,
            compiler_params=params(limit),
            cost_estimate=cost(micros),
            name=name,
        )(scalar, *inputs)

    table = by_r(rows, WIDE)
    block = [pltpu.VMEM((2, 1, rows, width), BF), pltpu.SemaphoreType.DMA((2,))]

    def prepare(b, weights):
        first = b == 0
        many = 1 if b < count - 1 else count
        held = tokens[b] + sum(tokens[: many - 1], [])
        outs = [struct((TEAM, rows, 2 * WIDE), BF), struct((TEAM, rows, WIDE), BF)]
        if first:
            outs += [struct((width, front_wide), BF), struct((8, width), F32)]
        else:
            outs += [struct((TEAM, many, rows, width), BF)]
        return call(
            functools.partial(prepare_kernel, len(weights), first, many, top, wide),
            own_rank,
            [*held, *weights, *tables],
            members * many + [whole(*part.shape) for part in [*weights, *tables]],
            [whole(*out.shape) for out in outs],
            outs,
            [pltpu.VMEM((many * TEAM, 1, rows, width), BF), pltpu.SemaphoreType.DMA((many * TEAM,))],
            16 if first else 24,
            0.5,
            "prepare",
            1,
        )

    *made_first, front, norm_rows = prepare(0, front_parts)
    prepared = [made_first]
    prepared[0], front, across[1:], more_got = hold(prepared[0], front, across[1:], more_got)
    for b in range(1, count):
        tokens.append([sequences[b], across[b], tokens_c[b], flip(across[b], 1, f"tokens{b}_yc")])
    more_got, join_more = begin_z(join_more(more_got), 1, "more", near_masks)
    prepared += [prepare(b, [front, norm_rows]) for b in range(1, count)]
    normed_mlp = prepared[-1][-1]
    queries, keyvals = [[part[index] for part in prepared] for index in range(2)]

    def keys_of_all(value, what):
        parts = [value]
        mask = 1
        while mask < wide:
            sent = jnp.concatenate(parts) if mask > 1 else parts[0]
            parts.append(flip(sent, 2 * mask, f"{what}_x{mask}"))
            mask *= 2
        return parts

    everyone = [keys_of_all(keyvals[b], f"keyval{b}") for b in range(count)]
    kv_specs = [whole(*part.shape) for part in everyone[0]]
    kv_scratch = [pltpu.VMEM((slots * rows, WIDE), BF)] * 2

    def by_pair(*last):
        return pl.BlockSpec((2, 1) + last, lambda y, *_: (0, y) + (0,) * len(last))

    def paired(value):
        return value.reshape((2, 2) + value.shape[1:])

    grads_y = flip(after(out_cotangent, tokens[-1][1]), top, "grads_y")
    grads_c = flip(out_cotangent, 1, "grads_c")
    everyone[0], queries, keyvals, more_got = hold(everyone[0], queries, keyvals, more_got)
    more_parts = gather_x(join_more(more_got).reshape(TEAM + 1, ndp * share, width), "more")
    down_got, join_down = begin_z(after(down_x, more_parts[0])[:, None], 1, "down", far_masks)
    contexts = []
    marked_queries = []
    for b in range(count):
        context, marked_query = call(
            functools.partial(forward_kernel, top, wide),
            own_rank,
            [paired(queries[b]), *everyone[b]],
            [by_pair(rows, 2 * WIDE)] + kv_specs,
            [by_pair(rows, 2 * WIDE), by_pair(MINE, rows, WIDE)],
            [struct((2, 2, rows, 2 * WIDE), BF), struct((2, 2, MINE, rows, WIDE), BF)],
            [
                pltpu.VMEM((2 * MINE * rows, WIDE), BF),
                pltpu.VMEM((slots // 2, 2 * MINE * rows, 2 * rows), F32),
                pltpu.VMEM((2 * MINE * rows, WIDE), F32),
            ]
            + kv_scratch,
            32,
            15,
            "attend",
            2,
        )
        context = context.reshape((TEAM,) + context.shape[2:])
        contexts.append(context)
        marked_queries.append(marked_query)
        if b == 0:
            contexts[0], everyone[1:], queries, grads_y, down_got = hold(
                contexts[0], everyone[1:], queries, grads_y, down_got
            )
            down_got, join_down = begin_z(join_down(down_got), 1, "down", near_masks)
            grads = [out_cotangent, grads_y, grads_c, flip(grads_y, 1, "grads_yc")]
    contexts, grads, more_parts, down_got = hold(contexts, grads, more_parts, down_got)
    down_parts = [join_down(down_got).reshape(wide, 1, ndp * down_share, width)]

    half = max(wide // 2, 1)
    more_half = (half, TEAM + 1, ndp * share, width)
    down_half = (wide, ndp // 2, down_share, width)
    made, made_far, d_normed, marked_grad, more_keep, more_send, down_keep, down_send = call(
        functools.partial(hidden_kernel, count, len(more_parts), len(down_parts)),
        own_place,
        [*grads, normed_mlp, *contexts, *more_parts, *down_parts],
        members
        + [by_r(count, rows, width)]
        + [by_r(rows, 2 * WIDE)] * count
        + [whole(*part.shape) for part in more_parts + down_parts],
        [
            near(count, rows, width),
            far(count, rows, width),
            by_r(count, rows, width),
            by_r(count, MINE, rows, WIDE),
            whole(*more_half),
            whole(*more_half),
            whole(*down_half),
            whole(*down_half),
        ],
        [
            struct((2, count, rows, width), BF),
            struct((2, count, rows, width), BF),
            struct((TEAM, count, rows, width), BF),
            struct((TEAM, count, MINE, rows, WIDE), BF),
            struct(more_half, BF),
            struct(more_half, BF),
            struct(down_half, BF),
            struct(down_half, BF),
        ],
        [
            pltpu.VMEM((width, hidden), F32),
            pltpu.VMEM((hidden + 2 * WIDE, width), F32),
            pltpu.VMEM((2, count, rows, width), BF),
            pltpu.SemaphoreType.DMA((2,)),
            pltpu.VMEM((width, hidden), BF),
            pltpu.VMEM((hidden + 2 * WIDE, width), BF),
        ],
        52,
        27,
        "hidden",
    )

    def sum_c(value, what, *others):
        return value[0].astype(F32) + after(flip(value[1], 1, what + "_c"), *others).astype(F32)

    def sum_y(value, what, *others):
        got = flip(value[1].astype(BF), top, what + "_y")
        return value[0] + after(got, *others).astype(F32)

    d_queries = []
    kept = []
    sent = []
    key_half = (slots // 2, rows, WIDE)
    for b in range(count):
        d_query, keep, send = call(
            functools.partial(backward_kernel, top, wide),
            own_rank,
            [marked_queries[b], paired(marked_grad), *tables, *everyone[b]],
            [
                by_pair(MINE, rows, WIDE),
                pl.BlockSpec((2, 1, None, MINE, rows, WIDE), lambda y, *_, b=b: (0, y, b, 0, 0, 0)),
            ]
            + [whole(*part.shape) for part in tables]
            + kv_specs,
            [by_pair(rows, 2 * WIDE), whole(*key_half), whole(*key_half)],
            [struct((2, 2, rows, 2 * WIDE), BF), struct(key_half, F32), struct(key_half, BF)],
            [pltpu.VMEM((2, MINE, WIDE, rows), F32)]
            + kv_scratch
            + [pltpu.VMEM((slots * rows, WIDE), F32)],
            16,
            20,
            "attend_back",
            2,
        )
        d_query = d_query.reshape((TEAM,) + d_query.shape[2:])
        d_queries.append(d_query)
        kept.append(keep)
        sent.append(send)
        if b == 0:
            got_c = flip(made_far, 1, "made_c")
            got_x = flip_x(more_send, "gmore")
            down_got = flip_z(down_send, 1, "gdown_z1")
            (d_queries, kept, sent, marked_grad, made, got_c, more_keep, got_x, down_keep, down_got) = hold(
                d_queries, kept, sent, marked_grad, made, got_c, more_keep, got_x, down_keep, down_got
            )
            made = made.astype(F32) + got_c.astype(F32)
            more_grads = scatter_x(more_keep, got_x, "gmore").reshape(TEAM + 1, ndp, share, width)
            got_y = flip(made[1].astype(BF), top, "made_y")
            more_z = halve_z(more_grads, 1, "gmore", 1)
            keys_got = flip_x(sent[0], "gkeyval0")
            down_grads = down_keep.astype(F32) + down_got.astype(F32)
            mask = 2
            while mask < ndp:
                down_z = halve_z(down_grads, 1, "gdown", mask)
                down_grads = add_z(down_z) if 2 * mask < ndp else down_grads
                mask *= 2
    (d_queries, kept, sent, made, got_y, more_z, keys_got) = hold(
        d_queries, kept, sent, made, got_y, more_z, keys_got
    )
    output = (inputs.astype(F32) + made[0] + got_y.astype(F32)).astype(BF)
    more_grads = add_z(more_z)
    keys_gots = [keys_got] + [flip_x(sent[b], f"gkeyval{b}") for b in range(1, count)]

    def keys_back(b):
        keep, got = kept[b], keys_gots[b]
        mask = wide // 2
        while True:
            value = keep + got.astype(F32)
            mask //= 2
            if mask == 0:
                return value
            keep = value[: value.shape[0] // 2]
            got = flip(value[value.shape[0] // 2 :].astype(BF), 2 * mask, f"gkeyval{b}_x{mask}")

    def join_c(value, got):
        mine = pick(value.reshape((2, 2) + value.shape[1:]), own_c, 1)
        got = got.astype(F32)
        return jnp.where(own_c == 0, mine, got), jnp.where(own_c == 0, got, mine)

    def join_y(value, got):
        mine = pick(value, own_y, 0)
        got = got.astype(F32)
        return jnp.where(own_y == 0, mine, got), jnp.where(own_y == 0, got, mine)

    pulled = []
    carried = []
    front_half = (half, TEAM, ndp * share, front_wide)
    for b in range(count):
        last = b == count - 1
        outs = [struct((2, rows, width), BF), struct((2, rows, width), BF)]
        out_specs = [near(rows, width), far(rows, width)]
        sums = [struct((width, front_wide), F32), struct((8, width), F32)]
        if last:
            outs += [struct(front_half, F32), struct(front_half, BF)]
        else:
            outs += sums
        d_tokens, d_tokens_far, *carried = call(
            functools.partial(tokens_kernel, last, top, wide),
            own_rank,
            [
                *tokens[b],
                d_normed,
                d_queries[b],
                keys_back(b),
                kv_cotangent,
                front,
                norm_rows,
                *tables,
                *carried,
            ],
            members
            + [
                pl.BlockSpec((1, 1, rows, width), lambda r, *_, b=b: (r, b, 0, 0)),
                by_r(rows, 2 * WIDE),
                table,
                pl.BlockSpec((1, rows, WIDE), lambda r, *_, b=b: (b, 0, 0)),
                whole(width, front_wide),
                whole(8, width),
            ]
            + [whole(*part.shape) for part in tables]
            + [whole(*part.shape) for part in carried],
            out_specs + [whole(*out.shape) for out in outs[2:]],
            outs,
            ([pltpu.VMEM(out.shape, F32) for out in sums] if last else []) + block,
            14,
            7,
            "pull_tokens",
        )
        pulled.append((d_tokens, d_tokens_far))
        if b == 0:
            mask = 2
            while mask < ndp:
                more_z = halve_z(more_grads, 1, "gmore", mask)
                more_grads = add_z(more_z) if 2 * mask < ndp else more_grads
                mask *= 2
            (carried, pulled, down_z, keys_gots, kept, d_queries) = hold(
                carried, pulled, down_z, keys_gots, kept, d_queries
            )
            got_c = flip(pulled[0][1], 1, "dtokens0_c")
            down_grads = jnp.squeeze(add_z(down_z), 1)
            x_half = down_grads.reshape((2, -1) + down_grads.shape[1:])
            x_bit = own_x // (wide // 2)
            down_keep = pick(x_half, x_bit, 0)
            down_got = flip_x(pick(x_half, 1 - x_bit, 0).astype(BF), "gdown")
    front_keep, front_send = carried
    front_keep, front_send, pulled, got_c, more_z = hold(front_keep, front_send, pulled, got_c, more_z)
    more_grads = jnp.squeeze(add_z(more_z), 1)
    down_grads = scatter_x(down_keep, down_got, "gdown")

    def add_c(pair, got):
        return pair[0].astype(F32) + got.astype(F32)

    front_got = flip_x(front_send, "gfront")
    halves = [add_c(pulled[0], got_c)]
    got_y = flip(halves[0][1].astype(BF), top, "dtokens0_y")
    gots_c = [flip(pulled[b][1], 1, f"dtokens{b}_c") for b in range(1, count)]
    ups_c = flip(
        pick(more_grads[:TEAM].reshape(2, 2, share, hidden), 1 - own_c, 1).astype(BF), 1, "gup_c"
    )
    front_keep, front_got, gots_c, more_grads, ups_c = hold(
        front_keep, front_got, gots_c, more_grads, ups_c
    )
    ups = jnp.concatenate(join_c(more_grads[:TEAM], ups_c), axis=-1)
    ups_y = flip(pick(ups, 1 - own_y, 0).astype(BF), top, "gup_y")
    halves += [add_c(pulled[b], gots_c[b - 1]) for b in range(1, count)]
    with jax.named_scope("swap_gout_moved"):
        grad_out = lax.ppermute(more_grads[TEAM].astype(BF), ("seq", "dp"), moved(False)).astype(F32)
    front_grads = scatter_x(front_keep, front_got, "gfront").reshape(TEAM, ndp, share, front_wide)
    mine = pick(front_grads, own_z, 1)
    got = [
        flip_z(pick(front_grads, own_z ^ mask, 1).astype(BF), mask, f"gfront_z{mask}")
        for mask in range(1, ndp)
    ]
    gots_y = [got_y] + [
        flip(halves[b][1].astype(BF), top, f"dtokens{b}_y") for b in range(1, count)
    ]
    mine, got, halves, ups, ups_y, gots_y = hold(mine, got, halves, ups, ups_y, gots_y)
    front_grads = sum([part.astype(F32) for part in got], mine).reshape(2, 2, share, front_wide)

    piece = hidden // wide
    ups = join_y(ups, ups_y)
    grad_up = jnp.concatenate(
        [
            ups[y][:, hidden * c + piece * x : hidden * c + piece * (x + 1)]
            for y in range(2)
            for x in range(wide)
            for c in range(2)
        ],
        axis=-1,
    )
    got = [
        flip(
            pick(pick(front_grads, own_y ^ (d // 2), 0), own_c ^ (d % 2), 0).astype(BF),
            top * (d // 2) + d % 2,
            f"gfront_{d}",
        )
        for d in range(1, TEAM)
    ]
    mine = pick(pick(front_grads, own_y, 0), own_c, 0)
    d_rows = [halves[b][0] + gots_y[b].astype(F32) for b in range(count)]
    grad_inputs = out_cotangent.astype(F32) + jnp.stack(d_rows)
    mine, got, grad_inputs, grad_up, grad_out = hold(mine, got, grad_inputs, grad_up, grad_out)
    grad_query, grad_keyval, grad_gain, grad_bias = pl.pallas_call(
        finish_kernel,
        in_specs=[pl.BlockSpec(memory_space=pltpu.SMEM)] + [whole(share, front_wide)] * TEAM,
        out_specs=[whole(share, TEAM * heads_wide), whole(share, WIDE), whole(2, share), whole(2, share)],
        out_shape=[
            struct((share, TEAM * heads_wide), F32),
            struct((share, WIDE), F32),
            struct((2, share), F32),
            struct((2, share), F32),
        ],
        scratch_shapes=[pltpu.VMEM((WIDE, WIDE), F32)],
        cost_estimate=cost(1),
        name="finish",
    )(jnp.stack([own_c, own_y]).astype(jnp.int32), mine, *got)
    return (
        output,
        jnp.stack([part[0] for part in keyvals]),
        grad_inputs,
        grad_query,
        grad_keyval,
        grad_out,
        grad_up,
        down_grads,
        grad_gain.T,
        grad_bias.T,
    )


def solution(mesh):
    rows = P("dp", "seq", None)
    split = P(("seq", "dp"), None)
    return jax.shard_map(
        functools.partial(on_device, mesh.shape["seq"], mesh.shape["dp"]),
        mesh=mesh,
        in_specs=(rows,) + (split,) * 7 + (rows, rows),
        out_specs=(rows,) * 3 + (split,) * 7,
        check_vma=False,
    )
```

```python
import functools
import math

import jax
import jax.numpy as jnp
import numpy as np
from jax import lax
from jax.experimental import pallas as pl
from jax.experimental.pallas import tpu as pltpu
from jax.sharding import PartitionSpec as P

HEADS = 12
HEAD = 64
ROT = 16
TEAM = 4
MINE = HEADS // TEAM
WIDE = 2 * HEAD
EPSILON = 1e-05
BF = jnp.bfloat16
F32 = jnp.float32
SCALE = 1.0 / math.sqrt(HEAD)
MB = 1 << 20


def dot(left, right):
    return lax.dot_general(left, right, (((1,), (0,)), ((), ())), preferred_element_type=F32)


def dot_rt(left, right):
    return lax.dot_general(left, right, (((1,), (1,)), ((), ())), preferred_element_type=F32)


def dot_lt(left, right):
    return lax.dot_general(left, right, (((0,), (0,)), ((), ())), preferred_element_type=F32)


def lanes(shape):
    return lax.broadcasted_iota(jnp.int32, shape, len(shape) - 1)


def angle_tables(rows, count):
    lane = np.arange(WIDE) % HEAD
    frequency = np.exp(-math.log(10000.0) * (lane % (ROT // 2)) * (2.0 / ROT)) * (lane < ROT)
    sign = np.where(lane < ROT // 2, -1.0, 1.0)
    out = []
    for positions in (np.arange(rows), np.arange(count) * rows):
        angles = 0.25 * positions[:, None] * frequency
        out.append(np.stack([np.cos(angles), sign * np.sin(angles)]).astype(np.float32))
    return out


def table_of(place_ref, start_ref, rank):
    cos_row, sin_row = place_ref[0], place_ref[1]
    cos_start, sin_start = start_ref[0, pl.ds(rank, 1)], start_ref[1, pl.ds(rank, 1)]
    return cos_row * cos_start - sin_row * sin_start, sin_row * cos_start + cos_row * sin_start


def keys_only(tables):
    keys_side = lanes(tables[0].shape) < HEAD
    return jnp.where(keys_side, tables[0], 1.0), jnp.where(keys_side, tables[1], 0.0)


def turn(values, tables, sign):
    near = (lanes(values.shape) % HEAD) < ROT // 2
    swapped = jnp.where(
        near, pltpu.roll(values, WIDE - ROT // 2, 1), pltpu.roll(values, ROT // 2, 1)
    )
    return values * tables[0] + (sign * swapped) * tables[1]


def standardize(tokens):
    center = tokens - jnp.mean(tokens, axis=-1, keepdims=True)
    spread = jnp.mean(center * center, axis=-1, keepdims=True)
    scale = lax.rsqrt(spread + EPSILON)
    return center * scale, scale


def norm_back(hat, scale, pulled):
    return scale * (
        pulled
        - jnp.mean(pulled, axis=-1, keepdims=True)
        - hat * jnp.mean(pulled * hat, axis=-1, keepdims=True)
    )


def three_parts(column):
    high = column.astype(BF)
    rest = column - high.astype(F32)
    mid = rest.astype(BF)
    low = (rest - mid.astype(F32)).astype(BF)
    return high, mid, low


def marked(lane, base, parts):
    out = jnp.zeros(lane.shape, BF)
    for index, part in enumerate(parts):
        out = jnp.where(lane == base + index, part, out)
    return out


def fetch(refs, held, arrived):
    step = pl.program_id(0)

    def start(r):
        for index, ref in enumerate(refs):

            @pl.when(r == index)
            def _(ref=ref):
                pltpu.make_async_copy(ref, held.at[r % 2], arrived.at[r % 2]).start()

    @pl.when(step == 0)
    def _():
        start(step)

    @pl.when(step + 1 < len(refs))
    def _():
        start(step + 1)

    pltpu.make_async_copy(refs[0], held.at[step % 2], arrived.at[step % 2]).wait()
    return held[step % 2]


def normalize(hat, norm_ref, which):
    return (hat * norm_ref[which : which + 1, :] + norm_ref[which + 2 : which + 3, :]).astype(BF)


def put(r, near_ref, far_ref, value):
    @pl.when(r < 2)
    def _():
        near_ref[0] = value

    @pl.when(r >= 2)
    def _():
        far_ref[0] = value


def assemble(own_x, refs, groups, held):
    wide = sum(ref.shape[0] for ref in refs)
    relative = 0
    for ref in refs:
        block = ref.shape[2]
        for index in range(ref.shape[0]):
            x = own_x ^ relative
            for group in range(groups):
                place = (group // 2 * wide + x) * 2 + group % 2 if groups > 1 else x
                start = pl.multiple_of(place * block, block)
                held[pl.ds(start, block), :] = ref[index, group]
            relative += 1


def prepare_kernel(parts, first, last, top, wide, own_ref, *refs):
    x_refs, refs = refs[: TEAM * last], refs[TEAM * last :]
    front_refs, refs = refs[:parts], refs[parts:]
    place_ref, start_ref, query_ref, keyval_ref, *refs = refs
    *refs, held, arrived = refs
    own = own_ref[0]
    copies = [pltpu.make_async_copy(ref, held.at[i], arrived.at[i]) for i, ref in enumerate(x_refs)]
    for copy in copies:
        copy.start()
    if first:
        front_ref, norm_ref = refs
        assemble((own // 2) % wide, front_refs, TEAM, front_ref)
        norm_ref[...] = jnp.transpose(front_ref[:, 2 * WIDE :].astype(F32))[HEAD : HEAD + 8]
    else:
        front_ref, norm_ref = front_refs
        (mlp_ref,) = refs

    for copy in copies:
        copy.wait()

    @pl.loop(0, TEAM)
    def _(r):
        hat, _ = standardize(held[r, 0].astype(F32))
        made = dot(normalize(hat, norm_ref, 0), front_ref[...])
        tables = table_of(place_ref, start_ref, rank_of(own, r, top))
        keyval_ref[r] = turn(made[:, :WIDE], keys_only(tables), 1.0).astype(BF)
        for part in range(2):
            piece = made[:, WIDE * (part + 1) : WIDE * (part + 2)]
            query_ref[r, :, WIDE * part : WIDE * (part + 1)] = (turn(piece, tables, 1.0) * SCALE).astype(BF)
        if not first:
            mlp_ref[r, last - 1] = normalize(hat, norm_ref, 1)
            for index in range(1, last):
                hat, _ = standardize(held[index * TEAM + r, 0].astype(F32))
                mlp_ref[r, index - 1] = normalize(hat, norm_ref, 1)


def rank_of(own, block, top):
    return own ^ ((block % 2) * top) ^ (block // 2)


def slot_of(away, top, wide):
    return ((away // 2) % wide) * TEAM + (away // top) % 2 + 2 * (away % 2)


def load_keyval(own, top, wide, refs, keys_ref, values_ref, base):
    slots = {}
    start = 0
    for ref in refs:
        for index in range(ref.shape[0]):
            slots[start + index] = ref, index
        start += ref.shape[0]
    for away in range(start):
        ref, index = slots[(away // 2) % wide * TEAM + (away // top) % 2 + 2 * (away % 2)]
        block = ref[index]
        rows = block.shape[0]
        at = pl.ds(pl.multiple_of((own ^ away) * rows, rows), rows)
        lane = lanes((rows, WIDE))
        keys_ref[at] = jnp.where(lane < HEAD, block, base[1])
        values_ref[at] = jnp.where(lane < HEAD, base[0], block)


def forward_kernel(top, wide, own_ref, query_ref, *refs):
    kv_refs, (context_ref, marked_ref, low_ref, score_ref, peak_ref, keys_ref, values_ref) = refs[:-7], refs[-7:]
    rows = query_ref.shape[2]
    groups = 2 * MINE
    own = own_ref[0]
    step = pl.program_id(0)
    mine = own ^ (step * top)
    base = mine // 2 * 2
    lane = lanes((rows, WIDE))

    @pl.when(step == 0)
    def _():
        one = jnp.ones((rows, WIDE), BF)
        load_keyval(own, top, wide, kv_refs, keys_ref, values_ref, (one, jnp.zeros_like(one)))

    for c in range(2):
        first = query_ref[c, 0, :, :WIDE]
        at = c * MINE * rows
        low_ref[at : at + rows] = first
        low_ref[at + rows : at + 2 * rows] = pltpu.roll(first.astype(F32), HEAD, 1).astype(BF)
        low_ref[at + 2 * rows : at + 3 * rows] = query_ref[c, 0, :, WIDE:]

    count = base // 2
    key = lax.broadcasted_iota(jnp.int32, (rows, 2 * rows), 1)
    query = lax.broadcasted_iota(jnp.int32, (rows, 2 * rows), 0)
    peak_ref[...] = jnp.full(peak_ref.shape, -1e30, F32)

    @pl.loop(0, count + 1)
    def _(index):
        at = pl.ds(pl.multiple_of(index * 2 * rows, 2 * rows), 2 * rows)
        scores = dot_rt(low_ref[...], keys_ref[at])
        keeps = [key <= query + ((mine ^ c) - 2 * index) * rows for c in range(2)]
        for group in range(groups):
            at = slice(group * rows, (group + 1) * rows)
            part = jnp.where(keeps[group // MINE], scores[at], -1e30)
            score_ref[index, at] = part
            best = functools.reduce(
                jnp.maximum, [part[:, column : column + WIDE] for column in range(0, 2 * rows, WIDE)]
            )
            peak_ref[at] = jnp.maximum(peak_ref[at], best)

    peak_ref[...] = jnp.broadcast_to(jnp.max(peak_ref[...], axis=-1, keepdims=True), peak_ref.shape)

    def weigh(index, sums):
        at = pl.ds(pl.multiple_of(index * 2 * rows, 2 * rows), 2 * rows)
        peak = peak_ref[...]
        weights = jnp.exp(score_ref[index] - jnp.concatenate([peak] * (2 * rows // WIDE), axis=1))
        return sums + dot(weights.astype(BF), values_ref[at])

    sums = lax.fori_loop(0, count + 1, weigh, jnp.zeros((groups * rows, WIDE), F32))
    for c in range(2):
        made = []
        for head in range(MINE):
            at = slice((c * MINE + head) * rows, (c * MINE + head + 1) * rows)
            part = sums[at]
            swapped = pltpu.roll(part, HEAD, 1)
            total = jnp.where(lane < HEAD, part, swapped)
            made.append(jnp.where(lane < HEAD, swapped, part) / total)
            logsum = peak_ref[at] + jnp.log(total)
            marked_ref[c, 0, head] = jnp.where(
                lane < HEAD, low_ref[at], marked(lane, HEAD, three_parts(-logsum))
            )
        context_ref[c, 0, :, :WIDE] = jnp.where(lane < HEAD, made[0], made[1]).astype(BF)
        context_ref[c, 0, :, WIDE:] = jnp.where(lane < HEAD, made[2], 0.0).astype(BF)


def backward_kernel(top, wide, own_ref, query_ref, grad_ref, place_ref, start_ref, *refs):
    kv_refs, (dquery_ref, keep_ref, send_ref, sum_ref, keys_ref, values_ref, dkeyval_ref) = refs[:-7], refs[-7:]
    rows = query_ref.shape[3]
    own = own_ref[0]
    step = pl.program_id(0)
    mine = own ^ (step * top)
    base = mine // 2 * 2
    lane = lanes((rows, WIDE))
    wide_lane = lanes((2 * rows, WIDE))

    @pl.when(step == 0)
    def _():
        dkeyval_ref[...] = jnp.zeros_like(dkeyval_ref)
        ones_low = jnp.where(lane < 3, 1.0, 0.0).astype(BF)
        ones_high = jnp.where((lane >= HEAD) & (lane < HEAD + 3), 1.0, 0.0).astype(BF)
        load_keyval(own, top, wide, kv_refs, keys_ref, values_ref, (ones_low, ones_high))

    key = lax.broadcasted_iota(jnp.int32, (2 * rows, rows), 0)
    row = lax.broadcasted_iota(jnp.int32, (2 * rows, rows), 1)
    sum_ref[...] = jnp.zeros_like(sum_ref)

    @pl.loop(0, base // 2 + 1)
    def _(index):
        at = pl.ds(pl.multiple_of(index * 2 * rows, 2 * rows), 2 * rows)
        keys = keys_ref[at]
        values = values_ref[at]
        d_keys = jnp.zeros((2 * rows, WIDE), F32)
        d_values = jnp.zeros((2 * rows, WIDE), F32)
        for c in range(2):
            keep = key <= row + ((mine ^ c) - 2 * index) * rows
            for head in range(MINE):
                query = query_ref[c, 0, head]
                grad = grad_ref[c, 0, head]
                probs = jnp.where(keep, jnp.exp(dot_rt(keys, query)), 0.0)
                d_scores = (probs * dot_rt(values, grad)).astype(BF)
                d_values += dot(probs.astype(BF), grad)
                d_keys += dot(d_scores, query)
                sum_ref[c, head] += dot_lt(keys, d_scores)
        dkeyval_ref[at] += jnp.where(wide_lane < HEAD, d_keys, d_values)

    for c in range(2):
        turned = [jnp.transpose(sum_ref[c, head]) * SCALE for head in range(MINE)]
        both = jnp.where(lane < HEAD, turned[0], pltpu.roll(turned[1], HEAD, 1))
        last = jnp.where(lane < HEAD, turned[2], 0.0)
        tables = table_of(place_ref, start_ref, mine ^ c)
        dquery_ref[c, 0, :, :WIDE] = turn(both, tables, -1.0).astype(BF)
        dquery_ref[c, 0, :, WIDE:] = turn(last, tables, -1.0).astype(BF)

    @pl.when(step == pl.num_programs(0) - 1)
    def _():
        half = send_ref.shape[0]
        for rank in range(2 * half):
            slot = slot_of(rank ^ own, top, wide)
            block = dkeyval_ref[rank * rows : (rank + 1) * rows]

            @pl.when(slot < half)
            def _():
                keep_ref[jnp.minimum(slot, half - 1)] = block

            @pl.when(slot >= half)
            def _():
                send_ref[jnp.maximum(slot - half, 0)] = block.astype(BF)


def split_rows(own_x, groups, total, keep_ref, send_ref):
    wide = 2 * keep_ref.shape[0]
    block = keep_ref.shape[2]
    for side, ref in enumerate((keep_ref, send_ref)):
        half = own_x // (wide // 2) ^ side
        for index in range(wide // 2):
            x = half * (wide // 2) + index
            for group in range(groups):
                place = (group // 2 * wide + x) * 2 + group % 2 if groups > 1 else x
                start = pl.multiple_of(place * block, block)
                ref[index, group] = total[pl.ds(start, block), :].astype(ref.dtype)


def split_z(own_z, total, keep_ref, send_ref):
    wide, half, block = keep_ref.shape[:3]
    for side, ref in enumerate((keep_ref, send_ref)):
        for x in range(wide):
            for index in range(half):
                place = (x * half + index) * 2 + (own_z % 2 ^ side)
                start = pl.multiple_of(place * block, block)
                ref[x, index] = total[pl.ds(start, block), :].astype(ref.dtype)


def hidden_kernel(count, parts, down_parts, own_ref, *refs):
    grad_refs, refs = refs[:4], refs[4:]
    normed_ref, *refs = refs
    context_refs, refs = refs[:count], refs[count:]
    more_refs, refs = refs[:parts], refs[parts:]
    down_refs, refs = refs[:down_parts], refs[down_parts:]
    (made_ref, made_far_ref, dnormed_ref, marked_ref, more_keep, more_send, down_keep, down_send, *refs) = refs
    (up_sum, low_sum, held, arrived, up_ref, low_ref) = refs
    step = pl.program_id(0)
    own_x = own_ref[0]
    rows = context_refs[0].shape[1]
    units = up_ref.shape[1]

    @pl.when(step == 0)
    def _():
        low_ref[units:] = jnp.zeros_like(low_ref[units:])
        assemble(own_x, more_refs, TEAM, up_ref)
        assemble(own_x, [ref.at[:, TEAM:] for ref in more_refs], 1, low_ref.at[units:])
        assemble(own_x, down_refs, 1, low_ref)

    normed = normed_ref[0].reshape(count * rows, normed_ref.shape[-1])
    context = jnp.concatenate([ref[0] for ref in context_refs], axis=0)
    grad = fetch(grad_refs, held, arrived).reshape(normed.shape)
    raw = dot(normed, up_ref[...])
    bell = 0.5 + 0.5 * lax.erf(raw * math.sqrt(0.5))
    slope = bell + raw * (jnp.exp(raw * raw * -0.5) * (1.0 / math.sqrt(2.0 * math.pi)))
    low = jnp.concatenate([(raw * bell).astype(BF), context], axis=1)
    pulled = dot_rt(grad, low_ref[...])
    d_raw = (pulled[:, :units] * slope).astype(BF)
    made = dot(low, low_ref[...]).astype(BF)
    put(step, made_ref, made_far_ref, made.reshape(made_ref.shape[1:]))
    dnormed_ref[0] = dot_rt(d_raw, up_ref[...]).astype(BF).reshape(dnormed_ref.shape[1:])
    glow = dot_lt(low, grad)
    gup = dot_lt(normed, d_raw)

    pulled = pulled[:, units:].astype(BF)
    product = pulled.astype(F32) * context.astype(F32)
    lane = lanes((grad.shape[0], WIDE))
    for head in range(MINE):
        column = WIDE * (head // 2)
        side = (lane < HEAD) if head % 2 == 0 else (lane >= HEAD)
        delta = jnp.sum(
            jnp.where(side, product[:, column : column + WIDE], 0.0), axis=-1, keepdims=True
        )
        piece = pulled[:, column : column + WIDE]
        if head % 2 == 0:
            piece = pltpu.roll(piece.astype(F32), HEAD, 1).astype(BF)
        piece = jnp.where(
            lane >= HEAD, piece, marked(lane, 0, three_parts(jnp.broadcast_to(-delta, lane.shape)))
        )
        marked_ref[0, :, head] = piece.reshape(count, rows, WIDE)

    @pl.when(step == 0)
    def _():
        low_sum[...] = glow
        up_sum[...] = gup

    @pl.when(step > 0)
    def _():
        low_sum[...] += glow
        up_sum[...] += gup

    @pl.when(step == pl.num_programs(0) - 1)
    def _():
        split_rows(own_x, TEAM, up_sum, more_keep, more_send)
        split_rows(own_x, 1, low_sum.at[units:], more_keep.at[:, TEAM:], more_send.at[:, TEAM:])
        split_z(own_ref[1], low_sum, down_keep, down_send)


def tokens_kernel(last, top, wide, own_ref, x0_ref, x1_ref, x2_ref, x3_ref, dnormed_ref, dquery_ref, dkeyval_ref, cotangent_ref, weight_ref, norm_ref, place_ref, start_ref, *refs):
    if last:
        before_ref, nbefore_ref, dx_ref, dx_far_ref, keep_ref, send_ref, gfront_ref, gnorm_ref, held, arrived = refs
    else:
        dx_ref, dx_far_ref, gfront_ref, gnorm_ref, held, arrived = refs
    step = pl.program_id(0)
    tokens = fetch((x0_ref, x1_ref, x2_ref, x3_ref), held, arrived)
    hat, scale = standardize(tokens[0].astype(F32))
    tables = table_of(place_ref, start_ref, rank_of(own_ref[0], step, top))
    d_keyval = dkeyval_ref[0] + jnp.where(step == 0, cotangent_ref[0].astype(F32), 0.0)
    d_keyval = turn(d_keyval, keys_only(tables), -1.0).astype(BF)
    d_front = jnp.concatenate([d_keyval, dquery_ref[0]], axis=1)
    d_attn = dot_rt(d_front, weight_ref[...])
    d_mlp = dnormed_ref[0, 0].astype(F32)
    d_tokens = norm_back(hat, scale, d_attn * norm_ref[0:1, :] + d_mlp * norm_ref[1:2, :])
    put(step, dx_ref, dx_far_ref, d_tokens.astype(BF))
    sums = [
        jnp.sum(piece, axis=0, keepdims=True) for piece in (d_attn * hat, d_mlp * hat, d_attn, d_mlp)
    ]
    sums = jnp.concatenate(sums + [jnp.zeros_like(sums[0])] * 4, axis=0)
    gfront = dot_lt(normalize(hat, norm_ref, 0), d_front)

    @pl.when(step == 0)
    def _():
        gfront_ref[...] = before_ref[...] + gfront if last else gfront
        gnorm_ref[...] = nbefore_ref[...] + sums if last else sums

    @pl.when(step > 0)
    def _():
        gfront_ref[...] += gfront
        gnorm_ref[...] += sums

    if last:

        @pl.when(step == pl.num_programs(0) - 1)
        def _():
            width = gnorm_ref.shape[1]
            sums = jnp.concatenate(
                [jnp.zeros((HEAD, width), F32), gnorm_ref[...], jnp.zeros((HEAD - 8, width), F32)], axis=0
            )
            gfront_ref[:, 2 * WIDE :] += jnp.transpose(sums)
            split_rows((own_ref[0] // 2) % wide, TEAM, gfront_ref, keep_ref, send_ref)


def finish_kernel(own_ref, mine_ref, c_ref, y_ref, both_ref, query_ref, keyval_ref, gain_ref, bias_ref, turned_ref):
    parts = [mine_ref[...]] + [ref[...].astype(F32) for ref in (c_ref, y_ref, both_ref)]
    total = parts[0] + parts[1] + parts[2] + parts[3]
    keyval_ref[...] = total[:, :WIDE]
    turned_ref[...] = jnp.zeros_like(turned_ref)
    turned_ref[: total.shape[0]] = total[:, 2 * WIDE :]
    ends = jnp.transpose(turned_ref[...])[HEAD : HEAD + 4, : total.shape[0]]
    gain_ref[...] = ends[:2]
    bias_ref[...] = ends[2:]
    for index in range(2):
        bit = own_ref[index] == 0
        parts = [jnp.where(bit, parts[place], parts[place ^ (1 << index)]) for place in range(TEAM)]
    query_ref[...] = jnp.concatenate([part[:, WIDE : WIDE + MINE * HEAD] for part in parts], axis=1)


def params(limit):
    return pltpu.CompilerParams(vmem_limit_bytes=limit * MB)


def cost(micros):
    return pl.CostEstimate(flops=int(micros * 1.1e9), bytes_accessed=0, transcendentals=0)


def struct(shape, kind):
    return jax.ShapeDtypeStruct(shape, kind)


def whole(*shape):
    return pl.BlockSpec(shape, lambda *_: (0,) * len(shape))


def on_device(nseq, ndp, inputs, w_query, w_keyval, w_out, w_up, w_down, norm_gain, norm_bias, out_cotangent, kv_cotangent):
    count, rows, width = inputs.shape
    top = nseq // 2
    wide = nseq // TEAM
    own = lax.axis_index("seq")
    own_y, own_x, own_c = own // top, (own // 2) % wide, own % 2
    own_z = lax.axis_index("dp")
    share = w_query.shape[0]
    down_share = w_down.shape[0]
    hidden = w_up.shape[1] // TEAM
    heads_wide = MINE * HEAD
    front_wide = 3 * WIDE
    slots = TEAM * wide

    def flip(value, mask, what):
        with jax.named_scope("swap_" + what):
            return lax.ppermute(value, "seq", [(i, i ^ mask) for i in range(nseq)])

    def flip_z(value, mask, what):
        with jax.named_scope("swap_" + what):
            return lax.ppermute(value, "dp", [(i, i ^ mask) for i in range(ndp)])

    def hold(*values):
        return lax.optimization_barrier(values)

    def after(value, *others):
        return hold(value, *others)[0]

    def in_order(bit, mine, other, axis):
        return jnp.where(
            bit == 0, jnp.stack([mine, other], axis), jnp.stack([other, mine], axis)
        )

    def merge(value, axis):
        return value.reshape(value.shape[:axis] + (-1,) + value.shape[axis + 2 :])

    def pick(value, index, axis):
        return lax.dynamic_index_in_dim(value, index, axis, keepdims=False)

    def swap_z(value, mask, axis, what):
        other = flip_z(value, mask, f"{what}_z{mask}")

        def join(other):
            return merge(in_order((own_z // mask) % 2, value, other, axis + 1), axis)

        return other, join

    def gather_z(value, axis, what, step=None):
        masks = [ndp >> (index + 1) for index in range(ndp.bit_length() - 1)]
        for mask in masks if step is None else masks[step]:
            other, join = swap_z(value, mask, axis, what)
            value = join(other)
        return value

    def by_place(relative, bits):
        for index, bit in enumerate(bits):
            relative = [
                jnp.where(bit == 0, relative[place], relative[place ^ (1 << index)])
                for place in range(len(relative))
            ]
        return relative

    z_bits = [(own_z >> index) % 2 for index in range(ndp.bit_length() - 1)]

    def gather_x(value, what):
        parts = [value[None]]
        mask = 1
        while mask < wide:
            sent = jnp.concatenate(parts) if mask > 1 else parts[0]
            parts.append(flip(sent, 2 * mask, f"{what}_x{mask}"))
            mask *= 2
        return parts

    def flip_x(send, what):
        return flip(send, wide, f"{what}_x{wide // 2}")

    def scatter_x(keep, got, what):
        mask = wide // 2
        while True:
            value = keep.astype(F32) + got.astype(F32)
            mask //= 2
            if mask == 0:
                return value[0]
            bit = (own_x // mask) % 2
            value = value.reshape((2, -1) + value.shape[1:])
            keep = pick(value, bit, 0)
            got = flip(pick(value, 1 - bit, 0).astype(BF), 2 * mask, f"{what}_x{mask}")

    def halve_z(value, axis, what, mask):
        bit = (own_z // mask) % 2
        value = value.reshape(value.shape[:axis] + (-1, 2) + value.shape[axis + 1 :])
        got = flip_z(pick(value, 1 - bit, axis + 1).astype(BF), mask, f"{what}_z{mask}")
        return pick(value, bit, axis + 1), got

    def add_z(pair):
        return pair[0].astype(F32) + pair[1].astype(F32)

    def finish_z(value, axis, what):
        mask = 2
        while mask < ndp:
            value = add_z(halve_z(value, axis, what, mask))
            mask *= 2
        return jnp.squeeze(value, axis)

    def moved(onward):
        pairs = []
        for rank in range(nseq):
            for z in range(ndp):
                member = 2 * (rank // top) + rank % 2
                place = ((rank // 2) % wide) * ndp + z
                pairs.append((member * (nseq * ndp // TEAM) + place, rank * ndp + z))
        return [pair if onward else pair[::-1] for pair in pairs]

    def team(value, what, first, second):
        across = flip(after(value, first), top, what + "_y")
        return [value, across, flip(value, 1, what + "_c"), flip(after(across, second), 1, what + "_yc")]

    norms = jnp.concatenate([norm_gain, norm_bias], axis=1)
    queries_of = w_query.reshape(share, 2, 2, heads_wide).transpose(1, 2, 0, 3)
    same = jnp.concatenate([w_keyval, norms], axis=1)
    ups = w_up.reshape(share, 2, wide, 2, hidden // wide).transpose(1, 3, 0, 2, 4)
    ups = ups.reshape(2, 2, share, hidden)
    pad = jnp.zeros((2, 2, share, 2 * WIDE - heads_wide - norms.shape[1]), BF)
    spread = (2, 2, share)
    pack = jnp.concatenate(
        [
            jnp.broadcast_to(same[:, :WIDE], spread + (WIDE,)),
            queries_of,
            jnp.broadcast_to(same[:, WIDE:], spread + (norms.shape[1],)),
            pad,
            ups,
        ],
        axis=3,
    )
    masks = [ndp >> (index + 1) for index in range(ndp.bit_length() - 1)]
    near_masks, far_masks = masks[-1:], masks[:-1]

    def spread_z(value, axis, what, some):
        for mask in some:
            other, join = swap_z(value, mask, axis, what)
            value = join(other)
        return value

    def begin_z(value, axis, what, some):
        if not some:
            return value, lambda value: value
        return swap_z(spread_z(value, axis, what, some[:-1]), some[-1], axis, what)

    sequences = [inputs[b : b + 1] for b in range(count)]
    got = [
        flip(pick(pick(pack, own_y ^ (d // 2), 0), own_c ^ (d % 2), 0), top * (d // 2) + d % 2, f"pack_{d}")
        for d in range(1, TEAM)
    ]
    pack, got, sequences, w_out = hold(pack, got, sequences, w_out)
    across = [flip(sequences[0], top, "tokens0_y")]
    mine = pick(pick(pack, own_y, 0), own_c, 0)
    pack = jnp.stack(by_place([mine] + got, [own_c, own_y])).reshape(2, 2, share, -1)
    with jax.named_scope("swap_out_moved"):
        out_rows = lax.ppermute(w_out, ("seq", "dp"), moved(True))
    tokens_c = [flip(sequences[b], 1, f"tokens{b}_c") for b in range(count)]

    front_z = pack[..., :front_wide].reshape(TEAM, share, front_wide)
    got = [flip_z(front_z, mask, f"front_z{mask}") for mask in range(1, ndp)]
    front_z = jnp.stack(by_place([front_z] + got, z_bits), axis=1)
    down_x = jnp.concatenate(gather_x(w_down[None], "down"))
    front_z, pack, out_rows, across[0] = hold(front_z, pack, out_rows, across[0])
    for b in range(1, count):
        across.append(flip(after(sequences[b], across[b - 1]), top, f"tokens{b}_y"))
    tokens = [[sequences[0], across[0], tokens_c[0], flip(across[0], 1, "tokens0_yc")]]
    front_parts = gather_x(front_z.reshape(TEAM, ndp * share, front_wide), "front")
    more = jnp.concatenate(
        [pack[..., front_wide:].reshape(TEAM, share, hidden), out_rows.reshape(1, share, width)]
    )
    more_got, join_more = begin_z(more[:, None], 1, "more", far_masks)
    front_parts, tokens[0], down_x = hold(front_parts, tokens[0], down_x)
    own_rank = own.reshape(1).astype(jnp.int32)
    own_place = jnp.stack([own_x, own_z]).astype(jnp.int32)
    tables = [jnp.asarray(part) for part in angle_tables(rows, nseq)]

    def by_r(*last):
        return pl.BlockSpec((1,) + last, lambda r, *_: (r,) + (0,) * len(last))

    members = [pl.BlockSpec(memory_space=pl.ANY)] * TEAM

    def near(*last):
        return pl.BlockSpec((1,) + last, lambda r, *_: (jnp.minimum(r, 1),) + (0,) * len(last))

    def far(*last):
        return pl.BlockSpec((1,) + last, lambda r, *_: (jnp.maximum(r - 2, 0),) + (0,) * len(last))

    def call(kernel, scalar, inputs, in_specs, out_specs, out_shape, scratch, limit, micros, name, steps=TEAM):
        return pl.pallas_call(
            kernel,
            grid_spec=pltpu.PrefetchScalarGridSpec(
                num_scalar_prefetch=1,
                grid=(steps,),
                in_specs=in_specs,
                out_specs=out_specs,
                scratch_shapes=scratch,
            ),
            out_shape=out_shape,
            compiler_params=params(limit),
            cost_estimate=cost(micros),
            name=name,
        )(scalar, *inputs)

    table = by_r(rows, WIDE)
    block = [pltpu.VMEM((2, 1, rows, width), BF), pltpu.SemaphoreType.DMA((2,))]

    def prepare(b, weights):
        first = b == 0
        many = 1 if b < count - 1 else count
        held = tokens[b] + sum(tokens[: many - 1], [])
        outs = [struct((TEAM, rows, 2 * WIDE), BF), struct((TEAM, rows, WIDE), BF)]
        if first:
            outs += [struct((width, front_wide), BF), struct((8, width), F32)]
        else:
            outs += [struct((TEAM, many, rows, width), BF)]
        return call(
            functools.partial(prepare_kernel, len(weights), first, many, top, wide),
            own_rank,
            [*held, *weights, *tables],
            members * many + [whole(*part.shape) for part in [*weights, *tables]],
            [whole(*out.shape) for out in outs],
            outs,
            [pltpu.VMEM((many * TEAM, 1, rows, width), BF), pltpu.SemaphoreType.DMA((many * TEAM,))],
            16 if first else 24,
            0.5,
            "prepare",
            1,
        )

    *made_first, front, norm_rows = prepare(0, front_parts)
    prepared = [made_first]
    prepared[0], front, across[1:], more_got = hold(prepared[0], front, across[1:], more_got)
    for b in range(1, count):
        tokens.append([sequences[b], across[b], tokens_c[b], flip(across[b], 1, f"tokens{b}_yc")])
    more_got, join_more = begin_z(join_more(more_got), 1, "more", near_masks)
    prepared += [prepare(b, [front, norm_rows]) for b in range(1, count)]
    normed_mlp = prepared[-1][-1]
    queries, keyvals = [[part[index] for part in prepared] for index in range(2)]

    def keys_of_all(value, what):
        parts = [value]
        mask = 1
        while mask < wide:
            sent = jnp.concatenate(parts) if mask > 1 else parts[0]
            parts.append(flip(sent, 2 * mask, f"{what}_x{mask}"))
            mask *= 2
        return parts

    everyone = [keys_of_all(keyvals[b], f"keyval{b}") for b in range(count)]
    kv_specs = [whole(*part.shape) for part in everyone[0]]
    kv_scratch = [pltpu.VMEM((slots * rows, WIDE), BF)] * 2

    def by_pair(*last):
        return pl.BlockSpec((2, 1) + last, lambda y, *_: (0, y) + (0,) * len(last))

    def paired(value):
        return value.reshape((2, 2) + value.shape[1:])

    grads_y = flip(after(out_cotangent, tokens[-1][1]), top, "grads_y")
    grads_c = flip(out_cotangent, 1, "grads_c")
    everyone[0], queries, keyvals, more_got = hold(everyone[0], queries, keyvals, more_got)
    more_parts = gather_x(join_more(more_got).reshape(TEAM + 1, ndp * share, width), "more")
    down_got, join_down = begin_z(after(down_x, more_parts[0])[:, None], 1, "down", far_masks)
    contexts = []
    marked_queries = []
    for b in range(count):
        context, marked_query = call(
            functools.partial(forward_kernel, top, wide),
            own_rank,
            [paired(queries[b]), *everyone[b]],
            [by_pair(rows, 2 * WIDE)] + kv_specs,
            [by_pair(rows, 2 * WIDE), by_pair(MINE, rows, WIDE)],
            [struct((2, 2, rows, 2 * WIDE), BF), struct((2, 2, MINE, rows, WIDE), BF)],
            [
                pltpu.VMEM((2 * MINE * rows, WIDE), BF),
                pltpu.VMEM((slots // 2, 2 * MINE * rows, 2 * rows), F32),
                pltpu.VMEM((2 * MINE * rows, WIDE), F32),
            ]
            + kv_scratch,
            32,
            15,
            "attend",
            2,
        )
        context = context.reshape((TEAM,) + context.shape[2:])
        contexts.append(context)
        marked_queries.append(marked_query)
        if b == 0:
            contexts[0], everyone[1:], queries, grads_y, down_got = hold(
                contexts[0], everyone[1:], queries, grads_y, down_got
            )
            down_got, join_down = begin_z(join_down(down_got), 1, "down", near_masks)
            grads = [out_cotangent, grads_y, grads_c, flip(grads_y, 1, "grads_yc")]
    contexts, grads, more_parts, down_got = hold(contexts, grads, more_parts, down_got)
    down_parts = [join_down(down_got).reshape(wide, 1, ndp * down_share, width)]

    half = max(wide // 2, 1)
    more_half = (half, TEAM + 1, ndp * share, width)
    down_half = (wide, ndp // 2, down_share, width)
    made, made_far, d_normed, marked_grad, more_keep, more_send, down_keep, down_send = call(
        functools.partial(hidden_kernel, count, len(more_parts), len(down_parts)),
        own_place,
        [*grads, normed_mlp, *contexts, *more_parts, *down_parts],
        members
        + [by_r(count, rows, width)]
        + [by_r(rows, 2 * WIDE)] * count
        + [whole(*part.shape) for part in more_parts + down_parts],
        [
            near(count, rows, width),
            far(count, rows, width),
            by_r(count, rows, width),
            by_r(count, MINE, rows, WIDE),
            whole(*more_half),
            whole(*more_half),
            whole(*down_half),
            whole(*down_half),
        ],
        [
            struct((2, count, rows, width), BF),
            struct((2, count, rows, width), BF),
            struct((TEAM, count, rows, width), BF),
            struct((TEAM, count, MINE, rows, WIDE), BF),
            struct(more_half, BF),
            struct(more_half, BF),
            struct(down_half, BF),
            struct(down_half, BF),
        ],
        [
            pltpu.VMEM((width, hidden), F32),
            pltpu.VMEM((hidden + 2 * WIDE, width), F32),
            pltpu.VMEM((2, count, rows, width), BF),
            pltpu.SemaphoreType.DMA((2,)),
            pltpu.VMEM((width, hidden), BF),
            pltpu.VMEM((hidden + 2 * WIDE, width), BF),
        ],
        52,
        27,
        "hidden",
    )

    def sum_c(value, what, *others):
        return value[0].astype(F32) + after(flip(value[1], 1, what + "_c"), *others).astype(F32)

    def sum_y(value, what, *others):
        got = flip(value[1].astype(BF), top, what + "_y")
        return value[0] + after(got, *others).astype(F32)

    d_queries = []
    kept = []
    sent = []
    key_half = (slots // 2, rows, WIDE)
    for b in range(count):
        d_query, keep, send = call(
            functools.partial(backward_kernel, top, wide),
            own_rank,
            [marked_queries[b], paired(marked_grad), *tables, *everyone[b]],
            [
                by_pair(MINE, rows, WIDE),
                pl.BlockSpec((2, 1, None, MINE, rows, WIDE), lambda y, *_, b=b: (0, y, b, 0, 0, 0)),
            ]
            + [whole(*part.shape) for part in tables]
            + kv_specs,
            [by_pair(rows, 2 * WIDE), whole(*key_half), whole(*key_half)],
            [struct((2, 2, rows, 2 * WIDE), BF), struct(key_half, F32), struct(key_half, BF)],
            [pltpu.VMEM((2, MINE, WIDE, rows), F32)]
            + kv_scratch
            + [pltpu.VMEM((slots * rows, WIDE), F32)],
            16,
            20,
            "attend_back",
            2,
        )
        d_query = d_query.reshape((TEAM,) + d_query.shape[2:])
        d_queries.append(d_query)
        kept.append(keep)
        sent.append(send)
        if b == 0:
            got_c = flip(made_far, 1, "made_c")
            got_x = flip_x(more_send, "gmore")
            down_got = flip_z(down_send, 1, "gdown_z1")
            (d_queries, kept, sent, marked_grad, made, got_c, more_keep, got_x, down_keep, down_got) = hold(
                d_queries, kept, sent, marked_grad, made, got_c, more_keep, got_x, down_keep, down_got
            )
            made = made.astype(F32) + got_c.astype(F32)
            more_grads = scatter_x(more_keep, got_x, "gmore").reshape(TEAM + 1, ndp, share, width)
            got_y = flip(made[1].astype(BF), top, "made_y")
            more_z = halve_z(more_grads, 1, "gmore", 1)
            keys_got = flip_x(sent[0], "gkeyval0")
            down_grads = down_keep.astype(F32) + down_got.astype(F32)
            mask = 2
            while mask < ndp:
                down_z = halve_z(down_grads, 1, "gdown", mask)
                down_grads = add_z(down_z) if 2 * mask < ndp else down_grads
                mask *= 2
    (d_queries, kept, sent, made, got_y, more_z, keys_got) = hold(
        d_queries, kept, sent, made, got_y, more_z, keys_got
    )
    output = (inputs.astype(F32) + made[0] + got_y.astype(F32)).astype(BF)
    more_grads = add_z(more_z)
    keys_gots = [keys_got] + [flip_x(sent[b], f"gkeyval{b}") for b in range(1, count)]

    def keys_back(b):
        keep, got = kept[b], keys_gots[b]
        mask = wide // 2
        while True:
            value = keep + got.astype(F32)
            mask //= 2
            if mask == 0:
                return value
            keep = value[: value.shape[0] // 2]
            got = flip(value[value.shape[0] // 2 :].astype(BF), 2 * mask, f"gkeyval{b}_x{mask}")

    def join_c(value, got):
        mine = pick(value.reshape((2, 2) + value.shape[1:]), own_c, 1)
        got = got.astype(F32)
        return jnp.where(own_c == 0, mine, got), jnp.where(own_c == 0, got, mine)

    def join_y(value, got):
        mine = pick(value, own_y, 0)
        got = got.astype(F32)
        return jnp.where(own_y == 0, mine, got), jnp.where(own_y == 0, got, mine)

    pulled = []
    carried = []
    front_half = (half, TEAM, ndp * share, front_wide)
    for b in range(count):
        last = b == count - 1
        outs = [struct((2, rows, width), BF), struct((2, rows, width), BF)]
        out_specs = [near(rows, width), far(rows, width)]
        sums = [struct((width, front_wide), F32), struct((8, width), F32)]
        if last:
            outs += [struct(front_half, F32), struct(front_half, BF)]
        else:
            outs += sums
        d_tokens, d_tokens_far, *carried = call(
            functools.partial(tokens_kernel, last, top, wide),
            own_rank,
            [
                *tokens[b],
                d_normed,
                d_queries[b],
                keys_back(b),
                kv_cotangent,
                front,
                norm_rows,
                *tables,
                *carried,
            ],
            members
            + [
                pl.BlockSpec((1, 1, rows, width), lambda r, *_, b=b: (r, b, 0, 0)),
                by_r(rows, 2 * WIDE),
                table,
                pl.BlockSpec((1, rows, WIDE), lambda r, *_, b=b: (b, 0, 0)),
                whole(width, front_wide),
                whole(8, width),
            ]
            + [whole(*part.shape) for part in tables]
            + [whole(*part.shape) for part in carried],
            out_specs + [whole(*out.shape) for out in outs[2:]],
            outs,
            ([pltpu.VMEM(out.shape, F32) for out in sums] if last else []) + block,
            14,
            7,
            "pull_tokens",
        )
        pulled.append((d_tokens, d_tokens_far))
        if b == 0:
            mask = 2
            while mask < ndp:
                more_z = halve_z(more_grads, 1, "gmore", mask)
                more_grads = add_z(more_z) if 2 * mask < ndp else more_grads
                mask *= 2
            (carried, pulled, down_z, keys_gots, kept, d_queries) = hold(
                carried, pulled, down_z, keys_gots, kept, d_queries
            )
            got_c = flip(pulled[0][1], 1, "dtokens0_c")
            down_grads = jnp.squeeze(add_z(down_z), 1)
            x_half = down_grads.reshape((2, -1) + down_grads.shape[1:])
            x_bit = own_x // (wide // 2)
            down_keep = pick(x_half, x_bit, 0)
            down_got = flip_x(pick(x_half, 1 - x_bit, 0).astype(BF), "gdown")
    front_keep, front_send = carried
    front_keep, front_send, pulled, got_c, more_z = hold(front_keep, front_send, pulled, got_c, more_z)
    more_grads = jnp.squeeze(add_z(more_z), 1)
    down_grads = scatter_x(down_keep, down_got, "gdown")

    def add_c(pair, got):
        return pair[0].astype(F32) + got.astype(F32)

    front_got = flip_x(front_send, "gfront")
    halves = [add_c(pulled[0], got_c)]
    got_y = flip(halves[0][1].astype(BF), top, "dtokens0_y")
    gots_c = [flip(pulled[b][1], 1, f"dtokens{b}_c") for b in range(1, count)]
    ups_c = flip(
        pick(more_grads[:TEAM].reshape(2, 2, share, hidden), 1 - own_c, 1).astype(BF), 1, "gup_c"
    )
    front_keep, front_got, gots_c, more_grads, ups_c = hold(
        front_keep, front_got, gots_c, more_grads, ups_c
    )
    ups = jnp.concatenate(join_c(more_grads[:TEAM], ups_c), axis=-1)
    ups_y = flip(pick(ups, 1 - own_y, 0).astype(BF), top, "gup_y")
    halves += [add_c(pulled[b], gots_c[b - 1]) for b in range(1, count)]
    with jax.named_scope("swap_gout_moved"):
        grad_out = lax.ppermute(more_grads[TEAM].astype(BF), ("seq", "dp"), moved(False)).astype(F32)
    front_grads = scatter_x(front_keep, front_got, "gfront").reshape(TEAM, ndp, share, front_wide)
    mine = pick(front_grads, own_z, 1)
    got = [
        flip_z(pick(front_grads, own_z ^ mask, 1).astype(BF), mask, f"gfront_z{mask}")
        for mask in range(1, ndp)
    ]
    gots_y = [got_y] + [
        flip(halves[b][1].astype(BF), top, f"dtokens{b}_y") for b in range(1, count)
    ]
    mine, got, halves, ups, ups_y, gots_y = hold(mine, got, halves, ups, ups_y, gots_y)
    front_grads = sum([part.astype(F32) for part in got], mine).reshape(2, 2, share, front_wide)

    piece = hidden // wide
    ups = join_y(ups, ups_y)
    grad_up = jnp.concatenate(
        [
            ups[y][:, hidden * c + piece * x : hidden * c + piece * (x + 1)]
            for y in range(2)
            for x in range(wide)
            for c in range(2)
        ],
        axis=-1,
    )
    got = [
        flip(
            pick(pick(front_grads, own_y ^ (d // 2), 0), own_c ^ (d % 2), 0).astype(BF),
            top * (d // 2) + d % 2,
            f"gfront_{d}",
        )
        for d in range(1, TEAM)
    ]
    mine = pick(pick(front_grads, own_y, 0), own_c, 0)
    d_rows = [halves[b][0] + gots_y[b].astype(F32) for b in range(count)]
    grad_inputs = out_cotangent.astype(F32) + jnp.stack(d_rows)
    mine, got, grad_inputs, grad_up, grad_out = hold(mine, got, grad_inputs, grad_up, grad_out)
    grad_query, grad_keyval, grad_gain, grad_bias = pl.pallas_call(
        finish_kernel,
        in_specs=[pl.BlockSpec(memory_space=pltpu.SMEM)] + [whole(share, front_wide)] * TEAM,
        out_specs=[whole(share, TEAM * heads_wide), whole(share, WIDE), whole(2, share), whole(2, share)],
        out_shape=[
            struct((share, TEAM * heads_wide), F32),
            struct((share, WIDE), F32),
            struct((2, share), F32),
            struct((2, share), F32),
        ],
        scratch_shapes=[pltpu.VMEM((WIDE, WIDE), F32)],
        cost_estimate=cost(1),
        name="finish",
    )(jnp.stack([own_c, own_y]).astype(jnp.int32), mine, *got)
    return (
        output,
        jnp.stack([part[0] for part in keyvals]),
        grad_inputs,
        grad_query,
        grad_keyval,
        grad_out,
        grad_up,
        down_grads,
        grad_gain.T,
        grad_bias.T,
    )


def solution(mesh):
    rows = P("dp", "seq", None)
    split = P(("seq", "dp"), None)
    return jax.shard_map(
        functools.partial(on_device, mesh.shape["seq"], mesh.shape["dp"]),
        mesh=mesh,
        in_specs=(rows,) + (split,) * 7 + (rows, rows),
        out_specs=(rows,) * 3 + (split,) * 7,
        check_vma=False,
    )
```

```python
import functools
import math

import jax
import jax.numpy as jnp
import numpy as np
from jax import lax
from jax.experimental import pallas as pl
from jax.experimental.pallas import tpu as pltpu
from jax.sharding import PartitionSpec as P

HEADS = 12
HEAD = 64
ROT = 16
TEAM = 4
MINE = HEADS // TEAM
WIDE = 2 * HEAD
EPSILON = 1e-05
BF = jnp.bfloat16
F32 = jnp.float32
SCALE = 1.0 / math.sqrt(HEAD)
MB = 1 << 20


def dot(left, right):
    return lax.dot_general(left, right, (((1,), (0,)), ((), ())), preferred_element_type=F32)


def dot_rt(left, right):
    return lax.dot_general(left, right, (((1,), (1,)), ((), ())), preferred_element_type=F32)


def dot_lt(left, right):
    return lax.dot_general(left, right, (((0,), (0,)), ((), ())), preferred_element_type=F32)


def lanes(shape):
    return lax.broadcasted_iota(jnp.int32, shape, len(shape) - 1)


def angle_tables(rows, count):
    lane = np.arange(WIDE) % HEAD
    frequency = np.exp(-math.log(10000.0) * (lane % (ROT // 2)) * (2.0 / ROT)) * (lane < ROT)
    sign = np.where(lane < ROT // 2, -1.0, 1.0)
    out = []
    for positions in (np.arange(rows), np.arange(count) * rows):
        angles = 0.25 * positions[:, None] * frequency
        out.append(np.stack([np.cos(angles), sign * np.sin(angles)]).astype(np.float32))
    return out


def table_of(place_ref, start_ref, rank):
    cos_row, sin_row = place_ref[0], place_ref[1]
    cos_start, sin_start = start_ref[0, pl.ds(rank, 1)], start_ref[1, pl.ds(rank, 1)]
    return cos_row * cos_start - sin_row * sin_start, sin_row * cos_start + cos_row * sin_start


def keys_only(tables):
    keys_side = lanes(tables[0].shape) < HEAD
    return jnp.where(keys_side, tables[0], 1.0), jnp.where(keys_side, tables[1], 0.0)


def turn(values, tables, sign):
    near = (lanes(values.shape) % HEAD) < ROT // 2
    swapped = jnp.where(
        near, pltpu.roll(values, WIDE - ROT // 2, 1), pltpu.roll(values, ROT // 2, 1)
    )
    return values * tables[0] + (sign * swapped) * tables[1]


def standardize(tokens):
    center = tokens - jnp.mean(tokens, axis=-1, keepdims=True)
    spread = jnp.mean(center * center, axis=-1, keepdims=True)
    scale = lax.rsqrt(spread + EPSILON)
    return center * scale, scale


def norm_back(hat, scale, pulled):
    return scale * (
        pulled
        - jnp.mean(pulled, axis=-1, keepdims=True)
        - hat * jnp.mean(pulled * hat, axis=-1, keepdims=True)
    )


def three_parts(column):
    high = column.astype(BF)
    rest = column - high.astype(F32)
    mid = rest.astype(BF)
    low = (rest - mid.astype(F32)).astype(BF)
    return high, mid, low


def marked(lane, base, parts):
    out = jnp.zeros(lane.shape, BF)
    for index, part in enumerate(parts):
        out = jnp.where(lane == base + index, part, out)
    return out


def fetch(refs, held, arrived):
    step = pl.program_id(0)

    def start(r):
        for index, ref in enumerate(refs):

            @pl.when(r == index)
            def _(ref=ref):
                pltpu.make_async_copy(ref, held.at[r % 2], arrived.at[r % 2]).start()

    @pl.when(step == 0)
    def _():
        start(step)

    @pl.when(step + 1 < len(refs))
    def _():
        start(step + 1)

    pltpu.make_async_copy(refs[0], held.at[step % 2], arrived.at[step % 2]).wait()
    return held[step % 2]


def normalize(hat, norm_ref, which):
    return (hat * norm_ref[which : which + 1, :] + norm_ref[which + 2 : which + 3, :]).astype(BF)


def put(r, near_ref, far_ref, value):
    @pl.when(r < 2)
    def _():
        near_ref[0] = value

    @pl.when(r >= 2)
    def _():
        far_ref[0] = value


def assemble(own_x, refs, groups, held):
    wide = sum(ref.shape[0] for ref in refs)
    relative = 0
    for ref in refs:
        block = ref.shape[2]
        for index in range(ref.shape[0]):
            x = own_x ^ relative
            for group in range(groups):
                place = (group // 2 * wide + x) * 2 + group % 2 if groups > 1 else x
                start = pl.multiple_of(place * block, block)
                held[pl.ds(start, block), :] = ref[index, group]
            relative += 1


def prepare_kernel(parts, first, last, top, wide, own_ref, *refs):
    x_refs, refs = refs[: TEAM * last], refs[TEAM * last :]
    front_refs, refs = refs[:parts], refs[parts:]
    place_ref, start_ref, query_ref, keyval_ref, *refs = refs
    *refs, held, arrived = refs
    own = own_ref[0]
    copies = [pltpu.make_async_copy(ref, held.at[i], arrived.at[i]) for i, ref in enumerate(x_refs)]
    for copy in copies:
        copy.start()
    if first:
        front_ref, norm_ref = refs
        assemble((own // 2) % wide, front_refs, TEAM, front_ref)
        norm_ref[...] = jnp.transpose(front_ref[:, 2 * WIDE :].astype(F32))[HEAD : HEAD + 8]
    else:
        front_ref, norm_ref = front_refs
        (mlp_ref,) = refs

    for copy in copies:
        copy.wait()

    @pl.loop(0, TEAM)
    def _(r):
        hat, _ = standardize(held[r, 0].astype(F32))
        made = dot(normalize(hat, norm_ref, 0), front_ref[...])
        tables = table_of(place_ref, start_ref, rank_of(own, r, top))
        keyval_ref[r] = turn(made[:, :WIDE], keys_only(tables), 1.0).astype(BF)
        for part in range(2):
            piece = made[:, WIDE * (part + 1) : WIDE * (part + 2)]
            query_ref[r, :, WIDE * part : WIDE * (part + 1)] = (turn(piece, tables, 1.0) * SCALE).astype(BF)
        if not first:
            mlp_ref[r, last - 1] = normalize(hat, norm_ref, 1)
            for index in range(1, last):
                hat, _ = standardize(held[index * TEAM + r, 0].astype(F32))
                mlp_ref[r, index - 1] = normalize(hat, norm_ref, 1)


def rank_of(own, block, top):
    return own ^ ((block % 2) * top) ^ (block // 2)


def slot_of(away, top, wide):
    return ((away // 2) % wide) * TEAM + (away // top) % 2 + 2 * (away % 2)


def load_keyval(own, top, wide, refs, keys_ref, values_ref, base):
    slots = {}
    start = 0
    for ref in refs:
        for index in range(ref.shape[0]):
            slots[start + index] = ref, index
        start += ref.shape[0]
    for away in range(start):
        ref, index = slots[(away // 2) % wide * TEAM + (away // top) % 2 + 2 * (away % 2)]
        block = ref[index]
        rows = block.shape[0]
        at = pl.ds(pl.multiple_of((own ^ away) * rows, rows), rows)
        lane = lanes((rows, WIDE))
        keys_ref[at] = jnp.where(lane < HEAD, block, base[1])
        values_ref[at] = jnp.where(lane < HEAD, base[0], block)


def forward_kernel(top, wide, own_ref, query_ref, *refs):
    kv_refs, (context_ref, marked_ref, low_ref, score_ref, peak_ref, keys_ref, values_ref) = refs[:-7], refs[-7:]
    rows = query_ref.shape[2]
    groups = 2 * MINE
    own = own_ref[0]
    step = pl.program_id(0)
    mine = own ^ (step * top)
    base = mine // 2 * 2
    lane = lanes((rows, WIDE))

    @pl.when(step == 0)
    def _():
        one = jnp.ones((rows, WIDE), BF)
        load_keyval(own, top, wide, kv_refs, keys_ref, values_ref, (one, jnp.zeros_like(one)))

    for c in range(2):
        first = query_ref[c, 0, :, :WIDE]
        at = c * MINE * rows
        low_ref[at : at + rows] = first
        low_ref[at + rows : at + 2 * rows] = pltpu.roll(first.astype(F32), HEAD, 1).astype(BF)
        low_ref[at + 2 * rows : at + 3 * rows] = query_ref[c, 0, :, WIDE:]

    count = base // 2
    key = lax.broadcasted_iota(jnp.int32, (rows, 2 * rows), 1)
    query = lax.broadcasted_iota(jnp.int32, (rows, 2 * rows), 0)
    peak_ref[...] = jnp.full(peak_ref.shape, -1e30, F32)

    @pl.loop(0, count + 1)
    def _(index):
        at = pl.ds(pl.multiple_of(index * 2 * rows, 2 * rows), 2 * rows)
        scores = dot_rt(low_ref[...], keys_ref[at])
        keeps = [key <= query + ((mine ^ c) - 2 * index) * rows for c in range(2)]
        for group in range(groups):
            at = slice(group * rows, (group + 1) * rows)
            part = jnp.where(keeps[group // MINE], scores[at], -1e30)
            score_ref[index, at] = part
            best = functools.reduce(
                jnp.maximum, [part[:, column : column + WIDE] for column in range(0, 2 * rows, WIDE)]
            )
            peak_ref[at] = jnp.maximum(peak_ref[at], best)

    peak_ref[...] = jnp.broadcast_to(jnp.max(peak_ref[...], axis=-1, keepdims=True), peak_ref.shape)

    def weigh(index, sums):
        at = pl.ds(pl.multiple_of(index * 2 * rows, 2 * rows), 2 * rows)
        peak = peak_ref[...]
        weights = jnp.exp(score_ref[index] - jnp.concatenate([peak] * (2 * rows // WIDE), axis=1))
        return sums + dot(weights.astype(BF), values_ref[at])

    sums = lax.fori_loop(0, count + 1, weigh, jnp.zeros((groups * rows, WIDE), F32))
    for c in range(2):
        made = []
        for head in range(MINE):
            at = slice((c * MINE + head) * rows, (c * MINE + head + 1) * rows)
            part = sums[at]
            swapped = pltpu.roll(part, HEAD, 1)
            total = jnp.where(lane < HEAD, part, swapped)
            made.append(jnp.where(lane < HEAD, swapped, part) / total)
            logsum = peak_ref[at] + jnp.log(total)
            marked_ref[c, 0, head] = jnp.where(
                lane < HEAD, low_ref[at], marked(lane, HEAD, three_parts(-logsum))
            )
        context_ref[c, 0, :, :WIDE] = jnp.where(lane < HEAD, made[0], made[1]).astype(BF)
        context_ref[c, 0, :, WIDE:] = jnp.where(lane < HEAD, made[2], 0.0).astype(BF)


def backward_kernel(top, wide, own_ref, query_ref, grad_ref, place_ref, start_ref, *refs):
    kv_refs, (dquery_ref, keep_ref, send_ref, sum_ref, keys_ref, values_ref, dkeyval_ref) = refs[:-7], refs[-7:]
    rows = query_ref.shape[3]
    own = own_ref[0]
    step = pl.program_id(0)
    mine = own ^ (step * top)
    base = mine // 2 * 2
    lane = lanes((rows, WIDE))
    wide_lane = lanes((2 * rows, WIDE))

    @pl.when(step == 0)
    def _():
        dkeyval_ref[...] = jnp.zeros_like(dkeyval_ref)
        ones_low = jnp.where(lane < 3, 1.0, 0.0).astype(BF)
        ones_high = jnp.where((lane >= HEAD) & (lane < HEAD + 3), 1.0, 0.0).astype(BF)
        load_keyval(own, top, wide, kv_refs, keys_ref, values_ref, (ones_low, ones_high))

    key = lax.broadcasted_iota(jnp.int32, (2 * rows, rows), 0)
    row = lax.broadcasted_iota(jnp.int32, (2 * rows, rows), 1)
    sum_ref[...] = jnp.zeros_like(sum_ref)

    @pl.loop(0, base // 2 + 1)
    def _(index):
        at = pl.ds(pl.multiple_of(index * 2 * rows, 2 * rows), 2 * rows)
        keys = keys_ref[at]
        values = values_ref[at]
        d_keys = jnp.zeros((2 * rows, WIDE), F32)
        d_values = jnp.zeros((2 * rows, WIDE), F32)
        for c in range(2):
            keep = key <= row + ((mine ^ c) - 2 * index) * rows
            for head in range(MINE):
                query = query_ref[c, 0, head]
                grad = grad_ref[c, 0, head]
                probs = jnp.where(keep, jnp.exp(dot_rt(keys, query)), 0.0)
                d_scores = (probs * dot_rt(values, grad)).astype(BF)
                d_values += dot(probs.astype(BF), grad)
                d_keys += dot(d_scores, query)
                sum_ref[c, head] += dot_lt(keys, d_scores)
        dkeyval_ref[at] += jnp.where(wide_lane < HEAD, d_keys, d_values)

    for c in range(2):
        turned = [jnp.transpose(sum_ref[c, head]) * SCALE for head in range(MINE)]
        both = jnp.where(lane < HEAD, turned[0], pltpu.roll(turned[1], HEAD, 1))
        last = jnp.where(lane < HEAD, turned[2], 0.0)
        tables = table_of(place_ref, start_ref, mine ^ c)
        dquery_ref[c, 0, :, :WIDE] = turn(both, tables, -1.0).astype(BF)
        dquery_ref[c, 0, :, WIDE:] = turn(last, tables, -1.0).astype(BF)

    @pl.when(step == pl.num_programs(0) - 1)
    def _():
        half = send_ref.shape[0]
        for rank in range(2 * half):
            slot = slot_of(rank ^ own, top, wide)
            block = dkeyval_ref[rank * rows : (rank + 1) * rows]

            @pl.when(slot < half)
            def _():
                keep_ref[jnp.minimum(slot, half - 1)] = block

            @pl.when(slot >= half)
            def _():
                send_ref[jnp.maximum(slot - half, 0)] = block.astype(BF)


def split_rows(own_x, groups, total, keep_ref, send_ref):
    wide = 2 * keep_ref.shape[0]
    block = keep_ref.shape[2]
    for side, ref in enumerate((keep_ref, send_ref)):
        half = own_x // (wide // 2) ^ side
        for index in range(wide // 2):
            x = half * (wide // 2) + index
            for group in range(groups):
                place = (group // 2 * wide + x) * 2 + group % 2 if groups > 1 else x
                start = pl.multiple_of(place * block, block)
                ref[index, group] = total[pl.ds(start, block), :].astype(ref.dtype)


def split_z(own_z, total, keep_ref, send_ref):
    wide, half, block = keep_ref.shape[:3]
    for side, ref in enumerate((keep_ref, send_ref)):
        for x in range(wide):
            for index in range(half):
                place = (x * half + index) * 2 + (own_z % 2 ^ side)
                start = pl.multiple_of(place * block, block)
                ref[x, index] = total[pl.ds(start, block), :].astype(ref.dtype)


def join_rows(own_x, own_z, refs, held):
    for side, ref in enumerate(refs):
        for away in range(ref.shape[0]):
            for index in range(ref.shape[1]):
                place = ((own_x ^ away) * ref.shape[1] + index) * 2 + (own_z % 2 ^ side)
                start = pl.multiple_of(place * ref.shape[2], ref.shape[2])
                held[pl.ds(start, ref.shape[2])] = ref[away, index]


def hidden_kernel(count, parts, down_parts, own_ref, *refs):
    grad_refs, refs = refs[:4], refs[4:]
    normed_ref, *refs = refs
    context_refs, refs = refs[:count], refs[count:]
    more_refs, refs = refs[:parts], refs[parts:]
    down_refs, refs = refs[:down_parts], refs[down_parts:]
    (made_ref, made_far_ref, dnormed_ref, marked_ref, more_keep, more_send, down_keep, down_send, *refs) = refs
    (up_sum, low_sum, held, arrived, up_ref, low_ref) = refs
    step = pl.program_id(0)
    own_x = own_ref[0]
    rows = context_refs[0].shape[1]
    units = up_ref.shape[1]

    @pl.when(step == 0)
    def _():
        low_ref[units:] = jnp.zeros_like(low_ref[units:])
        assemble(own_x, more_refs, TEAM, up_ref)
        assemble(own_x, [ref.at[:, TEAM:] for ref in more_refs], 1, low_ref.at[units:])
        if down_parts == 1:
            assemble(own_x, down_refs, 1, low_ref)
        else:
            join_rows(own_x, own_ref[1], down_refs, low_ref)

    rows = context_refs[0].shape[1]
    units = up_ref.shape[1]

    @pl.when(step == 0)
    def _():
        low_ref[units:] = jnp.zeros_like(low_ref[units:])
        assemble(own_x, more_refs, TEAM, up_ref)
        assemble(own_x, [ref.at[:, TEAM:] for ref in more_refs], 1, low_ref.at[units:])
        for side, ref in enumerate(down_refs):
            for away in range(ref.shape[0]):
                for index in range(ref.shape[1]):
                    place = ((own_x ^ away) * ref.shape[1] + index) * 2 + (own_ref[1] % 2 ^ side)
                    start = pl.multiple_of(place * ref.shape[2], ref.shape[2])
                    low_ref[pl.ds(start, ref.shape[2])] = ref[away, index]

    normed = normed_ref[0].reshape(count * rows, normed_ref.shape[-1])
    context = jnp.concatenate([ref[0] for ref in context_refs], axis=0)
    grad = fetch(grad_refs, held, arrived).reshape(normed.shape)
    raw = dot(normed, up_ref[...])
    bell = 0.5 + 0.5 * lax.erf(raw * math.sqrt(0.5))
    slope = bell + raw * (jnp.exp(raw * raw * -0.5) * (1.0 / math.sqrt(2.0 * math.pi)))
    low = jnp.concatenate([(raw * bell).astype(BF), context], axis=1)
    pulled = dot_rt(grad, low_ref[...])
    d_raw = (pulled[:, :units] * slope).astype(BF)
    made = dot(low, low_ref[...]).astype(BF)
    put(step, made_ref, made_far_ref, made.reshape(made_ref.shape[1:]))
    dnormed_ref[0] = dot_rt(d_raw, up_ref[...]).astype(BF).reshape(dnormed_ref.shape[1:])
    glow = dot_lt(low, grad)
    gup = dot_lt(normed, d_raw)

    pulled = pulled[:, units:].astype(BF)
    product = pulled.astype(F32) * context.astype(F32)
    lane = lanes((grad.shape[0], WIDE))
    for head in range(MINE):
        column = WIDE * (head // 2)
        side = (lane < HEAD) if head % 2 == 0 else (lane >= HEAD)
        delta = jnp.sum(
            jnp.where(side, product[:, column : column + WIDE], 0.0), axis=-1, keepdims=True
        )
        piece = pulled[:, column : column + WIDE]
        if head % 2 == 0:
            piece = pltpu.roll(piece.astype(F32), HEAD, 1).astype(BF)
        piece = jnp.where(
            lane >= HEAD, piece, marked(lane, 0, three_parts(jnp.broadcast_to(-delta, lane.shape)))
        )
        marked_ref[0, :, head] = piece.reshape(count, rows, WIDE)

    @pl.when(step == 0)
    def _():
        low_sum[...] = glow
        up_sum[...] = gup

    @pl.when(step > 0)
    def _():
        low_sum[...] += glow
        up_sum[...] += gup

    @pl.when(step == pl.num_programs(0) - 1)
    def _():
        split_rows(own_x, TEAM, up_sum, more_keep, more_send)
        split_rows(own_x, 1, low_sum.at[units:], more_keep.at[:, TEAM:], more_send.at[:, TEAM:])
        split_z(own_ref[1], low_sum, down_keep, down_send)


def tokens_kernel(last, top, wide, own_ref, x0_ref, x1_ref, x2_ref, x3_ref, dnormed_ref, dquery_ref, dkeyval_ref, cotangent_ref, weight_ref, norm_ref, place_ref, start_ref, *refs):
    if last:
        before_ref, nbefore_ref, dx_ref, dx_far_ref, keep_ref, send_ref, gfront_ref, gnorm_ref, held, arrived = refs
    else:
        dx_ref, dx_far_ref, gfront_ref, gnorm_ref, held, arrived = refs
    step = pl.program_id(0)
    tokens = fetch((x0_ref, x1_ref, x2_ref, x3_ref), held, arrived)
    hat, scale = standardize(tokens[0].astype(F32))
    tables = table_of(place_ref, start_ref, rank_of(own_ref[0], step, top))
    d_keyval = dkeyval_ref[0] + jnp.where(step == 0, cotangent_ref[0].astype(F32), 0.0)
    d_keyval = turn(d_keyval, keys_only(tables), -1.0).astype(BF)
    d_front = jnp.concatenate([d_keyval, dquery_ref[0]], axis=1)
    d_attn = dot_rt(d_front, weight_ref[...])
    d_mlp = dnormed_ref[0, 0].astype(F32)
    d_tokens = norm_back(hat, scale, d_attn * norm_ref[0:1, :] + d_mlp * norm_ref[1:2, :])
    put(step, dx_ref, dx_far_ref, d_tokens.astype(BF))
    sums = [
        jnp.sum(piece, axis=0, keepdims=True) for piece in (d_attn * hat, d_mlp * hat, d_attn, d_mlp)
    ]
    sums = jnp.concatenate(sums + [jnp.zeros_like(sums[0])] * 4, axis=0)
    gfront = dot_lt(normalize(hat, norm_ref, 0), d_front)

    @pl.when(step == 0)
    def _():
        gfront_ref[...] = before_ref[...] + gfront if last else gfront
        gnorm_ref[...] = nbefore_ref[...] + sums if last else sums

    @pl.when(step > 0)
    def _():
        gfront_ref[...] += gfront
        gnorm_ref[...] += sums

    if last:

        @pl.when(step == pl.num_programs(0) - 1)
        def _():
            width = gnorm_ref.shape[1]
            sums = jnp.concatenate(
                [jnp.zeros((HEAD, width), F32), gnorm_ref[...], jnp.zeros((HEAD - 8, width), F32)], axis=0
            )
            gfront_ref[:, 2 * WIDE :] += jnp.transpose(sums)
            split_rows((own_ref[0] // 2) % wide, TEAM, gfront_ref, keep_ref, send_ref)


def finish_kernel(own_ref, mine_ref, c_ref, y_ref, both_ref, query_ref, keyval_ref, gain_ref, bias_ref, turned_ref):
    mine = mine_ref[own_ref[1] * 2 + own_ref[0]]
    parts = [mine] + [ref[...].astype(F32) for ref in (c_ref, y_ref, both_ref)]
    total = parts[0] + parts[1] + parts[2] + parts[3]
    keyval_ref[...] = total[:, :WIDE]
    turned_ref[...] = jnp.zeros_like(turned_ref)
    turned_ref[: total.shape[0]] = total[:, 2 * WIDE :]
    ends = jnp.transpose(turned_ref[...])[HEAD : HEAD + 4, : total.shape[0]]
    gain_ref[...] = ends[:2]
    bias_ref[...] = ends[2:]
    for index in range(2):
        bit = own_ref[index] == 0
        parts = [jnp.where(bit, parts[place], parts[place ^ (1 << index)]) for place in range(TEAM)]
    query_ref[...] = jnp.concatenate([part[:, WIDE : WIDE + MINE * HEAD] for part in parts], axis=1)


def params(limit):
    return pltpu.CompilerParams(vmem_limit_bytes=limit * MB)


def cost(micros):
    return pl.CostEstimate(flops=int(micros * 1.1e9), bytes_accessed=0, transcendentals=0)


def struct(shape, kind):
    return jax.ShapeDtypeStruct(shape, kind)


def whole(*shape):
    return pl.BlockSpec(shape, lambda *_: (0,) * len(shape))


def on_device(nseq, ndp, inputs, w_query, w_keyval, w_out, w_up, w_down, norm_gain, norm_bias, out_cotangent, kv_cotangent):
    count, rows, width = inputs.shape
    top = nseq // 2
    wide = nseq // TEAM
    own = lax.axis_index("seq")
    own_y, own_x, own_c = own // top, (own // 2) % wide, own % 2
    own_z = lax.axis_index("dp")
    share = w_query.shape[0]
    down_share = w_down.shape[0]
    hidden = w_up.shape[1] // TEAM
    heads_wide = MINE * HEAD
    front_wide = 3 * WIDE
    slots = TEAM * wide

    def flip(value, mask, what):
        with jax.named_scope("swap_" + what):
            return lax.ppermute(value, "seq", [(i, i ^ mask) for i in range(nseq)])

    def flip_z(value, mask, what):
        with jax.named_scope("swap_" + what):
            return lax.ppermute(value, "dp", [(i, i ^ mask) for i in range(ndp)])

    def hold(*values):
        return lax.optimization_barrier(values)

    def after(value, *others):
        return hold(value, *others)[0]

    def in_order(bit, mine, other, axis):
        return jnp.where(
            bit == 0, jnp.stack([mine, other], axis), jnp.stack([other, mine], axis)
        )

    def merge(value, axis):
        return value.reshape(value.shape[:axis] + (-1,) + value.shape[axis + 2 :])

    def pick(value, index, axis):
        return lax.dynamic_index_in_dim(value, index, axis, keepdims=False)

    def swap_z(value, mask, axis, what):
        other = flip_z(value, mask, f"{what}_z{mask}")

        def join(other):
            return merge(in_order((own_z // mask) % 2, value, other, axis + 1), axis)

        return other, join

    def gather_z(value, axis, what, step=None):
        masks = [ndp >> (index + 1) for index in range(ndp.bit_length() - 1)]
        for mask in masks if step is None else masks[step]:
            other, join = swap_z(value, mask, axis, what)
            value = join(other)
        return value

    def by_place(relative, bits):
        for index, bit in enumerate(bits):
            relative = [
                jnp.where(bit == 0, relative[place], relative[place ^ (1 << index)])
                for place in range(len(relative))
            ]
        return relative

    z_bits = [(own_z >> index) % 2 for index in range(ndp.bit_length() - 1)]

    def gather_x(value, what):
        parts = [value[None]]
        mask = 1
        while mask < wide:
            sent = jnp.concatenate(parts) if mask > 1 else parts[0]
            parts.append(flip(sent, 2 * mask, f"{what}_x{mask}"))
            mask *= 2
        return parts

    def flip_x(send, what):
        return flip(send, wide, f"{what}_x{wide // 2}")

    def scatter_x(keep, got, what):
        mask = wide // 2
        while True:
            value = keep.astype(F32) + got.astype(F32)
            mask //= 2
            if mask == 0:
                return value[0]
            bit = (own_x // mask) % 2
            value = value.reshape((2, -1) + value.shape[1:])
            keep = pick(value, bit, 0)
            got = flip(pick(value, 1 - bit, 0).astype(BF), 2 * mask, f"{what}_x{mask}")

    def halve_z(value, axis, what, mask):
        bit = (own_z // mask) % 2
        value = value.reshape(value.shape[:axis] + (-1, 2) + value.shape[axis + 1 :])
        got = flip_z(pick(value, 1 - bit, axis + 1).astype(BF), mask, f"{what}_z{mask}")
        return pick(value, bit, axis + 1), got

    def add_z(pair):
        return pair[0].astype(F32) + pair[1].astype(F32)

    def finish_z(value, axis, what):
        mask = 2
        while mask < ndp:
            value = add_z(halve_z(value, axis, what, mask))
            mask *= 2
        return jnp.squeeze(value, axis)

    def moved(onward):
        pairs = []
        for rank in range(nseq):
            for z in range(ndp):
                member = 2 * (rank // top) + rank % 2
                place = ((rank // 2) % wide) * ndp + z
                pairs.append((member * (nseq * ndp // TEAM) + place, rank * ndp + z))
        return [pair if onward else pair[::-1] for pair in pairs]

    def team(value, what, first, second):
        across = flip(after(value, first), top, what + "_y")
        return [value, across, flip(value, 1, what + "_c"), flip(after(across, second), 1, what + "_yc")]

    norms = jnp.concatenate([norm_gain, norm_bias], axis=1)
    queries_of = w_query.reshape(share, 2, 2, heads_wide).transpose(1, 2, 0, 3)
    same = jnp.concatenate([w_keyval, norms], axis=1)
    ups = w_up.reshape(share, 2, wide, 2, hidden // wide).transpose(1, 3, 0, 2, 4)
    ups = ups.reshape(2, 2, share, hidden)
    pad = jnp.zeros((2, 2, share, 2 * WIDE - heads_wide - norms.shape[1]), BF)
    spread = (2, 2, share)
    pack = jnp.concatenate(
        [
            jnp.broadcast_to(same[:, :WIDE], spread + (WIDE,)),
            queries_of,
            jnp.broadcast_to(same[:, WIDE:], spread + (norms.shape[1],)),
            pad,
            ups,
        ],
        axis=3,
    )
    masks = [ndp >> (index + 1) for index in range(ndp.bit_length() - 1)]
    near_masks, far_masks = masks[-1:], masks[:-1]

    def spread_z(value, axis, what, some):
        for mask in some:
            other, join = swap_z(value, mask, axis, what)
            value = join(other)
        return value

    def begin_z(value, axis, what, some):
        if not some:
            return value, lambda value: value
        return swap_z(spread_z(value, axis, what, some[:-1]), some[-1], axis, what)

    sequences = [inputs[b : b + 1] for b in range(count)]
    got = [
        flip(pick(pick(pack, own_y ^ (d // 2), 0), own_c ^ (d % 2), 0), top * (d // 2) + d % 2, f"pack_{d}")
        for d in range(1, TEAM)
    ]
    pack, got, sequences, w_out = hold(pack, got, sequences, w_out)
    across = [flip(sequences[0], top, "tokens0_y")]
    mine = pick(pick(pack, own_y, 0), own_c, 0)
    pack = jnp.stack(by_place([mine] + got, [own_c, own_y])).reshape(2, 2, share, -1)
    tokens_c = [flip(sequences[b], 1, f"tokens{b}_c") for b in range(count)]

    front_z = pack[..., :front_wide].reshape(TEAM, share, front_wide)
    got = [flip_z(front_z, mask, f"front_z{mask}") for mask in range(1, ndp)]
    got, across[0] = hold(got, across[0])
    front_z = jnp.stack(by_place([front_z] + got, z_bits), axis=1)
    down_x = jnp.concatenate(gather_x(w_down[None], "down"))
    front_z, pack, w_out, across[0] = hold(front_z, pack, w_out, across[0])
    with jax.named_scope("swap_out_moved"):
        out_rows = lax.ppermute(w_out, ("seq", "dp"), moved(True))
    for b in range(1, count):
        across.append(flip(after(sequences[b], across[b - 1]), top, f"tokens{b}_y"))
    tokens = [[sequences[0], across[0], tokens_c[0], flip(across[0], 1, "tokens0_yc")]]
    front_parts = gather_x(front_z.reshape(TEAM, ndp * share, front_wide), "front")
    more = jnp.concatenate(
        [pack[..., front_wide:].reshape(TEAM, share, hidden), out_rows.reshape(1, share, width)]
    )
    more_got, join_more = begin_z(more[:, None], 1, "more", far_masks)
    front_parts, tokens[0] = hold(front_parts, tokens[0])
    own_rank = own.reshape(1).astype(jnp.int32)
    own_place = jnp.stack([own_x, own_z]).astype(jnp.int32)
    tables = [jnp.asarray(part) for part in angle_tables(rows, nseq)]

    def by_r(*last):
        return pl.BlockSpec((1,) + last, lambda r, *_: (r,) + (0,) * len(last))

    members = [pl.BlockSpec(memory_space=pl.ANY)] * TEAM

    def near(*last):
        return pl.BlockSpec((1,) + last, lambda r, *_: (jnp.minimum(r, 1),) + (0,) * len(last))

    def far(*last):
        return pl.BlockSpec((1,) + last, lambda r, *_: (jnp.maximum(r - 2, 0),) + (0,) * len(last))

    def call(kernel, scalar, inputs, in_specs, out_specs, out_shape, scratch, limit, micros, name, steps=TEAM):
        return pl.pallas_call(
            kernel,
            grid_spec=pltpu.PrefetchScalarGridSpec(
                num_scalar_prefetch=1,
                grid=(steps,),
                in_specs=in_specs,
                out_specs=out_specs,
                scratch_shapes=scratch,
            ),
            out_shape=out_shape,
            compiler_params=params(limit),
            cost_estimate=cost(micros),
            name=name,
        )(scalar, *inputs)

    table = by_r(rows, WIDE)
    block = [pltpu.VMEM((2, 1, rows, width), BF), pltpu.SemaphoreType.DMA((2,))]

    def prepare(b, weights):
        first = b == 0
        many = 1 if b < count - 1 else count
        held = tokens[b] + sum(tokens[: many - 1], [])
        outs = [struct((TEAM, rows, 2 * WIDE), BF), struct((TEAM, rows, WIDE), BF)]
        if first:
            outs += [struct((width, front_wide), BF), struct((8, width), F32)]
        else:
            outs += [struct((TEAM, many, rows, width), BF)]
        return call(
            functools.partial(prepare_kernel, len(weights), first, many, top, wide),
            own_rank,
            [*held, *weights, *tables],
            members * many + [whole(*part.shape) for part in [*weights, *tables]],
            [whole(*out.shape) for out in outs],
            outs,
            [pltpu.VMEM((many * TEAM, 1, rows, width), BF), pltpu.SemaphoreType.DMA((many * TEAM,))],
            16 if first else 24,
            0.5,
            "prepare",
            1,
        )

    *made_first, front, norm_rows = prepare(0, front_parts)
    prepared = [made_first]
    prepared[0], front, across[1:], more_got, down_x = hold(
        prepared[0], front, across[1:], more_got, down_x
    )
    down_got, join_down = begin_z(down_x[:, None], 1, "down", far_masks)
    for b in range(1, count):
        tokens.append([sequences[b], across[b], tokens_c[b], flip(across[b], 1, f"tokens{b}_yc")])
    more_got, join_more = begin_z(join_more(more_got), 1, "more", near_masks)
    prepared += [prepare(b, [front, norm_rows]) for b in range(1, count)]
    normed_mlp = prepared[-1][-1]
    queries, keyvals = [[part[index] for part in prepared] for index in range(2)]

    def keys_of_all(value, what):
        parts = [value]
        mask = 1
        while mask < wide:
            sent = jnp.concatenate(parts) if mask > 1 else parts[0]
            parts.append(flip(sent, 2 * mask, f"{what}_x{mask}"))
            mask *= 2
        return parts

    everyone = [keys_of_all(keyvals[b], f"keyval{b}") for b in range(count)]
    kv_specs = [whole(*part.shape) for part in everyone[0]]
    kv_scratch = [pltpu.VMEM((slots * rows, WIDE), BF)] * 2

    def by_pair(*last):
        return pl.BlockSpec((2, 1) + last, lambda y, *_: (0, y) + (0,) * len(last))

    def paired(value):
        return value.reshape((2, 2) + value.shape[1:])

    grads_y = flip(after(out_cotangent, tokens[-1][1]), top, "grads_y")
    grads_c = flip(out_cotangent, 1, "grads_c")
    everyone[0], queries, keyvals = hold(everyone[0], queries, keyvals)
    contexts = []
    marked_queries = []
    for b in range(count):
        context, marked_query = call(
            functools.partial(forward_kernel, top, wide),
            own_rank,
            [paired(queries[b]), *everyone[b]],
            [by_pair(rows, 2 * WIDE)] + kv_specs,
            [by_pair(rows, 2 * WIDE), by_pair(MINE, rows, WIDE)],
            [struct((2, 2, rows, 2 * WIDE), BF), struct((2, 2, MINE, rows, WIDE), BF)],
            [
                pltpu.VMEM((2 * MINE * rows, WIDE), BF),
                pltpu.VMEM((slots // 2, 2 * MINE * rows, 2 * rows), F32),
                pltpu.VMEM((2 * MINE * rows, WIDE), F32),
            ]
            + kv_scratch,
            7 + 7 * slots // 4,
            15,
            "attend",
            2,
        )
        context = context.reshape((TEAM,) + context.shape[2:])
        contexts.append(context)
        marked_queries.append(marked_query)
        if b == 0:
            contexts[0], everyone[1:], queries, grads_y, down_got, more_got = hold(
                contexts[0], everyone[1:], queries, grads_y, down_got, more_got
            )
            more_parts = gather_x(join_more(more_got).reshape(TEAM + 1, ndp * share, width), "more")
            down_z = join_down(down_got)
            down_got = flip_z(down_z, 1, "down_z1")
            grads = [out_cotangent, grads_y, grads_c, flip(grads_y, 1, "grads_yc")]
    contexts, grads, more_parts, down_got = hold(contexts, grads, more_parts, down_got)
    if down_share % 16:
        down_parts = [in_order(own_z % 2, down_z, down_got, 2).reshape(wide, 1, ndp * down_share, width)]
    else:
        down_parts = [part.reshape(wide, ndp // 2, down_share, width) for part in (down_z, down_got)]

    half = max(wide // 2, 1)
    more_half = (half, TEAM + 1, ndp * share, width)
    down_half = (wide, ndp // 2, down_share, width)
    made, made_far, d_normed, marked_grad, more_keep, more_send, down_keep, down_send = call(
        functools.partial(hidden_kernel, count, len(more_parts), len(down_parts)),
        own_place,
        [*grads, normed_mlp, *contexts, *more_parts, *down_parts],
        members
        + [by_r(count, rows, width)]
        + [by_r(rows, 2 * WIDE)] * count
        + [whole(*part.shape) for part in more_parts + down_parts],
        [
            near(count, rows, width),
            far(count, rows, width),
            by_r(count, rows, width),
            by_r(count, MINE, rows, WIDE),
            whole(*more_half),
            whole(*more_half),
            whole(*down_half),
            whole(*down_half),
        ],
        [
            struct((2, count, rows, width), BF),
            struct((2, count, rows, width), BF),
            struct((TEAM, count, rows, width), BF),
            struct((TEAM, count, MINE, rows, WIDE), BF),
            struct(more_half, BF),
            struct(more_half, BF),
            struct(down_half, BF),
            struct(down_half, BF),
        ],
        [
            pltpu.VMEM((width, hidden), F32),
            pltpu.VMEM((hidden + 2 * WIDE, width), F32),
            pltpu.VMEM((2, count, rows, width), BF),
            pltpu.SemaphoreType.DMA((2,)),
            pltpu.VMEM((width, hidden), BF),
            pltpu.VMEM((hidden + 2 * WIDE, width), BF),
        ],
        36,
        27,
        "hidden",
    )

    def sum_c(value, what, *others):
        return value[0].astype(F32) + after(flip(value[1], 1, what + "_c"), *others).astype(F32)

    def sum_y(value, what, *others):
        got = flip(value[1].astype(BF), top, what + "_y")
        return value[0] + after(got, *others).astype(F32)

    d_queries = []
    kept = []
    sent = []
    key_half = (slots // 2, rows, WIDE)
    for b in range(count):
        d_query, keep, send = call(
            functools.partial(backward_kernel, top, wide),
            own_rank,
            [marked_queries[b], paired(marked_grad), *tables, *everyone[b]],
            [
                by_pair(MINE, rows, WIDE),
                pl.BlockSpec((2, 1, None, MINE, rows, WIDE), lambda y, *_, b=b: (0, y, b, 0, 0, 0)),
            ]
            + [whole(*part.shape) for part in tables]
            + kv_specs,
            [by_pair(rows, 2 * WIDE), whole(*key_half), whole(*key_half)],
            [struct((2, 2, rows, 2 * WIDE), BF), struct(key_half, F32), struct(key_half, BF)],
            [pltpu.VMEM((2, MINE, WIDE, rows), F32)]
            + kv_scratch
            + [pltpu.VMEM((slots * rows, WIDE), F32)],
            16,
            20,
            "attend_back",
            2,
        )
        d_query = d_query.reshape((TEAM,) + d_query.shape[2:])
        d_queries.append(d_query)
        kept.append(keep)
        sent.append(send)
        if b == 0:
            got_c = flip(made_far, 1, "made_c")
            got_x = flip_x(more_send, "gmore")
            down_got = flip_z(down_send, 1, "gdown_z1")
            (d_queries, kept, sent, marked_grad, made, got_c, more_keep, got_x, down_keep, down_got) = hold(
                d_queries, kept, sent, marked_grad, made, got_c, more_keep, got_x, down_keep, down_got
            )
            made = made.astype(F32) + got_c.astype(F32)
            more_grads = scatter_x(more_keep, got_x, "gmore").reshape(TEAM + 1, ndp, share, width)
            got_y = flip(made[1].astype(BF), top, "made_y")
            more_z = halve_z(more_grads, 1, "gmore", 1)
            keys_got = flip_x(sent[0], "gkeyval0")
            down_grads = down_keep.astype(F32) + down_got.astype(F32)
            mask = 2
            while mask < ndp:
                down_z = halve_z(down_grads, 1, "gdown", mask)
                down_grads = add_z(down_z) if 2 * mask < ndp else down_grads
                mask *= 2
    (d_queries, kept, sent, made, got_y, more_z, keys_got) = hold(
        d_queries, kept, sent, made, got_y, more_z, keys_got
    )
    output = (inputs.astype(F32) + made[0] + got_y.astype(F32)).astype(BF)
    more_grads = add_z(more_z)
    keys_gots = [keys_got] + [flip_x(sent[b], f"gkeyval{b}") for b in range(1, count)]

    def keys_back(b):
        keep, got = kept[b], keys_gots[b]
        mask = wide // 2
        while True:
            value = keep + got.astype(F32)
            mask //= 2
            if mask == 0:
                return value
            keep = value[: value.shape[0] // 2]
            got = flip(value[value.shape[0] // 2 :].astype(BF), 2 * mask, f"gkeyval{b}_x{mask}")

    def join_c(value, got):
        mine = pick(value.reshape((2, 2) + value.shape[1:]), own_c, 1)
        got = got.astype(F32)
        return jnp.where(own_c == 0, mine, got), jnp.where(own_c == 0, got, mine)

    def join_y(value, got):
        mine = pick(value, own_y, 0)
        got = got.astype(F32)
        return jnp.where(own_y == 0, mine, got), jnp.where(own_y == 0, got, mine)

    pulled = []
    carried = []
    front_half = (half, TEAM, ndp * share, front_wide)
    for b in range(count):
        last = b == count - 1
        outs = [struct((2, rows, width), BF), struct((2, rows, width), BF)]
        out_specs = [near(rows, width), far(rows, width)]
        sums = [struct((width, front_wide), F32), struct((8, width), F32)]
        if last:
            outs += [struct(front_half, F32), struct(front_half, BF)]
        else:
            outs += sums
        d_tokens, d_tokens_far, *carried = call(
            functools.partial(tokens_kernel, last, top, wide),
            own_rank,
            [
                *tokens[b],
                d_normed,
                d_queries[b],
                keys_back(b),
                kv_cotangent,
                front,
                norm_rows,
                *tables,
                *carried,
            ],
            members
            + [
                pl.BlockSpec((1, 1, rows, width), lambda r, *_, b=b: (r, b, 0, 0)),
                by_r(rows, 2 * WIDE),
                table,
                pl.BlockSpec((1, rows, WIDE), lambda r, *_, b=b: (b, 0, 0)),
                whole(width, front_wide),
                whole(8, width),
            ]
            + [whole(*part.shape) for part in tables]
            + [whole(*part.shape) for part in carried],
            out_specs + [whole(*out.shape) for out in outs[2:]],
            outs,
            ([pltpu.VMEM(out.shape, F32) for out in sums] if last else []) + block,
            14,
            7,
            "pull_tokens",
        )
        pulled.append((d_tokens, d_tokens_far))
        if b == 0:
            mask = 2
            while mask < ndp:
                more_z = halve_z(more_grads, 1, "gmore", mask)
                more_grads = add_z(more_z) if 2 * mask < ndp else more_grads
                mask *= 2
            (carried, pulled, down_z, more_z, keys_gots, kept, d_queries) = hold(
                carried, pulled, down_z, more_z, keys_gots, kept, d_queries
            )
            more_grads = jnp.squeeze(add_z(more_z), 1)
            ups_c = flip(
                pick(more_grads[:TEAM].reshape(2, 2, share, hidden), 1 - own_c, 1).astype(BF), 1, "gup_c"
            )
            got_c = flip(pulled[0][1], 1, "dtokens0_c")
            down_grads = jnp.squeeze(add_z(down_z), 1)
            x_half = down_grads.reshape((2, -1) + down_grads.shape[1:])
            x_bit = own_x // (wide // 2)
            down_keep = pick(x_half, x_bit, 0)
            down_got = flip_x(pick(x_half, 1 - x_bit, 0).astype(BF), "gdown")
    front_keep, front_send = carried
    front_keep, front_send, pulled, got_c, ups_c = hold(front_keep, front_send, pulled, got_c, ups_c)
    ups = jnp.concatenate(join_c(more_grads[:TEAM], ups_c), axis=-1)
    ups_y = flip(pick(ups, 1 - own_y, 0).astype(BF), top, "gup_y")
    down_grads = scatter_x(down_keep, down_got, "gdown")

    def add_c(pair, got):
        return pair[0].astype(F32) + got.astype(F32)

    front_got = flip_x(front_send, "gfront")
    halves = [add_c(pulled[0], got_c)]
    got_y = flip(halves[0][1].astype(BF), top, "dtokens0_y")
    gots_c = [flip(pulled[b][1], 1, f"dtokens{b}_c") for b in range(1, count)]
    front_keep, front_got, gots_c, more_grads = hold(front_keep, front_got, gots_c, more_grads)
    with jax.named_scope("swap_gout_moved"):
        grad_out = lax.ppermute(more_grads[TEAM].astype(BF), ("seq", "dp"), moved(False)).astype(F32)
    halves += [add_c(pulled[b], gots_c[b - 1]) for b in range(1, count)]
    front_grads = scatter_x(front_keep, front_got, "gfront").reshape(TEAM, ndp, share, front_wide)
    mine = pick(front_grads, own_z, 1)
    got = [
        flip_z(pick(front_grads, own_z ^ mask, 1).astype(BF), mask, f"gfront_z{mask}")
        for mask in range(1, ndp)
    ]
    gots_y = [got_y] + [
        flip(halves[b][1].astype(BF), top, f"dtokens{b}_y") for b in range(1, count)
    ]
    mine, got, halves, ups, ups_y, gots_y = hold(mine, got, halves, ups, ups_y, gots_y)
    front_grads = sum([part.astype(F32) for part in got], mine).reshape(2, 2, share, front_wide)

    piece = hidden // wide
    ups = join_y(ups, ups_y)
    grad_up = jnp.concatenate(
        [
            ups[y][:, hidden * c + piece * x : hidden * c + piece * (x + 1)]
            for y in range(2)
            for x in range(wide)
            for c in range(2)
        ],
        axis=-1,
    )
    got = [
        flip(
            pick(pick(front_grads, own_y ^ (d // 2), 0), own_c ^ (d % 2), 0).astype(BF),
            top * (d // 2) + d % 2,
            f"gfront_{d}",
        )
        for d in range(1, TEAM)
    ]
    mine = front_grads.reshape(TEAM, share, front_wide)
    d_rows = [halves[b][0] + gots_y[b].astype(F32) for b in range(count)]
    grad_inputs = out_cotangent.astype(F32) + jnp.stack(d_rows)
    mine, got, grad_inputs, grad_up, grad_out = hold(mine, got, grad_inputs, grad_up, grad_out)
    grad_query, grad_keyval, grad_gain, grad_bias = pl.pallas_call(
        finish_kernel,
        in_specs=[pl.BlockSpec(memory_space=pltpu.SMEM), whole(TEAM, share, front_wide)]
        + [whole(share, front_wide)] * (TEAM - 1),
        out_specs=[whole(share, TEAM * heads_wide), whole(share, WIDE), whole(2, share), whole(2, share)],
        out_shape=[
            struct((share, TEAM * heads_wide), F32),
            struct((share, WIDE), F32),
            struct((2, share), F32),
            struct((2, share), F32),
        ],
        scratch_shapes=[pltpu.VMEM((WIDE, WIDE), F32)],
        compiler_params=params(60),
        cost_estimate=cost(1),
        name="finish",
    )(jnp.stack([own_c, own_y]).astype(jnp.int32), mine, *got)
    return (
        output,
        jnp.stack([part[0] for part in keyvals]),
        grad_inputs,
        grad_query,
        grad_keyval,
        grad_out,
        grad_up,
        down_grads,
        grad_gain.T,
        grad_bias.T,
    )


def solution(mesh):
    rows = P("dp", "seq", None)
    split = P(("seq", "dp"), None)
    return jax.shard_map(
        functools.partial(on_device, mesh.shape["seq"], mesh.shape["dp"]),
        mesh=mesh,
        in_specs=(rows,) + (split,) * 7 + (rows, rows),
        out_specs=(rows,) * 3 + (split,) * 7,
        check_vma=False,
    )
```

```python
import functools
import math

import jax
import jax.numpy as jnp
import numpy as np
from jax import lax
from jax.experimental import pallas as pl
from jax.experimental.pallas import tpu as pltpu
from jax.sharding import PartitionSpec as P

HEADS = 12
HEAD = 64
ROT = 16
TEAM = 4
MINE = HEADS // TEAM
WIDE = 2 * HEAD
EPSILON = 1e-05
BF = jnp.bfloat16
F32 = jnp.float32
SCALE = 1.0 / math.sqrt(HEAD)
MB = 1 << 20


def dot(left, right):
    return lax.dot_general(left, right, (((1,), (0,)), ((), ())), preferred_element_type=F32)


def dot_rt(left, right):
    return lax.dot_general(left, right, (((1,), (1,)), ((), ())), preferred_element_type=F32)


def dot_lt(left, right):
    return lax.dot_general(left, right, (((0,), (0,)), ((), ())), preferred_element_type=F32)


def lanes(shape):
    return lax.broadcasted_iota(jnp.int32, shape, len(shape) - 1)


def angle_tables(rows, count):
    lane = np.arange(WIDE) % HEAD
    frequency = np.exp(-math.log(10000.0) * (lane % (ROT // 2)) * (2.0 / ROT)) * (lane < ROT)
    sign = np.where(lane < ROT // 2, -1.0, 1.0)
    out = []
    for positions in (np.arange(rows), np.arange(count) * rows):
        angles = 0.25 * positions[:, None] * frequency
        out.append(np.stack([np.cos(angles), sign * np.sin(angles)]).astype(np.float32))
    return out


def table_of(place_ref, start_ref, rank):
    cos_row, sin_row = place_ref[0], place_ref[1]
    cos_start, sin_start = start_ref[0, pl.ds(rank, 1)], start_ref[1, pl.ds(rank, 1)]
    return cos_row * cos_start - sin_row * sin_start, sin_row * cos_start + cos_row * sin_start


def keys_only(tables):
    keys_side = lanes(tables[0].shape) < HEAD
    return jnp.where(keys_side, tables[0], 1.0), jnp.where(keys_side, tables[1], 0.0)


def turn(values, tables, sign):
    near = (lanes(values.shape) % HEAD) < ROT // 2
    swapped = jnp.where(
        near, pltpu.roll(values, WIDE - ROT // 2, 1), pltpu.roll(values, ROT // 2, 1)
    )
    return values * tables[0] + (sign * swapped) * tables[1]


def standardize(tokens):
    center = tokens - jnp.mean(tokens, axis=-1, keepdims=True)
    spread = jnp.mean(center * center, axis=-1, keepdims=True)
    scale = lax.rsqrt(spread + EPSILON)
    return center * scale, scale


def norm_back(hat, scale, pulled):
    return scale * (
        pulled
        - jnp.mean(pulled, axis=-1, keepdims=True)
        - hat * jnp.mean(pulled * hat, axis=-1, keepdims=True)
    )


def three_parts(column):
    high = column.astype(BF)
    rest = column - high.astype(F32)
    mid = rest.astype(BF)
    low = (rest - mid.astype(F32)).astype(BF)
    return high, mid, low


def marked(lane, base, parts):
    out = jnp.zeros(lane.shape, BF)
    for index, part in enumerate(parts):
        out = jnp.where(lane == base + index, part, out)
    return out


def fetch(refs, held, arrived):
    step = pl.program_id(0)

    def start(r):
        for index, ref in enumerate(refs):

            @pl.when(r == index)
            def _(ref=ref):
                pltpu.make_async_copy(ref, held.at[r % 2], arrived.at[r % 2]).start()

    @pl.when(step == 0)
    def _():
        start(step)

    @pl.when(step + 1 < len(refs))
    def _():
        start(step + 1)

    pltpu.make_async_copy(refs[0], held.at[step % 2], arrived.at[step % 2]).wait()
    return held[step % 2]


def normalize(hat, norm_ref, which):
    return (hat * norm_ref[which : which + 1, :] + norm_ref[which + 2 : which + 3, :]).astype(BF)


def put(r, near_ref, far_ref, value):
    @pl.when(r < 2)
    def _():
        near_ref[0] = value

    @pl.when(r >= 2)
    def _():
        far_ref[0] = value


def assemble(own_x, refs, groups, held):
    wide = sum(ref.shape[0] for ref in refs)
    relative = 0
    for ref in refs:
        block = ref.shape[2]
        for index in range(ref.shape[0]):
            x = own_x ^ relative
            for group in range(groups):
                place = (group // 2 * wide + x) * 2 + group % 2 if groups > 1 else x
                start = pl.multiple_of(place * block, block)
                held[pl.ds(start, block), :] = ref[index, group]
            relative += 1


def prepare_kernel(parts, first, last, top, wide, own_ref, *refs):
    x_refs, refs = refs[: TEAM * last], refs[TEAM * last :]
    front_refs, refs = refs[:parts], refs[parts:]
    place_ref, start_ref, query_ref, keyval_ref, *refs = refs
    *refs, held, arrived = refs
    own = own_ref[0]
    copies = [pltpu.make_async_copy(ref, held.at[i], arrived.at[i]) for i, ref in enumerate(x_refs)]
    for copy in copies:
        copy.start()
    if first:
        front_ref, norm_ref = refs
        assemble((own // 2) % wide, front_refs, TEAM, front_ref)
        norm_ref[...] = jnp.transpose(front_ref[:, 2 * WIDE :].astype(F32))[HEAD : HEAD + 8]
    else:
        front_ref, norm_ref = front_refs
        (mlp_ref,) = refs

    for copy in copies:
        copy.wait()

    @pl.loop(0, TEAM)
    def _(r):
        hat, _ = standardize(held[r, 0].astype(F32))
        made = dot(normalize(hat, norm_ref, 0), front_ref[...])
        tables = table_of(place_ref, start_ref, rank_of(own, r, top))
        keyval_ref[r] = turn(made[:, :WIDE], keys_only(tables), 1.0).astype(BF)
        for part in range(2):
            piece = made[:, WIDE * (part + 1) : WIDE * (part + 2)]
            query_ref[r, :, WIDE * part : WIDE * (part + 1)] = (turn(piece, tables, 1.0) * SCALE).astype(BF)
        if not first:
            mlp_ref[r, last - 1] = normalize(hat, norm_ref, 1)
            for index in range(1, last):
                hat, _ = standardize(held[index * TEAM + r, 0].astype(F32))
                mlp_ref[r, index - 1] = normalize(hat, norm_ref, 1)


def rank_of(own, block, top):
    return own ^ ((block % 2) * top) ^ (block // 2)


def slot_of(away, top, wide):
    return ((away // 2) % wide) * TEAM + (away // top) % 2 + 2 * (away % 2)


def load_keyval(own, top, wide, refs, keys_ref, values_ref, base):
    slots = {}
    start = 0
    for ref in refs:
        for index in range(ref.shape[0]):
            slots[start + index] = ref, index
        start += ref.shape[0]
    for away in range(start):
        ref, index = slots[(away // 2) % wide * TEAM + (away // top) % 2 + 2 * (away % 2)]
        block = ref[index]
        rows = block.shape[0]
        at = pl.ds(pl.multiple_of((own ^ away) * rows, rows), rows)
        lane = lanes((rows, WIDE))
        keys_ref[at] = jnp.where(lane < HEAD, block, base[1])
        values_ref[at] = jnp.where(lane < HEAD, base[0], block)


def forward_kernel(top, wide, own_ref, query_ref, *refs):
    kv_refs, (context_ref, marked_ref, low_ref, score_ref, peak_ref, keys_ref, values_ref) = refs[:-7], refs[-7:]
    rows = query_ref.shape[2]
    groups = 2 * MINE
    own = own_ref[0]
    step = pl.program_id(0)
    mine = own ^ (step * top)
    base = mine // 2 * 2
    lane = lanes((rows, WIDE))

    @pl.when(step == 0)
    def _():
        one = jnp.ones((rows, WIDE), BF)
        load_keyval(own, top, wide, kv_refs, keys_ref, values_ref, (one, jnp.zeros_like(one)))

    for c in range(2):
        first = query_ref[c, 0, :, :WIDE]
        at = c * MINE * rows
        low_ref[at : at + rows] = first
        low_ref[at + rows : at + 2 * rows] = pltpu.roll(first.astype(F32), HEAD, 1).astype(BF)
        low_ref[at + 2 * rows : at + 3 * rows] = query_ref[c, 0, :, WIDE:]

    count = base // 2
    key = lax.broadcasted_iota(jnp.int32, (rows, 2 * rows), 1)
    query = lax.broadcasted_iota(jnp.int32, (rows, 2 * rows), 0)
    peak_ref[...] = jnp.full(peak_ref.shape, -1e30, F32)

    @pl.loop(0, count + 1)
    def _(index):
        at = pl.ds(pl.multiple_of(index * 2 * rows, 2 * rows), 2 * rows)
        scores = dot_rt(low_ref[...], keys_ref[at])
        keeps = [key <= query + ((mine ^ c) - 2 * index) * rows for c in range(2)]
        for group in range(groups):
            at = slice(group * rows, (group + 1) * rows)
            part = jnp.where(keeps[group // MINE], scores[at], -1e30)
            score_ref[index, at] = part
            best = functools.reduce(
                jnp.maximum, [part[:, column : column + WIDE] for column in range(0, 2 * rows, WIDE)]
            )
            peak_ref[at] = jnp.maximum(peak_ref[at], best)

    peak_ref[...] = jnp.broadcast_to(jnp.max(peak_ref[...], axis=-1, keepdims=True), peak_ref.shape)

    def weigh(index, sums):
        at = pl.ds(pl.multiple_of(index * 2 * rows, 2 * rows), 2 * rows)
        peak = peak_ref[...]
        weights = jnp.exp(score_ref[index] - jnp.concatenate([peak] * (2 * rows // WIDE), axis=1))
        return sums + dot(weights.astype(BF), values_ref[at])

    sums = lax.fori_loop(0, count + 1, weigh, jnp.zeros((groups * rows, WIDE), F32))
    for c in range(2):
        made = []
        for head in range(MINE):
            at = slice((c * MINE + head) * rows, (c * MINE + head + 1) * rows)
            part = sums[at]
            swapped = pltpu.roll(part, HEAD, 1)
            total = jnp.where(lane < HEAD, part, swapped)
            made.append(jnp.where(lane < HEAD, swapped, part) / total)
            logsum = peak_ref[at] + jnp.log(total)
            marked_ref[c, 0, head] = jnp.where(
                lane < HEAD, low_ref[at], marked(lane, HEAD, three_parts(-logsum))
            )
        context_ref[c, 0, :, :WIDE] = jnp.where(lane < HEAD, made[0], made[1]).astype(BF)
        context_ref[c, 0, :, WIDE:] = jnp.where(lane < HEAD, made[2], 0.0).astype(BF)


def backward_kernel(top, wide, own_ref, query_ref, grad_ref, place_ref, start_ref, *refs):
    kv_refs, (dquery_ref, keep_ref, send_ref, sum_ref, keys_ref, values_ref, dkeyval_ref) = refs[:-7], refs[-7:]
    rows = query_ref.shape[3]
    own = own_ref[0]
    step = pl.program_id(0)
    mine = own ^ (step * top)
    base = mine // 2 * 2
    lane = lanes((rows, WIDE))
    wide_lane = lanes((2 * rows, WIDE))

    @pl.when(step == 0)
    def _():
        dkeyval_ref[...] = jnp.zeros_like(dkeyval_ref)
        ones_low = jnp.where(lane < 3, 1.0, 0.0).astype(BF)
        ones_high = jnp.where((lane >= HEAD) & (lane < HEAD + 3), 1.0, 0.0).astype(BF)
        load_keyval(own, top, wide, kv_refs, keys_ref, values_ref, (ones_low, ones_high))

    key = lax.broadcasted_iota(jnp.int32, (2 * rows, rows), 0)
    row = lax.broadcasted_iota(jnp.int32, (2 * rows, rows), 1)
    sum_ref[...] = jnp.zeros_like(sum_ref)

    @pl.loop(0, base // 2 + 1)
    def _(index):
        at = pl.ds(pl.multiple_of(index * 2 * rows, 2 * rows), 2 * rows)
        keys = keys_ref[at]
        values = values_ref[at]
        d_keys = jnp.zeros((2 * rows, WIDE), F32)
        d_values = jnp.zeros((2 * rows, WIDE), F32)
        for c in range(2):
            keep = key <= row + ((mine ^ c) - 2 * index) * rows
            for head in range(MINE):
                query = query_ref[c, 0, head]
                grad = grad_ref[c, 0, head]
                probs = jnp.where(keep, jnp.exp(dot_rt(keys, query)), 0.0)
                d_scores = (probs * dot_rt(values, grad)).astype(BF)
                d_values += dot(probs.astype(BF), grad)
                d_keys += dot(d_scores, query)
                sum_ref[c, head] += dot_lt(keys, d_scores)
        dkeyval_ref[at] += jnp.where(wide_lane < HEAD, d_keys, d_values)

    for c in range(2):
        turned = [jnp.transpose(sum_ref[c, head]) * SCALE for head in range(MINE)]
        both = jnp.where(lane < HEAD, turned[0], pltpu.roll(turned[1], HEAD, 1))
        last = jnp.where(lane < HEAD, turned[2], 0.0)
        tables = table_of(place_ref, start_ref, mine ^ c)
        dquery_ref[c, 0, :, :WIDE] = turn(both, tables, -1.0).astype(BF)
        dquery_ref[c, 0, :, WIDE:] = turn(last, tables, -1.0).astype(BF)

    @pl.when(step == pl.num_programs(0) - 1)
    def _():
        half = send_ref.shape[0]
        for rank in range(2 * half):
            slot = slot_of(rank ^ own, top, wide)
            block = dkeyval_ref[rank * rows : (rank + 1) * rows]

            @pl.when(slot < half)
            def _():
                keep_ref[jnp.minimum(slot, half - 1)] = block

            @pl.when(slot >= half)
            def _():
                send_ref[jnp.maximum(slot - half, 0)] = block.astype(BF)


def split_rows(own_x, groups, total, keep_ref, send_ref):
    wide = 2 * keep_ref.shape[0]
    block = keep_ref.shape[2]
    for side, ref in enumerate((keep_ref, send_ref)):
        half = own_x // (wide // 2) ^ side
        for index in range(wide // 2):
            x = half * (wide // 2) + index
            for group in range(groups):
                place = (group // 2 * wide + x) * 2 + group % 2 if groups > 1 else x
                start = pl.multiple_of(place * block, block)
                ref[index, group] = total[pl.ds(start, block), :].astype(ref.dtype)


def split_z(own_z, total, keep_ref, send_ref):
    wide, half, block = keep_ref.shape[:3]
    for side, ref in enumerate((keep_ref, send_ref)):
        for x in range(wide):
            for index in range(half):
                place = (x * half + index) * 2 + (own_z % 2 ^ side)
                start = pl.multiple_of(place * block, block)
                ref[x, index] = total[pl.ds(start, block), :].astype(ref.dtype)


def join_rows(own_x, own_z, refs, held):
    for side, ref in enumerate(refs):
        for away in range(ref.shape[0]):
            for index in range(ref.shape[1]):
                place = ((own_x ^ away) * ref.shape[1] + index) * 2 + (own_z % 2 ^ side)
                start = pl.multiple_of(place * ref.shape[2], ref.shape[2])
                held[pl.ds(start, ref.shape[2])] = ref[away, index]


def hidden_kernel(count, parts, down_parts, own_ref, *refs):
    grad_refs, refs = refs[:4], refs[4:]
    normed_ref, *refs = refs
    context_refs, refs = refs[:count], refs[count:]
    more_refs, refs = refs[:parts], refs[parts:]
    down_refs, refs = refs[:down_parts], refs[down_parts:]
    (made_ref, made_far_ref, dnormed_ref, marked_ref, more_keep, more_send, down_keep, down_send, *refs) = refs
    (up_sum, low_sum, held, arrived, up_ref, low_ref) = refs
    step = pl.program_id(0)
    own_x = own_ref[0]
    rows = context_refs[0].shape[1]
    units = up_ref.shape[1]

    @pl.when(step == 0)
    def _():
        low_ref[units:] = jnp.zeros_like(low_ref[units:])
        assemble(own_x, more_refs, TEAM, up_ref)
        assemble(own_x, [ref.at[:, TEAM:] for ref in more_refs], 1, low_ref.at[units:])
        if down_parts == 1:
            assemble(own_x, down_refs, 1, low_ref)
        else:
            join_rows(own_x, own_ref[1], down_refs, low_ref)

    rows = context_refs[0].shape[1]
    units = up_ref.shape[1]

    @pl.when(step == 0)
    def _():
        low_ref[units:] = jnp.zeros_like(low_ref[units:])
        assemble(own_x, more_refs, TEAM, up_ref)
        assemble(own_x, [ref.at[:, TEAM:] for ref in more_refs], 1, low_ref.at[units:])
        for side, ref in enumerate(down_refs):
            for away in range(ref.shape[0]):
                for index in range(ref.shape[1]):
                    place = ((own_x ^ away) * ref.shape[1] + index) * 2 + (own_ref[1] % 2 ^ side)
                    start = pl.multiple_of(place * ref.shape[2], ref.shape[2])
                    low_ref[pl.ds(start, ref.shape[2])] = ref[away, index]

    normed = normed_ref[0].reshape(count * rows, normed_ref.shape[-1])
    context = jnp.concatenate([ref[0] for ref in context_refs], axis=0)
    grad = fetch(grad_refs, held, arrived).reshape(normed.shape)
    raw = dot(normed, up_ref[...])
    bell = 0.5 + 0.5 * lax.erf(raw * math.sqrt(0.5))
    slope = bell + raw * (jnp.exp(raw * raw * -0.5) * (1.0 / math.sqrt(2.0 * math.pi)))
    low = jnp.concatenate([(raw * bell).astype(BF), context], axis=1)
    pulled = dot_rt(grad, low_ref[...])
    d_raw = (pulled[:, :units] * slope).astype(BF)
    made = dot(low, low_ref[...]).astype(BF)
    put(step, made_ref, made_far_ref, made.reshape(made_ref.shape[1:]))
    dnormed_ref[0] = dot_rt(d_raw, up_ref[...]).astype(BF).reshape(dnormed_ref.shape[1:])
    glow = dot_lt(low, grad)
    gup = dot_lt(normed, d_raw)

    pulled = pulled[:, units:].astype(BF)
    product = pulled.astype(F32) * context.astype(F32)
    lane = lanes((grad.shape[0], WIDE))
    for head in range(MINE):
        column = WIDE * (head // 2)
        side = (lane < HEAD) if head % 2 == 0 else (lane >= HEAD)
        delta = jnp.sum(
            jnp.where(side, product[:, column : column + WIDE], 0.0), axis=-1, keepdims=True
        )
        piece = pulled[:, column : column + WIDE]
        if head % 2 == 0:
            piece = pltpu.roll(piece.astype(F32), HEAD, 1).astype(BF)
        piece = jnp.where(
            lane >= HEAD, piece, marked(lane, 0, three_parts(jnp.broadcast_to(-delta, lane.shape)))
        )
        marked_ref[0, :, head] = piece.reshape(count, rows, WIDE)

    @pl.when(step == 0)
    def _():
        low_sum[...] = glow
        up_sum[...] = gup

    @pl.when(step > 0)
    def _():
        low_sum[...] += glow
        up_sum[...] += gup

    @pl.when(step == pl.num_programs(0) - 1)
    def _():
        split_rows(own_x, TEAM, up_sum, more_keep, more_send)
        split_rows(own_x, 1, low_sum.at[units:], more_keep.at[:, TEAM:], more_send.at[:, TEAM:])
        split_z(own_ref[1], low_sum, down_keep, down_send)


def tokens_kernel(last, top, wide, own_ref, x0_ref, x1_ref, x2_ref, x3_ref, dnormed_ref, dquery_ref, dkeyval_ref, cotangent_ref, weight_ref, norm_ref, place_ref, start_ref, *refs):
    if last:
        before_ref, nbefore_ref, dx_ref, dx_far_ref, keep_ref, send_ref, gfront_ref, gnorm_ref, held, arrived = refs
    else:
        dx_ref, dx_far_ref, gfront_ref, gnorm_ref, held, arrived = refs
    step = pl.program_id(0)
    tokens = fetch((x0_ref, x1_ref, x2_ref, x3_ref), held, arrived)
    hat, scale = standardize(tokens[0].astype(F32))
    tables = table_of(place_ref, start_ref, rank_of(own_ref[0], step, top))
    d_keyval = dkeyval_ref[0] + jnp.where(step == 0, cotangent_ref[0].astype(F32), 0.0)
    d_keyval = turn(d_keyval, keys_only(tables), -1.0).astype(BF)
    d_front = jnp.concatenate([d_keyval, dquery_ref[0]], axis=1)
    d_attn = dot_rt(d_front, weight_ref[...])
    d_mlp = dnormed_ref[0, 0].astype(F32)
    d_tokens = norm_back(hat, scale, d_attn * norm_ref[0:1, :] + d_mlp * norm_ref[1:2, :])
    put(step, dx_ref, dx_far_ref, d_tokens.astype(BF))
    sums = [
        jnp.sum(piece, axis=0, keepdims=True) for piece in (d_attn * hat, d_mlp * hat, d_attn, d_mlp)
    ]
    sums = jnp.concatenate(sums + [jnp.zeros_like(sums[0])] * 4, axis=0)
    gfront = dot_lt(normalize(hat, norm_ref, 0), d_front)

    @pl.when(step == 0)
    def _():
        gfront_ref[...] = before_ref[...] + gfront if last else gfront
        gnorm_ref[...] = nbefore_ref[...] + sums if last else sums

    @pl.when(step > 0)
    def _():
        gfront_ref[...] += gfront
        gnorm_ref[...] += sums

    if last:

        @pl.when(step == pl.num_programs(0) - 1)
        def _():
            width = gnorm_ref.shape[1]
            sums = jnp.concatenate(
                [jnp.zeros((HEAD, width), F32), gnorm_ref[...], jnp.zeros((HEAD - 8, width), F32)], axis=0
            )
            gfront_ref[:, 2 * WIDE :] += jnp.transpose(sums)
            split_rows((own_ref[0] // 2) % wide, TEAM, gfront_ref, keep_ref, send_ref)


def finish_kernel(own_ref, mine_ref, c_ref, y_ref, both_ref, query_ref, keyval_ref, gain_ref, bias_ref, turned_ref):
    mine = mine_ref[own_ref[1] * 2 + own_ref[0]]
    parts = [mine] + [ref[...].astype(F32) for ref in (c_ref, y_ref, both_ref)]
    total = parts[0] + parts[1] + parts[2] + parts[3]
    keyval_ref[...] = total[:, :WIDE]
    turned_ref[...] = jnp.zeros_like(turned_ref)
    turned_ref[: total.shape[0]] = total[:, 2 * WIDE :]
    ends = jnp.transpose(turned_ref[...])[HEAD : HEAD + 4, : total.shape[0]]
    gain_ref[...] = ends[:2]
    bias_ref[...] = ends[2:]
    for index in range(2):
        bit = own_ref[index] == 0
        parts = [jnp.where(bit, parts[place], parts[place ^ (1 << index)]) for place in range(TEAM)]
    query_ref[...] = jnp.concatenate([part[:, WIDE : WIDE + MINE * HEAD] for part in parts], axis=1)


def params(limit):
    return pltpu.CompilerParams(vmem_limit_bytes=limit * MB)


def cost(micros):
    return pl.CostEstimate(flops=int(micros * 1.1e9), bytes_accessed=0, transcendentals=0)


def struct(shape, kind):
    return jax.ShapeDtypeStruct(shape, kind)


def whole(*shape):
    return pl.BlockSpec(shape, lambda *_: (0,) * len(shape))


def on_device(nseq, ndp, inputs, w_query, w_keyval, w_out, w_up, w_down, norm_gain, norm_bias, out_cotangent, kv_cotangent):
    count, rows, width = inputs.shape
    top = nseq // 2
    wide = nseq // TEAM
    own = lax.axis_index("seq")
    own_y, own_x, own_c = own // top, (own // 2) % wide, own % 2
    own_z = lax.axis_index("dp")
    share = w_query.shape[0]
    down_share = w_down.shape[0]
    hidden = w_up.shape[1] // TEAM
    heads_wide = MINE * HEAD
    front_wide = 3 * WIDE
    slots = TEAM * wide

    def flip(value, mask, what):
        with jax.named_scope("swap_" + what):
            return lax.ppermute(value, "seq", [(i, i ^ mask) for i in range(nseq)])

    def flip_z(value, mask, what):
        with jax.named_scope("swap_" + what):
            return lax.ppermute(value, "dp", [(i, i ^ mask) for i in range(ndp)])

    def hold(*values):
        return lax.optimization_barrier(values)

    def after(value, *others):
        return hold(value, *others)[0]

    def in_order(bit, mine, other, axis):
        return jnp.where(
            bit == 0, jnp.stack([mine, other], axis), jnp.stack([other, mine], axis)
        )

    def merge(value, axis):
        return value.reshape(value.shape[:axis] + (-1,) + value.shape[axis + 2 :])

    def pick(value, index, axis):
        return lax.dynamic_index_in_dim(value, index, axis, keepdims=False)

    def swap_z(value, mask, axis, what):
        other = flip_z(value, mask, f"{what}_z{mask}")

        def join(other):
            return merge(in_order((own_z // mask) % 2, value, other, axis + 1), axis)

        return other, join

    def gather_z(value, axis, what, step=None):
        masks = [ndp >> (index + 1) for index in range(ndp.bit_length() - 1)]
        for mask in masks if step is None else masks[step]:
            other, join = swap_z(value, mask, axis, what)
            value = join(other)
        return value

    def by_place(relative, bits):
        for index, bit in enumerate(bits):
            relative = [
                jnp.where(bit == 0, relative[place], relative[place ^ (1 << index)])
                for place in range(len(relative))
            ]
        return relative

    z_bits = [(own_z >> index) % 2 for index in range(ndp.bit_length() - 1)]

    def gather_x(value, what):
        parts = [value[None]]
        mask = 1
        while mask < wide:
            sent = jnp.concatenate(parts) if mask > 1 else parts[0]
            parts.append(flip(sent, 2 * mask, f"{what}_x{mask}"))
            mask *= 2
        return parts

    def flip_x(send, what):
        return flip(send, wide, f"{what}_x{wide // 2}")

    def scatter_x(keep, got, what):
        mask = wide // 2
        while True:
            value = keep.astype(F32) + got.astype(F32)
            mask //= 2
            if mask == 0:
                return value[0]
            bit = (own_x // mask) % 2
            value = value.reshape((2, -1) + value.shape[1:])
            keep = pick(value, bit, 0)
            got = flip(pick(value, 1 - bit, 0).astype(BF), 2 * mask, f"{what}_x{mask}")

    def halve_z(value, axis, what, mask):
        bit = (own_z // mask) % 2
        value = value.reshape(value.shape[:axis] + (-1, 2) + value.shape[axis + 1 :])
        got = flip_z(pick(value, 1 - bit, axis + 1).astype(BF), mask, f"{what}_z{mask}")
        return pick(value, bit, axis + 1), got

    def add_z(pair):
        return pair[0].astype(F32) + pair[1].astype(F32)

    def finish_z(value, axis, what):
        mask = 2
        while mask < ndp:
            value = add_z(halve_z(value, axis, what, mask))
            mask *= 2
        return jnp.squeeze(value, axis)

    def moved(onward):
        pairs = []
        for rank in range(nseq):
            for z in range(ndp):
                member = 2 * (rank // top) + rank % 2
                place = ((rank // 2) % wide) * ndp + z
                pairs.append((member * (nseq * ndp // TEAM) + place, rank * ndp + z))
        return [pair if onward else pair[::-1] for pair in pairs]

    def team(value, what, first, second):
        across = flip(after(value, first), top, what + "_y")
        return [value, across, flip(value, 1, what + "_c"), flip(after(across, second), 1, what + "_yc")]

    norms = jnp.concatenate([norm_gain, norm_bias], axis=1)
    queries_of = w_query.reshape(share, 2, 2, heads_wide).transpose(1, 2, 0, 3)
    same = jnp.concatenate([w_keyval, norms], axis=1)
    ups = w_up.reshape(share, 2, wide, 2, hidden // wide).transpose(1, 3, 0, 2, 4)
    ups = ups.reshape(2, 2, share, hidden)
    pad = jnp.zeros((2, 2, share, 2 * WIDE - heads_wide - norms.shape[1]), BF)
    spread = (2, 2, share)
    pack = jnp.concatenate(
        [
            jnp.broadcast_to(same[:, :WIDE], spread + (WIDE,)),
            queries_of,
            jnp.broadcast_to(same[:, WIDE:], spread + (norms.shape[1],)),
            pad,
            ups,
        ],
        axis=3,
    )
    masks = [ndp >> (index + 1) for index in range(ndp.bit_length() - 1)]
    near_masks, far_masks = masks[-1:], masks[:-1]

    def spread_z(value, axis, what, some):
        for mask in some:
            other, join = swap_z(value, mask, axis, what)
            value = join(other)
        return value

    def begin_z(value, axis, what, some):
        if not some:
            return value, lambda value: value
        return swap_z(spread_z(value, axis, what, some[:-1]), some[-1], axis, what)

    sequences = [inputs[b : b + 1] for b in range(count)]
    got = [
        flip(pick(pick(pack, own_y ^ (d // 2), 0), own_c ^ (d % 2), 0), top * (d // 2) + d % 2, f"pack_{d}")
        for d in range(1, TEAM)
    ]
    pack, got, sequences, w_out = hold(pack, got, sequences, w_out)
    across = [flip(sequences[0], top, "tokens0_y")]
    mine = pick(pick(pack, own_y, 0), own_c, 0)
    pack = jnp.stack(by_place([mine] + got, [own_c, own_y])).reshape(2, 2, share, -1)
    tokens_c = [flip(sequences[b], 1, f"tokens{b}_c") for b in range(count)]

    front_z = pack[..., :front_wide].reshape(TEAM, share, front_wide)
    got = [flip_z(front_z, mask, f"front_z{mask}") for mask in range(1, ndp)]
    got, across[0] = hold(got, across[0])
    front_z = jnp.stack(by_place([front_z] + got, z_bits), axis=1)
    down_x = jnp.concatenate(gather_x(w_down[None], "down"))
    front_z, pack, w_out, across[0] = hold(front_z, pack, w_out, across[0])
    with jax.named_scope("swap_out_moved"):
        out_rows = lax.ppermute(w_out, ("seq", "dp"), moved(True))
    for b in range(1, count):
        across.append(flip(after(sequences[b], across[b - 1]), top, f"tokens{b}_y"))
    tokens = [[sequences[0], across[0], tokens_c[0], flip(across[0], 1, "tokens0_yc")]]
    front_parts = gather_x(front_z.reshape(TEAM, ndp * share, front_wide), "front")
    more = jnp.concatenate(
        [pack[..., front_wide:].reshape(TEAM, share, hidden), out_rows.reshape(1, share, width)]
    )
    more_got, join_more = begin_z(more[:, None], 1, "more", far_masks)
    front_parts, tokens[0] = hold(front_parts, tokens[0])
    own_rank = own.reshape(1).astype(jnp.int32)
    own_place = jnp.stack([own_x, own_z]).astype(jnp.int32)
    tables = [jnp.asarray(part) for part in angle_tables(rows, nseq)]

    def by_r(*last):
        return pl.BlockSpec((1,) + last, lambda r, *_: (r,) + (0,) * len(last))

    members = [pl.BlockSpec(memory_space=pl.ANY)] * TEAM

    def near(*last):
        return pl.BlockSpec((1,) + last, lambda r, *_: (jnp.minimum(r, 1),) + (0,) * len(last))

    def far(*last):
        return pl.BlockSpec((1,) + last, lambda r, *_: (jnp.maximum(r - 2, 0),) + (0,) * len(last))

    def call(kernel, scalar, inputs, in_specs, out_specs, out_shape, scratch, limit, micros, name, steps=TEAM):
        return pl.pallas_call(
            kernel,
            grid_spec=pltpu.PrefetchScalarGridSpec(
                num_scalar_prefetch=1,
                grid=(steps,),
                in_specs=in_specs,
                out_specs=out_specs,
                scratch_shapes=scratch,
            ),
            out_shape=out_shape,
            compiler_params=params(limit),
            cost_estimate=cost(micros),
            name=name,
        )(scalar, *inputs)

    table = by_r(rows, WIDE)
    block = [pltpu.VMEM((2, 1, rows, width), BF), pltpu.SemaphoreType.DMA((2,))]

    def prepare(b, weights):
        first = b == 0
        many = 1 if b < count - 1 else count
        held = tokens[b] + sum(tokens[: many - 1], [])
        outs = [struct((TEAM, rows, 2 * WIDE), BF), struct((TEAM, rows, WIDE), BF)]
        if first:
            outs += [struct((width, front_wide), BF), struct((8, width), F32)]
        else:
            outs += [struct((TEAM, many, rows, width), BF)]
        return call(
            functools.partial(prepare_kernel, len(weights), first, many, top, wide),
            own_rank,
            [*held, *weights, *tables],
            members * many + [whole(*part.shape) for part in [*weights, *tables]],
            [whole(*out.shape) for out in outs],
            outs,
            [pltpu.VMEM((many * TEAM, 1, rows, width), BF), pltpu.SemaphoreType.DMA((many * TEAM,))],
            16 if first else 24,
            0.5,
            "prepare",
            1,
        )

    *made_first, front, norm_rows = prepare(0, front_parts)
    prepared = [made_first]
    prepared[0], front, across[1:], more_got, down_x = hold(
        prepared[0], front, across[1:], more_got, down_x
    )
    down_got, join_down = begin_z(down_x[:, None], 1, "down", far_masks)
    for b in range(1, count):
        tokens.append([sequences[b], across[b], tokens_c[b], flip(across[b], 1, f"tokens{b}_yc")])
    more_got, join_more = begin_z(join_more(more_got), 1, "more", near_masks)
    prepared += [prepare(b, [front, norm_rows]) for b in range(1, count)]
    normed_mlp = prepared[-1][-1]
    queries, keyvals = [[part[index] for part in prepared] for index in range(2)]

    def keys_of_all(value, what):
        parts = [value]
        mask = 1
        while mask < wide:
            sent = jnp.concatenate(parts) if mask > 1 else parts[0]
            parts.append(flip(sent, 2 * mask, f"{what}_x{mask}"))
            mask *= 2
        return parts

    everyone = [keys_of_all(keyvals[b], f"keyval{b}") for b in range(count)]
    kv_specs = [whole(*part.shape) for part in everyone[0]]
    kv_scratch = [pltpu.VMEM((slots * rows, WIDE), BF)] * 2

    def by_pair(*last):
        return pl.BlockSpec((2, 1) + last, lambda y, *_: (0, y) + (0,) * len(last))

    def paired(value):
        return value.reshape((2, 2) + value.shape[1:])

    grads_y = flip(after(out_cotangent, tokens[-1][1]), top, "grads_y")
    grads_c = flip(out_cotangent, 1, "grads_c")
    everyone[0], queries, keyvals = hold(everyone[0], queries, keyvals)
    contexts = []
    marked_queries = []
    for b in range(count):
        context, marked_query = call(
            functools.partial(forward_kernel, top, wide),
            own_rank,
            [paired(queries[b]), *everyone[b]],
            [by_pair(rows, 2 * WIDE)] + kv_specs,
            [by_pair(rows, 2 * WIDE), by_pair(MINE, rows, WIDE)],
            [struct((2, 2, rows, 2 * WIDE), BF), struct((2, 2, MINE, rows, WIDE), BF)],
            [
                pltpu.VMEM((2 * MINE * rows, WIDE), BF),
                pltpu.VMEM((slots // 2, 2 * MINE * rows, 2 * rows), F32),
                pltpu.VMEM((2 * MINE * rows, WIDE), F32),
            ]
            + kv_scratch,
            7 + 7 * slots // 4,
            15,
            "attend",
            2,
        )
        context = context.reshape((TEAM,) + context.shape[2:])
        contexts.append(context)
        marked_queries.append(marked_query)
        if b == 0:
            contexts[0], everyone[1:], queries, grads_y, down_got, more_got = hold(
                contexts[0], everyone[1:], queries, grads_y, down_got, more_got
            )
            more_parts = gather_x(join_more(more_got).reshape(TEAM + 1, ndp * share, width), "more")
            down_z = join_down(down_got)
            down_got = flip_z(down_z, 1, "down_z1")
            grads = [out_cotangent, grads_y, grads_c, flip(grads_y, 1, "grads_yc")]
    contexts, grads, more_parts, down_got = hold(contexts, grads, more_parts, down_got)
    if down_share % 16:
        down_parts = [in_order(own_z % 2, down_z, down_got, 2).reshape(wide, 1, ndp * down_share, width)]
    else:
        down_parts = [part.reshape(wide, ndp // 2, down_share, width) for part in (down_z, down_got)]

    half = max(wide // 2, 1)
    more_half = (half, TEAM + 1, ndp * share, width)
    down_half = (wide, ndp // 2, down_share, width)
    made, made_far, d_normed, marked_grad, more_keep, more_send, down_keep, down_send = call(
        functools.partial(hidden_kernel, count, len(more_parts), len(down_parts)),
        own_place,
        [*grads, normed_mlp, *contexts, *more_parts, *down_parts],
        members
        + [by_r(count, rows, width)]
        + [by_r(rows, 2 * WIDE)] * count
        + [whole(*part.shape) for part in more_parts + down_parts],
        [
            near(count, rows, width),
            far(count, rows, width),
            by_r(count, rows, width),
            by_r(count, MINE, rows, WIDE),
            whole(*more_half),
            whole(*more_half),
            whole(*down_half),
            whole(*down_half),
        ],
        [
            struct((2, count, rows, width), BF),
            struct((2, count, rows, width), BF),
            struct((TEAM, count, rows, width), BF),
            struct((TEAM, count, MINE, rows, WIDE), BF),
            struct(more_half, BF),
            struct(more_half, BF),
            struct(down_half, BF),
            struct(down_half, BF),
        ],
        [
            pltpu.VMEM((width, hidden), F32),
            pltpu.VMEM((hidden + 2 * WIDE, width), F32),
            pltpu.VMEM((2, count, rows, width), BF),
            pltpu.SemaphoreType.DMA((2,)),
            pltpu.VMEM((width, hidden), BF),
            pltpu.VMEM((hidden + 2 * WIDE, width), BF),
        ],
        36,
        27,
        "hidden",
    )

    def sum_c(value, what, *others):
        return value[0].astype(F32) + after(flip(value[1], 1, what + "_c"), *others).astype(F32)

    def sum_y(value, what, *others):
        got = flip(value[1].astype(BF), top, what + "_y")
        return value[0] + after(got, *others).astype(F32)

    d_queries = []
    kept = []
    sent = []
    key_half = (slots // 2, rows, WIDE)
    for b in range(count):
        d_query, keep, send = call(
            functools.partial(backward_kernel, top, wide),
            own_rank,
            [marked_queries[b], paired(marked_grad), *tables, *everyone[b]],
            [
                by_pair(MINE, rows, WIDE),
                pl.BlockSpec((2, 1, None, MINE, rows, WIDE), lambda y, *_, b=b: (0, y, b, 0, 0, 0)),
            ]
            + [whole(*part.shape) for part in tables]
            + kv_specs,
            [by_pair(rows, 2 * WIDE), whole(*key_half), whole(*key_half)],
            [struct((2, 2, rows, 2 * WIDE), BF), struct(key_half, F32), struct(key_half, BF)],
            [pltpu.VMEM((2, MINE, WIDE, rows), F32)]
            + kv_scratch
            + [pltpu.VMEM((slots * rows, WIDE), F32)],
            16,
            20,
            "attend_back",
            2,
        )
        d_query = d_query.reshape((TEAM,) + d_query.shape[2:])
        d_queries.append(d_query)
        kept.append(keep)
        sent.append(send)
        if b == 0:
            got_c = flip(made_far, 1, "made_c")
            got_x = flip_x(more_send, "gmore")
            down_got = flip_z(down_send, 1, "gdown_z1")
            (d_queries, kept, sent, marked_grad, made, got_c, more_keep, got_x, down_keep, down_got) = hold(
                d_queries, kept, sent, marked_grad, made, got_c, more_keep, got_x, down_keep, down_got
            )
            made = made.astype(F32) + got_c.astype(F32)
            more_grads = scatter_x(more_keep, got_x, "gmore").reshape(TEAM + 1, ndp, share, width)
            got_y = flip(made[1].astype(BF), top, "made_y")
            more_z = halve_z(more_grads, 1, "gmore", 1)
            keys_got = flip_x(sent[0], "gkeyval0")
            down_grads = down_keep.astype(F32) + down_got.astype(F32)
            mask = 2
            while mask < ndp:
                down_z = halve_z(down_grads, 1, "gdown", mask)
                down_grads = add_z(down_z) if 2 * mask < ndp else down_grads
                mask *= 2
    (d_queries, kept, sent, made, got_y, more_z, keys_got) = hold(
        d_queries, kept, sent, made, got_y, more_z, keys_got
    )
    made_rows, made_got = made[0], got_y
    more_grads = add_z(more_z)
    keys_gots = [keys_got] + [flip_x(sent[b], f"gkeyval{b}") for b in range(1, count)]

    def keys_back(b):
        keep, got = kept[b], keys_gots[b]
        mask = wide // 2
        while True:
            value = keep + got.astype(F32)
            mask //= 2
            if mask == 0:
                return value
            keep = value[: value.shape[0] // 2]
            got = flip(value[value.shape[0] // 2 :].astype(BF), 2 * mask, f"gkeyval{b}_x{mask}")

    def join_c(value, got):
        mine = pick(value.reshape((2, 2) + value.shape[1:]), own_c, 1)
        got = got.astype(F32)
        return jnp.where(own_c == 0, mine, got), jnp.where(own_c == 0, got, mine)

    def join_y(value, got):
        mine = pick(value, own_y, 0)
        got = got.astype(F32)
        return jnp.where(own_y == 0, mine, got), jnp.where(own_y == 0, got, mine)

    pulled = []
    carried = []
    front_half = (half, TEAM, ndp * share, front_wide)
    for b in range(count):
        last = b == count - 1
        outs = [struct((2, rows, width), BF), struct((2, rows, width), BF)]
        out_specs = [near(rows, width), far(rows, width)]
        sums = [struct((width, front_wide), F32), struct((8, width), F32)]
        if last:
            outs += [struct(front_half, F32), struct(front_half, BF)]
        else:
            outs += sums
        d_tokens, d_tokens_far, *carried = call(
            functools.partial(tokens_kernel, last, top, wide),
            own_rank,
            [
                *tokens[b],
                d_normed,
                d_queries[b],
                keys_back(b),
                kv_cotangent,
                front,
                norm_rows,
                *tables,
                *carried,
            ],
            members
            + [
                pl.BlockSpec((1, 1, rows, width), lambda r, *_, b=b: (r, b, 0, 0)),
                by_r(rows, 2 * WIDE),
                table,
                pl.BlockSpec((1, rows, WIDE), lambda r, *_, b=b: (b, 0, 0)),
                whole(width, front_wide),
                whole(8, width),
            ]
            + [whole(*part.shape) for part in tables]
            + [whole(*part.shape) for part in carried],
            out_specs + [whole(*out.shape) for out in outs[2:]],
            outs,
            ([pltpu.VMEM(out.shape, F32) for out in sums] if last else []) + block,
            14,
            7,
            "pull_tokens",
        )
        pulled.append((d_tokens, d_tokens_far))
        if b == 0:
            mask = 2
            while mask < ndp:
                more_z = halve_z(more_grads, 1, "gmore", mask)
                more_grads = add_z(more_z) if 2 * mask < ndp else more_grads
                mask *= 2
            (carried, pulled, down_z, more_z, keys_gots, kept, d_queries) = hold(
                carried, pulled, down_z, more_z, keys_gots, kept, d_queries
            )
            more_grads = jnp.squeeze(add_z(more_z), 1)
            ups_c = flip(
                pick(more_grads[:TEAM].reshape(2, 2, share, hidden), 1 - own_c, 1).astype(BF), 1, "gup_c"
            )
            got_c = flip(pulled[0][1], 1, "dtokens0_c")
            down_grads = jnp.squeeze(add_z(down_z), 1)
            x_half = down_grads.reshape((2, -1) + down_grads.shape[1:])
            x_bit = own_x // (wide // 2)
            down_keep = pick(x_half, x_bit, 0)
            down_got = flip_x(pick(x_half, 1 - x_bit, 0).astype(BF), "gdown")
    front_keep, front_send = carried
    front_keep, front_send, pulled, got_c, ups_c = hold(front_keep, front_send, pulled, got_c, ups_c)
    ups = jnp.concatenate(join_c(more_grads[:TEAM], ups_c), axis=-1)
    ups_y = flip(pick(ups, 1 - own_y, 0).astype(BF), top, "gup_y")

    def add_c(pair, got):
        return pair[0].astype(F32) + got.astype(F32)

    front_got = flip_x(front_send, "gfront")
    halves = [add_c(pulled[0], got_c)]
    got_y = flip(halves[0][1].astype(BF), top, "dtokens0_y")
    gots_c = [flip(pulled[b][1], 1, f"dtokens{b}_c") for b in range(1, count)]
    made_got, down_got = hold(made_got, down_got, front_send)[:2]
    down_grads = scatter_x(down_keep, down_got, "gdown")
    output = (inputs.astype(F32) + made_rows + made_got.astype(F32)).astype(BF)
    front_keep, front_got, gots_c, more_grads, output = hold(
        front_keep, front_got, gots_c, more_grads, output
    )
    with jax.named_scope("swap_gout_moved"):
        grad_out = lax.ppermute(more_grads[TEAM].astype(BF), ("seq", "dp"), moved(False)).astype(F32)
    halves += [add_c(pulled[b], gots_c[b - 1]) for b in range(1, count)]
    front_grads = scatter_x(front_keep, front_got, "gfront").reshape(TEAM, ndp, share, front_wide)
    mine = pick(front_grads, own_z, 1)
    got = [
        flip_z(pick(front_grads, own_z ^ mask, 1).astype(BF), mask, f"gfront_z{mask}")
        for mask in range(1, ndp)
    ]
    gots_y = [got_y] + [
        flip(halves[b][1].astype(BF), top, f"dtokens{b}_y") for b in range(1, count)
    ]
    mine, got, halves, ups, ups_y, gots_y = hold(mine, got, halves, ups, ups_y, gots_y)
    front_grads = sum([part.astype(F32) for part in got], mine).reshape(2, 2, share, front_wide)

    piece = hidden // wide
    ups = join_y(ups, ups_y)
    grad_up = jnp.concatenate(
        [
            ups[y][:, hidden * c + piece * x : hidden * c + piece * (x + 1)]
            for y in range(2)
            for x in range(wide)
            for c in range(2)
        ],
        axis=-1,
    )
    got = [
        flip(
            pick(pick(front_grads, own_y ^ (d // 2), 0), own_c ^ (d % 2), 0).astype(BF),
            top * (d // 2) + d % 2,
            f"gfront_{d}",
        )
        for d in range(1, TEAM)
    ]
    mine = front_grads.reshape(TEAM, share, front_wide)
    d_rows = [halves[b][0] + gots_y[b].astype(F32) for b in range(count)]
    grad_inputs = out_cotangent.astype(F32) + jnp.stack(d_rows)
    mine, got, grad_inputs, grad_up, grad_out = hold(mine, got, grad_inputs, grad_up, grad_out)
    grad_query, grad_keyval, grad_gain, grad_bias = pl.pallas_call(
        finish_kernel,
        in_specs=[pl.BlockSpec(memory_space=pltpu.SMEM), whole(TEAM, share, front_wide)]
        + [whole(share, front_wide)] * (TEAM - 1),
        out_specs=[whole(share, TEAM * heads_wide), whole(share, WIDE), whole(2, share), whole(2, share)],
        out_shape=[
            struct((share, TEAM * heads_wide), F32),
            struct((share, WIDE), F32),
            struct((2, share), F32),
            struct((2, share), F32),
        ],
        scratch_shapes=[pltpu.VMEM((WIDE, WIDE), F32)],
        compiler_params=params(60),
        cost_estimate=cost(1),
        name="finish",
    )(jnp.stack([own_c, own_y]).astype(jnp.int32), mine, *got)
    return (
        output,
        jnp.stack([part[0] for part in keyvals]),
        grad_inputs,
        grad_query,
        grad_keyval,
        grad_out,
        grad_up,
        down_grads,
        grad_gain.T,
        grad_bias.T,
    )


def solution(mesh):
    rows = P("dp", "seq", None)
    split = P(("seq", "dp"), None)
    return jax.shard_map(
        functools.partial(on_device, mesh.shape["seq"], mesh.shape["dp"]),
        mesh=mesh,
        in_specs=(rows,) + (split,) * 7 + (rows, rows),
        out_specs=(rows,) * 3 + (split,) * 7,
        check_vma=False,
    )
```
